128 devices in a mesh: lat: 8 (over x_lo, z), lon: 16 (over x_hi, y, core).
Axes of the slice: x: 4 (x_hi: 2, x_lo: 2; x = x_hi * 2 + x_lo), y: 4, z: 4, core: 2. Of those that a mesh axis runs over, the one named last changes fastest.
Arguments:
- tokens: float32 [256, 256, 384], P('lat', 'lon'), may hold values from -60 to 60
- wet_flags: int32 [4, 32, 16], replicated, may hold values from 0 to 1, as said below
- ln_attn: float32 [4, 384], replicated, may hold values from 0.1 to 1.9
- w_qkv: bfloat16 [4, 384, 1152], replicated, may hold values from -0.3125 to 0.3125
- w_out: bfloat16 [4, 384, 384], replicated, may hold values from -0.3125 to 0.3125
- pos_bias: float32 [4, 12, 128, 128], replicated, may hold values from -4 to 300
- ln_mlp: float32 [4, 384], replicated, may hold values from 0.1 to 1.9
- w_up: bfloat16 [4, 384, 1536], replicated, may hold values from -0.3125 to 0.3125
- w_down: bfloat16 [4, 1536, 384], replicated, may hold values from -0.15625 to 0.15625
Outputs:
- evolved: float32 [256, 256, 384], P('lat', 'lon')
The draws below stay inside these ranges and needn't reach their ends.
Inputs may be any that keep to these rules, and one draw needn't show every extreme that they name: `wet_flags`: in each layer every longitude strip (column b of windows) holds exactly 16 wet windows, and in every strip some run of 4 windows a = k * 4 .. k * 4 + 3 is all wet.
All inputs are finite; a program needn't handle non-finite values.
Results may differ from the reference program's by a relative error of at most 0.007.
Values sent between devices are 32-bit elements; how exact they have to be, the bound alone decides.
No kernel may reach another device: no remote copies, remote signals or barrier semaphores. Data moves between devices by JAX's collectives and lax.ppermute only.
A program may use at most 128 MiB of HBM per device.

```python
import math
import jax
import jax.numpy as jnp
from jax import lax

C = 384
HEADS = 12
FFN = 1536
WROWS = 8
WCOLS = 16
WTOK = 128
LAYER_TOTAL = 4
DEVICE_WINDOWS = 4
WET_DEV = 2
WINDOW_ROW_COUNT = 32
WINDOW_COL_COUNT = 16
NLATP = 256
NLONP = 256
N_LAT = 8


def draw_tokens(key, part):
    key = jax.random.fold_in(key, 5)
    key_main, key_cols, key_rows = jax.random.split(key, 3)
    col_scale = jnp.exp(jax.random.uniform(key_cols, (1, 1, C), jnp.float32, math.log(0.3), math.log(3.0)))
    row_scale = jnp.exp(jax.random.uniform(key_rows, (NLATP, NLONP, 1), jnp.float32, math.log(0.3), math.log(3.0)))
    noise_field = jnp.clip(jax.random.normal(key_main, (NLATP, NLONP, C), jnp.float32), -6.0, 6.0)
    return noise_field * col_scale * row_scale


def draw_wet_flags(key, part):
    key = jax.random.fold_in(key, 7)
    wobble_key, reward_key, loaded_key = jax.random.split(key, 3)
    random_wobble = jax.random.randint(wobble_key, (LAYER_TOTAL, WINDOW_ROW_COUNT, WINDOW_COL_COUNT), 0, 65536)
    device_reward = jax.random.randint(reward_key, (LAYER_TOTAL, N_LAT, 1, WINDOW_COL_COUNT), 0, 4)
    device_loaded = jax.random.randint(loaded_key, (LAYER_TOTAL, 1, 1, WINDOW_COL_COUNT), 0, N_LAT)
    device_labels = jnp.arange(N_LAT).reshape(1, N_LAT, 1, 1)
    device_reward = jnp.where(device_labels == device_loaded, 64, device_reward)
    device_reward = jnp.broadcast_to(device_reward, (LAYER_TOTAL, N_LAT, DEVICE_WINDOWS, WINDOW_COL_COUNT)).reshape(LAYER_TOTAL, WINDOW_ROW_COUNT, WINDOW_COL_COUNT)
    slot_position = jnp.arange(WINDOW_ROW_COUNT).reshape(1, WINDOW_ROW_COUNT, 1)
    score_values = (device_reward * 24000 + random_wobble) * WINDOW_ROW_COUNT + slot_position
    sorted_order = jnp.argsort(-score_values, axis=1)
    window_rank = jnp.argsort(sorted_order, axis=1)
    return (window_rank < WET_DEV * N_LAT).astype(jnp.int32)


def draw_pos_bias(key, part):
    key = jax.random.fold_in(key, 11)
    subkeys = jax.random.split(key, 1)
    full_shape = (LAYER_TOTAL, HEADS, WTOK, WTOK)
    values = jnp.clip(jax.random.normal(subkeys[0], full_shape, jnp.float32), -4.0, 4.0)
    return values


def normal_values(own_key, extent, width, most, held_as=jnp.bfloat16):
    drawn = jax.random.normal(own_key, extent, jnp.float32) * width
    return jnp.minimum(jnp.maximum(drawn, -most), most).astype(held_as)


def setup_inputs(seed: int = 0) -> dict:
    streams_of = jax.random.split(jax.random.key(seed), 10)
    tokens = draw_tokens(jax.random.fold_in(streams_of[9], 71), 0)
    wet_flags = draw_wet_flags(jax.random.fold_in(streams_of[9], 71), 0)
    ln_attn = jnp.clip(1.0 + 0.18 * jax.random.normal(streams_of[2], (LAYER_TOTAL, C), jnp.float32), 0.1, 1.9)
    w_qkv = normal_values(streams_of[3], (LAYER_TOTAL, C, 3 * C), C ** -0.5, 0.3125)
    w_out = normal_values(streams_of[4], (LAYER_TOTAL, C, C), C ** -0.5, 0.3125)
    pos_bias = draw_pos_bias(jax.random.fold_in(streams_of[9], 71), 0)
    ln_mlp = jnp.clip(1.0 + 0.18 * jax.random.normal(streams_of[6], (LAYER_TOTAL, C), jnp.float32), 0.1, 1.9)
    w_up = normal_values(streams_of[7], (LAYER_TOTAL, C, FFN), C ** -0.5, 0.3125)
    w_down = normal_values(streams_of[8], (LAYER_TOTAL, FFN, C), FFN ** -0.5, 0.15625)
    return {"tokens": tokens, "wet_flags": wet_flags, "ln_attn": ln_attn, "w_qkv": w_qkv, "w_out": w_out, "pos_bias": pos_bias, "ln_mlp": ln_mlp, "w_up": w_up, "w_down": w_down}


norm_eps = 1e-05
mask_fill = -1000000000.0

def layer_norm(inputs, gain):
    center = lax.optimization_barrier(jnp.mean(inputs, axis=-1, keepdims=True))
    spread = lax.optimization_barrier(jnp.mean(jnp.square(inputs - center), axis=-1, keepdims=True))
    return (inputs - center) * lax.rsqrt(spread + norm_eps) * gain

def matmul_wide(left, right):
    return jnp.dot(left.astype(jnp.float32), right.astype(jnp.float32), precision=lax.Precision.HIGHEST)

def window_layer(inputs, masked, gain_attn, qkv_weight, out_weight, bias, gain_mlp, up_weight, down_weight):
    win_count, win_tokens, channels = inputs.shape
    head_count = bias.shape[0]
    head_size = channels // head_count
    normed = layer_norm(inputs, gain_attn).astype(jnp.bfloat16).reshape(win_count * win_tokens, channels)
    projected = matmul_wide(normed, qkv_weight).astype(jnp.bfloat16)
    projected = projected.reshape(win_count, win_tokens, 3, head_count, head_size).astype(jnp.float32)
    score_values = jnp.einsum('bqhd,bkhd->bhqk', projected[:, :, 0], projected[:, :, 1], precision=lax.Precision.HIGHEST)
    score_values = score_values * head_size ** (-0.5) + bias[None]
    region = jnp.arange(win_tokens) // WCOLS >= WROWS // 2
    same_region = region[:, None] == region[None, :]
    allowed = jnp.logical_or(same_region[None, None], jnp.logical_not(masked)[:, None, None, None])
    score_values = jnp.where(allowed, score_values, mask_fill)
    attention = jax.nn.softmax(score_values, axis=-1).astype(jnp.bfloat16).astype(jnp.float32)
    attended = jnp.einsum('bhqk,bkhd->bqhd', attention, projected[:, :, 2], precision=lax.Precision.HIGHEST)
    attended = attended.astype(jnp.bfloat16).reshape(win_count * win_tokens, channels)
    resid = inputs + matmul_wide(attended, out_weight).reshape(inputs.shape)
    mlp_in = layer_norm(resid, gain_mlp).astype(jnp.bfloat16).reshape(win_count * win_tokens, channels)
    activated = jax.nn.gelu(matmul_wide(mlp_in, up_weight), approximate=False).astype(jnp.bfloat16)
    return resid + matmul_wide(activated, down_weight).reshape(inputs.shape)

def to_windows(patch_grid):
    lat_rows, lon_cols, channels = patch_grid.shape
    blocks = patch_grid.reshape(lat_rows // WROWS, WROWS, lon_cols // WCOLS, WCOLS, channels)
    return blocks.transpose(0, 2, 1, 3, 4).reshape(lat_rows // WROWS, lon_cols // WCOLS, WROWS * WCOLS, channels)

def from_windows(blocks, lat_rows, lon_cols):
    channels = blocks.shape[-1]
    blocks = blocks.reshape(lat_rows // WROWS, lon_cols // WCOLS, WROWS, WCOLS, channels)
    return blocks.transpose(0, 2, 1, 3, 4).reshape(lat_rows, lon_cols, channels)

def reference(tokens, wet_flags, ln_attn, w_qkv, w_out, pos_bias, ln_mlp, w_up, w_down):
    patch_grid = tokens
    lat_rows, lon_cols, channels = tokens.shape
    half_rows = WROWS // 2
    half_cols = WCOLS // 2
    for layer_index in range(LAYER_TOTAL):
        shifted = layer_index % 2 == 1
        if shifted:
            patch_grid = jnp.roll(patch_grid, (-half_rows, -half_cols), axis=(0, 1))
        blocks = to_windows(patch_grid)
        row_count = blocks.shape[0]
        masked_rows = jnp.logical_and(jnp.arange(row_count) == row_count - 1, shifted)
        params = (ln_attn[layer_index], w_qkv[layer_index], w_out[layer_index], pos_bias[layer_index], ln_mlp[layer_index], w_up[layer_index], w_down[layer_index])

        def one_row(pieces):
            row_blocks, wet_row, masked_row = pieces
            masked = jnp.broadcast_to(masked_row, (row_blocks.shape[0],))
            updated = window_layer(row_blocks, masked, params[0], params[1], params[2], params[3], params[4], params[5], params[6])
            return jnp.where(wet_row[:, None, None] == 1, updated, row_blocks)
        blocks = lax.map(one_row, (blocks, wet_flags[layer_index], masked_rows))
        patch_grid = from_windows(blocks, lat_rows, lon_cols)
        if shifted:
            patch_grid = jnp.roll(patch_grid, (half_rows, half_cols), axis=(0, 1))
    return patch_grid
```

```python
import functools

import jax
import jax.numpy as jnp
from jax import lax
from jax.experimental import pallas as pl
from jax.experimental.pallas import tpu as pltpu
from jax.sharding import PartitionSpec as P

C = 384
HEADS = 12
FFN = 1536
TOK = 128
LANES = 128
GROUP = 4
HEAD = 32
LAYERS = 4
CHUNK = 256
norm_eps = 1e-05
mask_fill = -1000000000.0
ERF_POLY = (
    0.7978830000512025,
    0.03633754443795962,
    -3.569087070491613e-05,
    -5.440885213149521e-05,
    3.8449560401057786e-06,
    -1.2507491956239078e-07,
    1.601666137598869e-09,
)
ERF_FLAT = 5.7 * 5.7
f32 = jnp.float32
bf16 = jnp.bfloat16
ANY = pl.BlockSpec(memory_space=pl.ANY)


def gelu(x):
    square = jnp.minimum(x * x, ERF_FLAT)
    poly = jnp.float32(ERF_POLY[-1])
    for factor in ERF_POLY[-2::-1]:
        poly = poly * square + factor
    half = 0.5 * x
    return half + half * jnp.tanh(x * poly)


def layer_norm(x, gain):
    center = jnp.mean(x, axis=-1, keepdims=True)
    away = x - center
    spread = jnp.mean(away * away, axis=-1, keepdims=True)
    return (away * lax.rsqrt(spread + norm_eps) * gain).astype(bf16)


def attend(q, k, v, bias_ref, group, masked):
    owner = lax.broadcasted_iota(jnp.int32, (TOK, LANES), 1) // HEAD
    zero = jnp.zeros((TOK, LANES), bf16)
    one = jnp.ones((TOK, LANES), bf16)
    keys = jnp.concatenate([jnp.where(owner == h, k, zero) for h in range(GROUP)], axis=0)
    scores = lax.dot_general(q, keys, (((1,), (1,)), ((), ())), preferred_element_type=f32)
    parts = []
    for h in range(GROUP):
        s = scores[:, h * TOK : (h + 1) * TOK] * HEAD ** (-0.5) + bias_ref[group * GROUP + h]
        if masked is not None:
            s = jnp.where(masked, mask_fill, s)
        parts.append(jnp.exp(s - jnp.max(s, axis=-1, keepdims=True)).astype(bf16))
    weights = jnp.concatenate(parts, axis=1)
    values = jnp.concatenate(
        [
            jnp.concatenate([jnp.where(owner == h, v, zero), jnp.where(owner == h, one, zero)], axis=1)
            for h in range(GROUP)
        ],
        axis=0,
    )
    both = jnp.dot(weights, values, preferred_element_type=f32)
    return (both[:, :LANES] / both[:, LANES:]).astype(bf16)


class Buffers:
    pass


def run_windows(b, ids, masked):
    count = len(ids)
    rows = count * TOK
    x = jnp.concatenate([b.xs[pl.ds(i * 8, 8)].reshape(TOK, C) for i in ids], axis=0)
    b.qkv[:rows] = jnp.dot(layer_norm(x, b.ga[...]), b.wq[...], preferred_element_type=f32).astype(bf16)
    for w in range(count):
        span = slice(w * TOK, (w + 1) * TOK)
        hide = None
        if masked is not None:
            low_q = lax.broadcasted_iota(jnp.int32, (TOK, TOK), 0) >= TOK // 2
            low_k = lax.broadcasted_iota(jnp.int32, (TOK, TOK), 1) >= TOK // 2
            hide = jnp.logical_and(low_q != low_k, masked[w])
        for g in range(HEADS // GROUP):
            at = g * LANES
            b.att[span, at : at + LANES] = attend(
                b.qkv[span, at : at + LANES],
                b.qkv[span, C + at : C + at + LANES],
                b.qkv[span, 2 * C + at : 2 * C + at + LANES],
                b.bias,
                g,
                hide,
            )
    resid = x + jnp.dot(b.att[:rows], b.wo[...], preferred_element_type=f32)
    mlp_in = layer_norm(resid, b.gm[...])
    total = resid
    for f in range(0, FFN, CHUNK):
        up = jnp.dot(mlp_in, b.wu[:, f : f + CHUNK], preferred_element_type=f32)
        total = total + jnp.dot(gelu(up).astype(bf16), b.wd[f : f + CHUNK, :], preferred_element_type=f32)
    for w, i in enumerate(ids):
        b.xs[pl.ds(i * 8, 8)] = total[w * TOK : (w + 1) * TOK].reshape(8, 2, 8, C)


def stage_kernel(layer, first, loads, stores, n_in, n_alias, n_out, *refs):
    wet, ga, wq, wo, bias, gm, wu, wd = refs[:8]
    ins = refs[8 : 8 + n_in]
    outs = refs[8 + n_in + n_alias : 8 + n_in + n_alias + n_out]
    (xs, qkv, att, s_wet, s_ga, s_wq, s_wo, s_bias, s_gm, s_wu, s_wd, sem, out_sem) = refs[
        8 + n_in + n_alias + n_out :
    ]
    copies = []

    def copy(source, target):
        c = pltpu.make_async_copy(source, target, sem.at[len(copies)])
        c.start()
        copies.append(c)
        return c

    first_wait = [copy(wet.at[layer], s_wet)]
    for source, low, high, to, half in loads:
        part = ins[source].at[low:high]
        target = xs.at[to : to + high - low] if half is None else xs.at[to : to + high - low, half]
        first_wait.append(copy(part, target))
    first_wait.append(copy(ga.at[pl.ds(layer, 1)], s_ga))
    first_wait.append(copy(wq.at[layer], s_wq))
    late = [copy(bias.at[layer], s_bias), copy(wo.at[layer], s_wo), copy(gm.at[pl.ds(layer, 1)], s_gm)]
    late += [copy(wu.at[layer], s_wu), copy(wd.at[layer], s_wd)]
    for c in first_wait:
        c.wait()
    for c in late:
        c.wait()
    b = Buffers()
    b.xs, b.qkv, b.att = xs, qkv, att
    b.ga, b.wq, b.wo, b.bias, b.gm, b.wu, b.wd = s_ga, s_wq, s_wo, s_bias, s_gm, s_wu, s_wd
    lat = lax.axis_index("lat")
    lon = lax.axis_index("lon")
    bands = lax.axis_size("lat")
    wet0 = s_wet[lat * 4 + first, lon] == 1
    wet1 = s_wet[lat * 4 + first + 1, lon] == 1
    masked = None
    if layer % 2 == 1 and first == 2:
        masked = lat == bands - 1

    @pl.when(jnp.logical_and(wet0, wet1))
    def _():
        run_windows(b, [0, 1], None if masked is None else [jnp.bool_(False), masked])

    @pl.when(wet0 != wet1)
    def _():
        which = jnp.where(wet1, 1, 0)
        run_windows(b, [which], None if masked is None else [jnp.logical_and(masked, wet1)])

    ends = []
    for n, (low, high, half, target, to) in enumerate(stores):
        part = xs.at[low:high] if half is None else xs.at[low:high, half]
        c = pltpu.make_async_copy(part, _place(outs[target], to, high - low), out_sem.at[n])
        c.start()
        ends.append(c)
    for c in ends:
        c.wait()


def _place(ref, to, count):
    low, half = to
    return ref.at[low : low + count] if half is None else ref.at[low : low + count, half]


def stage(layer, first, params, ins, loads, aliased, outs, stores, name):
    n_in, n_alias = len(ins), len(aliased)
    shapes = [jax.ShapeDtypeStruct(a.shape, a.dtype) for a in aliased]
    shapes += [jax.ShapeDtypeStruct(s, f32) for s in outs]
    kernel = functools.partial(stage_kernel, layer, first, loads, stores, n_in, n_alias, len(shapes))
    return pl.pallas_call(
        kernel,
        out_shape=shapes,
        in_specs=[ANY] * (8 + n_in + n_alias),
        out_specs=[ANY] * len(shapes),
        input_output_aliases={8 + n_in + i: i for i in range(n_alias)},
        scratch_shapes=[
            pltpu.VMEM((16, 2, 8, C), f32),
            pltpu.VMEM((2 * TOK, 3 * C), bf16),
            pltpu.VMEM((2 * TOK, C), bf16),
            pltpu.SMEM((32, 16), jnp.int32),
            pltpu.VMEM((1, C), f32),
            pltpu.VMEM((C, 3 * C), bf16),
            pltpu.VMEM((C, C), bf16),
            pltpu.VMEM((HEADS, TOK, TOK), f32),
            pltpu.VMEM((1, C), f32),
            pltpu.VMEM((C, FFN), bf16),
            pltpu.VMEM((FFN, C), bf16),
            pltpu.SemaphoreType.DMA((8 + len(loads),)),
            pltpu.SemaphoreType.DMA((len(stores),)),
        ],
        compiler_params=pltpu.CompilerParams(vmem_limit_bytes=56 << 20),
        cost_estimate=pl.CostEstimate(flops=1_000_000_000, bytes_accessed=6_000_000, transcendentals=800_000),
        name=name,
    )(*params, *ins, *aliased)


def send(block, d_lat, d_lon):
    n_lat, n_lon = lax.axis_size("lat"), lax.axis_size("lon")
    route = [
        (a * n_lon + b, (a + d_lat) % n_lat * n_lon + (b + d_lon) % n_lon)
        for a in range(n_lat)
        for b in range(n_lon)
    ]
    return lax.ppermute(block, ("lat", "lon"), route)


def finish_kernel(lat_ref, diag_ref, lon_ref, _, out_ref, sem):
    copies = [
        pltpu.make_async_copy(lat_ref, out_ref.at[0:4, 1], sem.at[0]),
        pltpu.make_async_copy(diag_ref, out_ref.at[0:4, 0], sem.at[1]),
        pltpu.make_async_copy(lon_ref, out_ref.at[4:32, 0], sem.at[2]),
    ]
    for c in copies:
        c.start()
    for c in copies:
        c.wait()


SMALL = (4, 8, C)
STRIP = (28, 8, C)


def local(tokens, wet_flags, ln_attn, w_qkv, w_out, pos_bias, ln_mlp, w_up, w_down):
    params = (wet_flags, ln_attn, w_qkv, w_out, pos_bias, ln_mlp, w_up, w_down)
    grid = tokens.reshape(32, 2, 8, C)
    for pair in range(LAYERS // 2):
        even, odd = 2 * pair, 2 * pair + 1
        if pair == 0:
            ins_a = ins_b = [grid]
            loads_a = [(0, 0, 16, 0, None)]
            loads_b = [(0, 16, 32, 0, None)]
        else:
            ins_a = [back_lat, back_diag, keep, back_lon]
            loads_a = [(0, 0, 4, 0, 1), (1, 0, 4, 0, 0), (2, 0, 12, 4, 1), (3, 0, 12, 4, 0)]
            ins_b = [keep, back_lon]
            loads_b = [(0, 12, 28, 0, 1), (1, 12, 28, 0, 0)]
        up_lat, up_diag, lon, keep_a = stage(
            even, 0, params, ins_a, loads_a, [], [SMALL, SMALL, STRIP, STRIP],
            [(0, 4, 1, 0, (0, None)), (0, 4, 0, 1, (0, None)), (4, 16, 0, 2, (0, None)), (4, 16, 1, 3, (0, None))],
            f"even{pair}a",
        )
        up_lat = send(up_lat, -1, 0)
        up_diag = send(up_diag, -1, -1)
        lon, keep = stage(
            even, 2, params, ins_b, loads_b, [lon, keep_a], [],
            [(0, 16, 0, 0, (12, None)), (0, 16, 1, 1, (12, None))],
            f"even{pair}b",
        )
        lon = send(lon, 0, -1)
        last = pair == LAYERS // 2 - 1
        row, half, shape = (4, 1, (32, 2, 8, C)) if last else (0, None, STRIP)
        back_lat, back_diag, back_lon, keep_a = stage(
            odd, 2, params, [keep, lon, up_lat, up_diag],
            [(0, 16, 28, 0, 0), (1, 16, 28, 0, 1), (2, 0, 4, 12, 0), (3, 0, 4, 12, 1)],
            [], [SMALL, SMALL, STRIP, shape],
            [(12, 16, 0, 0, (0, None)), (12, 16, 1, 1, (0, None)), (0, 12, 1, 2, (16, None)), (0, 12, 0, 3, (row + 16, half))],
            f"odd{pair}a",
        )
        back_lat = send(back_lat, 1, 0)
        back_diag = send(back_diag, 1, 1)
        back_lon, keep = stage(
            odd, 0, params, [keep, lon], [(0, 0, 16, 0, 0), (1, 0, 16, 0, 1)],
            [back_lon, keep_a], [],
            [(0, 16, 1, 0, (0, None)), (0, 16, 0, 1, (row, half))],
            f"odd{pair}b",
        )
        back_lon = send(back_lon, 0, 1)
    out = pl.pallas_call(
        finish_kernel,
        out_shape=jax.ShapeDtypeStruct(keep.shape, f32),
        in_specs=[ANY] * 4,
        out_specs=ANY,
        input_output_aliases={3: 0},
        scratch_shapes=[pltpu.SemaphoreType.DMA((3,))],
        name="finish",
    )(back_lat, back_diag, back_lon, keep)
    return out.reshape(32, 16, C)


def solution(mesh):
    in_specs = (P("lat", "lon", None), P(), P(), P(), P(), P(), P(), P(), P())
    out_specs = P("lat", "lon", None)
    return jax.shard_map(local, mesh=mesh, in_specs=in_specs, out_specs=out_specs, check_vma=False)
```

```python
import functools

import jax
import jax.numpy as jnp
from jax import lax
from jax.experimental import pallas as pl
from jax.experimental.pallas import tpu as pltpu
from jax.sharding import PartitionSpec as P

C = 384
HEADS = 12
FFN = 1536
TOK = 128
LANES = 128
GROUP = 4
HEAD = 32
LAYERS = 4
CHUNK = 256
norm_eps = 1e-05
mask_fill = -1000000000.0
ERF_POLY = (
    0.7978830000512025,
    0.03633754443795962,
    -3.569087070491613e-05,
    -5.440885213149521e-05,
    3.8449560401057786e-06,
    -1.2507491956239078e-07,
    1.601666137598869e-09,
)
ERF_FLAT = 5.7 * 5.7
f32 = jnp.float32
bf16 = jnp.bfloat16
HBM = pl.BlockSpec(memory_space=pltpu.HBM)


def gelu(x):
    square = jnp.minimum(x * x, ERF_FLAT)
    poly = jnp.float32(ERF_POLY[-1])
    for factor in ERF_POLY[-2::-1]:
        poly = poly * square + factor
    half = 0.5 * x
    return half + half * jnp.tanh(x * poly)


def layer_norm(x, gain):
    center = jnp.mean(x, axis=-1, keepdims=True)
    away = x - center
    spread = jnp.mean(away * away, axis=-1, keepdims=True)
    return (away * lax.rsqrt(spread + norm_eps) * gain).astype(bf16)


def attend(q, k, v, bias_ref, group, masked):
    owner = lax.broadcasted_iota(jnp.int32, (TOK, LANES), 1) // HEAD
    zero = jnp.zeros((TOK, LANES), bf16)
    one = jnp.ones((TOK, LANES), bf16)
    keys = jnp.concatenate([jnp.where(owner == h, k, zero) for h in range(GROUP)], axis=0)
    scores = lax.dot_general(q, keys, (((1,), (1,)), ((), ())), preferred_element_type=f32)
    parts = []
    for h in range(GROUP):
        s = scores[:, h * TOK : (h + 1) * TOK] * HEAD ** (-0.5) + bias_ref[group * GROUP + h]
        if masked is not None:
            s = jnp.where(masked, mask_fill, s)
        parts.append(jnp.exp(s - jnp.max(s, axis=-1, keepdims=True)).astype(bf16))
    weights = jnp.concatenate(parts, axis=1)
    values = jnp.concatenate(
        [
            jnp.concatenate([jnp.where(owner == h, v, zero), jnp.where(owner == h, one, zero)], axis=1)
            for h in range(GROUP)
        ],
        axis=0,
    )
    both = jnp.dot(weights, values, preferred_element_type=f32)
    return (both[:, :LANES] / both[:, LANES:]).astype(bf16)


class Buffers:
    pass


def run_windows(b, ids, masked):
    count = len(ids)
    rows = count * TOK
    x = jnp.concatenate([b.xs[pl.ds(i * 8, 8)].reshape(TOK, C) for i in ids], axis=0)
    b.qkv[:rows] = jnp.dot(layer_norm(x, b.ga[...]), b.wq[...], preferred_element_type=f32).astype(bf16)
    for w in range(count):
        span = slice(w * TOK, (w + 1) * TOK)
        hide = None
        if masked is not None:
            low_q = lax.broadcasted_iota(jnp.int32, (TOK, TOK), 0) >= TOK // 2
            low_k = lax.broadcasted_iota(jnp.int32, (TOK, TOK), 1) >= TOK // 2
            hide = jnp.logical_and(low_q != low_k, masked[w])
        for g in range(HEADS // GROUP):
            at = g * LANES
            b.att[span, at : at + LANES] = attend(
                b.qkv[span, at : at + LANES],
                b.qkv[span, C + at : C + at + LANES],
                b.qkv[span, 2 * C + at : 2 * C + at + LANES],
                b.bias,
                g,
                hide,
            )
    resid = x + jnp.dot(b.att[:rows], b.wo[...], preferred_element_type=f32)
    mlp_in = layer_norm(resid, b.gm[...])
    total = resid
    for f in range(0, FFN, CHUNK):
        up = jnp.dot(mlp_in, b.wu[:, f : f + CHUNK], preferred_element_type=f32)
        total = total + jnp.dot(gelu(up).astype(bf16), b.wd[f : f + CHUNK, :], preferred_element_type=f32)
    for w, i in enumerate(ids):
        b.xs[pl.ds(i * 8, 8)] = total[w * TOK : (w + 1) * TOK].reshape(8, 2, 8, C)


def load_layer(params, held, layer, sem, at):
    copies = []
    for n, (source, target) in enumerate(zip(params, held)):
        part = source.at[pl.ds(layer, 1)] if len(source.shape) == 2 else source.at[layer]
        c = pltpu.make_async_copy(part, target.at[layer % 2], sem.at[at + n])
        c.start()
        copies.append(c)
    return copies


def stage_kernel(layer, first, loads, stores, fetch, n_in, n_alias, n_out, *refs):
    refs = list(refs)

    def take(count):
        got, refs[:count] = refs[:count], []
        return got

    wet, *params = take(8) if fetch else take(1)
    held = [] if fetch and layer in fetch else take(7)
    ins = take(n_in)
    take(n_alias)
    outs = take(n_out)
    fetched = take(7) if fetch else []
    if not held:
        held = fetched
    xs, qkv, att, s_wet, sem, out_sem = refs
    flags = pltpu.make_async_copy(wet.at[layer], s_wet, sem.at[0])
    flags.start()
    early, late = [], []
    for n, which in enumerate(fetch):
        got = load_layer(params, fetched, which, sem, 1 + 7 * n)
        if which == layer:
            early += got
        else:
            late += got
    for n, (source, low, high, to, half) in enumerate(loads):
        target = xs.at[to : to + high - low] if half is None else xs.at[to : to + high - low, half]
        if fetch:
            c = pltpu.make_async_copy(ins[source].at[low:high], target, out_sem.at[n])
            c.start()
            early.append(c)
        else:
            target[...] = ins[source][low:high]
    flags.wait()
    for c in early:
        c.wait()
    b = Buffers()
    b.xs, b.qkv, b.att = xs, qkv, att
    b.ga, b.wq, b.wo, b.bias, b.gm, b.wu, b.wd = [r.at[layer % 2] for r in held]
    lat = lax.axis_index("lat")
    lon = lax.axis_index("lon")
    bands = lax.axis_size("lat")
    wet0 = s_wet[lon, lat * 4 + first] == 1
    wet1 = s_wet[lon, lat * 4 + first + 1] == 1
    masked = None
    if layer % 2 == 1 and first == 2:
        masked = lat == bands - 1

    @pl.when(jnp.logical_and(wet0, wet1))
    def _():
        run_windows(b, [0, 1], None if masked is None else [jnp.bool_(False), masked])

    @pl.when(wet0 != wet1)
    def _():
        which = jnp.where(wet1, 1, 0)
        run_windows(b, [which], None if masked is None else [jnp.logical_and(masked, wet1)])

    for low, high, half, target, to in stores:
        outs[target][to : to + high - low] = xs[low:high, half]
    for c in late:
        c.wait()


VM = pl.BlockSpec(memory_space=pltpu.VMEM)


def stage(layer, first, wet, params, held, ins, loads, aliased, outs, stores, name):
    n_in, n_alias = len(ins), len(aliased)
    fetch = () if params is None else (layer, layer + 1) if held is None else (layer + 2, layer + 3)
    shapes = [jax.ShapeDtypeStruct(a.shape, a.dtype) for a in aliased]
    shapes += [jax.ShapeDtypeStruct(s, f32) for s in outs]
    kernel = functools.partial(stage_kernel, layer, first, loads, stores, fetch, n_in, n_alias, len(shapes))
    args = [wet, *(params if fetch else []), *(held or [])]
    before = [HBM] * (8 if fetch else 1) + [VM] * len(held or [])
    start = len(args) + n_in
    extra = []
    for p in params if fetch else []:
        extra.append(jax.ShapeDtypeStruct((2, 1, C) if p.ndim == 2 else (2, *p.shape[1:]), p.dtype))
    n_sems = 1 + 7 * len(fetch)
    return pl.pallas_call(
        kernel,
        out_shape=shapes + extra,
        in_specs=before + [HBM if fetch else VM] * n_in + [VM] * n_alias,
        out_specs=[VM] * len(shapes + extra),
        input_output_aliases={start + i: i for i in range(n_alias)},
        scratch_shapes=[
            pltpu.VMEM((16, 2, 8, C), f32),
            pltpu.VMEM((2 * TOK, 3 * C), bf16),
            pltpu.VMEM((2 * TOK, C), bf16),
            pltpu.SMEM((16, 32), jnp.int32),
            pltpu.SemaphoreType.DMA((n_sems,)),
            pltpu.SemaphoreType.DMA((max(1, len(loads)),)),
        ],
        compiler_params=pltpu.CompilerParams(vmem_limit_bytes=24 << 20),
        cost_estimate=pl.CostEstimate(flops=4_000_000_000, bytes_accessed=6_000_000, transcendentals=800_000),
        name=name,
    )(*args, *ins, *aliased)


def send(block, d_lat, d_lon):
    n_lat, n_lon = lax.axis_size("lat"), lax.axis_size("lon")
    route = [
        (a * n_lon + b, (a + d_lat) % n_lat * n_lon + (b + d_lon) % n_lon)
        for a in range(n_lat)
        for b in range(n_lon)
    ]
    return lax.ppermute(block, ("lat", "lon"), route)


def finish_kernel(lat_ref, diag_ref, lon_ref, keep_ref, out_ref, sem):
    copies = [
        pltpu.make_async_copy(keep_ref, out_ref.at[4:32, 1], sem.at[3]),
        pltpu.make_async_copy(lat_ref, out_ref.at[0:4, 1], sem.at[0]),
        pltpu.make_async_copy(diag_ref, out_ref.at[0:4, 0], sem.at[1]),
        pltpu.make_async_copy(lon_ref, out_ref.at[4:32, 0], sem.at[2]),
    ]
    for c in copies:
        c.start()
    for c in copies:
        c.wait()


SMALL = (4, 8, C)
STRIP = (28, 8, C)


def local(tokens, wet_flags, ln_attn, w_qkv, w_out, pos_bias, ln_mlp, w_up, w_down):
    params = [ln_attn, w_qkv, w_out, pos_bias, ln_mlp, w_up, w_down]
    wet = wet_flags.transpose(0, 2, 1)
    grid = tokens.reshape(32, 2, 8, C)
    params = [pltpu.with_memory_space_constraint(p, pltpu.HBM) for p in params]
    wet = pltpu.with_memory_space_constraint(wet, pltpu.HBM)
    grid = pltpu.with_memory_space_constraint(grid, pltpu.HBM)
    held = None
    for pair in range(LAYERS // 2):
        even, odd = 2 * pair, 2 * pair + 1
        if pair == 0:
            ins_a = ins_b = [grid]
            loads_a = [(0, 16, 32, 0, None)]
            loads_b = [(0, 0, 16, 0, None)]
        else:
            ins_a = [keep, back_lon]
            loads_a = [(0, 12, 28, 0, 1), (1, 12, 28, 0, 0)]
            ins_b = [keep, back_lon, back_lat, back_diag]
            loads_b = [(0, 0, 12, 4, 1), (1, 0, 12, 4, 0), (2, 0, 4, 0, 1), (3, 0, 4, 0, 0)]
        fetch = params if pair == 0 else None
        lon, keep_a, *fetched = stage(
            even, 2, wet, fetch, held, ins_a, loads_a, [], [STRIP, STRIP],
            [(0, 16, 0, 0, 12), (0, 16, 1, 1, 12)],
            f"even{pair}a",
        )
        held = fetched or held
        lon, keep, up_lat, up_diag, *fetched = stage(
            even, 0, wet, fetch, held, ins_b, loads_b, [lon, keep_a], [SMALL, SMALL],
            [(4, 16, 0, 0, 0), (4, 16, 1, 1, 0), (0, 4, 1, 2, 0), (0, 4, 0, 3, 0)],
            f"even{pair}b",
        )
        lon = send(lon, 0, -1)
        up_lat = send(up_lat, -1, 0)
        up_diag = send(up_diag, -1, -1)
        back_lon, keep_a = stage(
            odd, 0, wet, None, held, [keep, lon], [(0, 0, 16, 0, 0), (1, 0, 16, 0, 1)],
            [], [STRIP, STRIP],
            [(0, 16, 1, 0, 0), (0, 16, 0, 1, 0)],
            f"odd{pair}a",
        )
        back_lon, keep, back_lat, back_diag = stage(
            odd, 2, wet, None, held, [keep, lon, up_lat, up_diag],
            [(0, 16, 28, 0, 0), (1, 16, 28, 0, 1), (2, 0, 4, 12, 0), (3, 0, 4, 12, 1)],
            [back_lon, keep_a], [SMALL, SMALL],
            [(0, 12, 1, 0, 16), (0, 12, 0, 1, 16), (12, 16, 0, 2, 0), (12, 16, 1, 3, 0)],
            f"odd{pair}b",
        )
        back_lon = send(back_lon, 0, 1)
        back_lat = send(back_lat, 1, 0)
        back_diag = send(back_diag, 1, 1)
        held = fetched
    out = pl.pallas_call(
        finish_kernel,
        out_shape=jax.ShapeDtypeStruct((32, 2, 8, C), f32),
        in_specs=[VM] * 4,
        out_specs=HBM,
        scratch_shapes=[pltpu.SemaphoreType.DMA((4,))],
        compiler_params=pltpu.CompilerParams(vmem_limit_bytes=4 << 20),
        name="finish",
    )(back_lat, back_diag, back_lon, keep)
    return out.reshape(32, 16, C)


def solution(mesh):
    in_specs = (P("lat", "lon", None), P(), P(), P(), P(), P(), P(), P(), P())
    out_specs = P("lat", "lon", None)
    return jax.shard_map(local, mesh=mesh, in_specs=in_specs, out_specs=out_specs, check_vma=False)
```

```python
import functools

import jax
import jax.numpy as jnp
from jax import lax
from jax.experimental import pallas as pl
from jax.experimental.pallas import tpu as pltpu
from jax.sharding import PartitionSpec as P

C = 384
HEADS = 12
FFN = 1536
TOK = 128
LANES = 128
GROUP = 4
HEAD = 32
LAYERS = 4
CHUNK = 256
norm_eps = 1e-05
mask_fill = -1000000000.0
ERF_POLY = (
    0.7978830000512025,
    0.03633754443795962,
    -3.569087070491613e-05,
    -5.440885213149521e-05,
    3.8449560401057786e-06,
    -1.2507491956239078e-07,
    1.601666137598869e-09,
)
ERF_FLAT = 5.7 * 5.7
f32 = jnp.float32
bf16 = jnp.bfloat16
HBM = pl.BlockSpec(memory_space=pltpu.HBM)


def gelu(x):
    square = jnp.minimum(x * x, ERF_FLAT)
    poly = jnp.float32(ERF_POLY[-1])
    for factor in ERF_POLY[-2::-1]:
        poly = poly * square + factor
    half = 0.5 * x
    return half + half * jnp.tanh(x * poly)


def layer_norm(x, gain):
    center = jnp.mean(x, axis=-1, keepdims=True)
    away = x - center
    spread = jnp.mean(away * away, axis=-1, keepdims=True)
    return (away * lax.rsqrt(spread + norm_eps) * gain).astype(bf16)


def attend(q, k, v, bias_ref, group, masked):
    owner = lax.broadcasted_iota(jnp.int32, (TOK, LANES), 1) // HEAD
    zero = jnp.zeros((TOK, LANES), bf16)
    one = jnp.ones((TOK, LANES), bf16)
    keys = jnp.concatenate([jnp.where(owner == h, k, zero) for h in range(GROUP)], axis=0)
    scores = lax.dot_general(q, keys, (((1,), (1,)), ((), ())), preferred_element_type=f32)
    parts = []
    for h in range(GROUP):
        s = scores[:, h * TOK : (h + 1) * TOK] * HEAD ** (-0.5) + bias_ref[group * GROUP + h]
        if masked is not None:
            s = jnp.where(masked, mask_fill, s)
        parts.append(jnp.exp(s - jnp.max(s, axis=-1, keepdims=True)).astype(bf16))
    weights = jnp.concatenate(parts, axis=1)
    values = jnp.concatenate(
        [
            jnp.concatenate([jnp.where(owner == h, v, zero), jnp.where(owner == h, one, zero)], axis=1)
            for h in range(GROUP)
        ],
        axis=0,
    )
    both = jnp.dot(weights, values, preferred_element_type=f32)
    return (both[:, :LANES] / both[:, LANES:]).astype(bf16)


class Buffers:
    pass


def run_windows(b, ids, masked, ready):
    count = len(ids)
    rows = count * TOK
    x = jnp.concatenate([b.xs[pl.ds(i * 8, 8)].reshape(TOK, C) for i in ids], axis=0)
    ready("ga", "wq")
    b.qkv[:rows] = jnp.dot(layer_norm(x, b.ga[...]), b.wq[...], preferred_element_type=f32).astype(bf16)
    ready("bias")
    for w in range(count):
        span = slice(w * TOK, (w + 1) * TOK)
        hide = None
        if masked is not None:
            low_q = lax.broadcasted_iota(jnp.int32, (TOK, TOK), 0) >= TOK // 2
            low_k = lax.broadcasted_iota(jnp.int32, (TOK, TOK), 1) >= TOK // 2
            hide = jnp.logical_and(low_q != low_k, masked[w])
        for g in range(HEADS // GROUP):
            at = g * LANES
            b.att[span, at : at + LANES] = attend(
                b.qkv[span, at : at + LANES],
                b.qkv[span, C + at : C + at + LANES],
                b.qkv[span, 2 * C + at : 2 * C + at + LANES],
                b.bias,
                g,
                hide,
            )
    ready("wo", "gm")
    resid = x + jnp.dot(b.att[:rows], b.wo[...], preferred_element_type=f32)
    mlp_in = layer_norm(resid, b.gm[...])
    total = resid
    ready("wu", "wd")
    for f in range(0, FFN, CHUNK):
        up = jnp.dot(mlp_in, b.wu[:, f : f + CHUNK], preferred_element_type=f32)
        total = total + jnp.dot(gelu(up).astype(bf16), b.wd[f : f + CHUNK, :], preferred_element_type=f32)
    for w, i in enumerate(ids):
        b.xs[pl.ds(i * 8, 8)] = total[w * TOK : (w + 1) * TOK].reshape(8, 2, 8, C)


NAMES = ("ga", "wq", "bias", "wo", "gm", "wu", "wd")


def start_loads(params, held, layer, sem):
    copies = {}
    for n, name in enumerate(NAMES):
        source = params[n]
        part = source.at[pl.ds(layer, 1)] if len(source.shape) == 2 else source.at[layer]
        copies[name] = pltpu.make_async_copy(part, held[n], sem.at[n])
        copies[name].start()
    return copies


def loader_kernel(layer, *refs):
    for c in start_loads(refs[:7], refs[7:14], layer, refs[14]).values():
        c.wait()


def held_shapes(params):
    return [jax.ShapeDtypeStruct((1, C) if p.ndim == 2 else p.shape[1:], p.dtype) for p in params]


def load_params(layer, params):
    return pl.pallas_call(
        functools.partial(loader_kernel, layer),
        out_shape=held_shapes(params),
        in_specs=[HBM] * 7,
        out_specs=[VM] * 7,
        scratch_shapes=[pltpu.SemaphoreType.DMA((7,))],
        compiler_params=pltpu.CompilerParams(vmem_limit_bytes=8 << 20),
        cost_estimate=pl.CostEstimate(flops=0, bytes_accessed=4_400_000, transcendentals=0),
        name=f"load{layer}",
    )(*params)


def stage_kernel(layer, first, loads, stores, opening, n_in, n_alias, n_out, *refs):
    refs = list(refs)

    def take(count):
        got, refs[:count] = refs[:count], []
        return got

    (wet,) = take(1)
    given = take(7)
    ins = take(n_in)
    take(n_alias)
    outs = take(n_out)
    row = wet
    held = given
    if opening:
        held = take(7)
        (row,) = take(1)
    xs, qkv, att, s_wet, sem, in_sem = refs
    lat = lax.axis_index("lat")
    lon = lax.axis_index("lon")
    bands = lax.axis_size("lat")
    blocks = []
    pending = {}
    if opening:
        flags = pltpu.make_async_copy(wet, s_wet, in_sem.at[len(loads)])
        flags.start()
    for n, (source, low, high, to, half) in enumerate(loads):
        target = xs.at[to : to + high - low] if half is None else xs.at[to : to + high - low, half]
        if half is None:
            blocks.append(pltpu.make_async_copy(ins[source].at[low:high], target, in_sem.at[n]))
            blocks[-1].start()
        else:
            target[...] = ins[source][low:high]
    if opening:
        pending = start_loads(given, held, layer, sem)
        flags.wait()
        which_layer = lax.broadcasted_iota(jnp.int32, (8, LANES), 0)
        which_window = lax.broadcasted_iota(jnp.int32, (8, LANES), 1)
        mine = jnp.zeros((8, LANES), jnp.int32)
        for n in range(LAYERS):
            for j in range(4):
                here = jnp.logical_and(which_layer == n, which_window == j)
                mine = jnp.where(here, s_wet[n, lon, lat * 4 + j], mine)
        row[...] = mine
        wet0 = s_wet[layer, lon, lat * 4 + first] == 1
        wet1 = s_wet[layer, lon, lat * 4 + first + 1] == 1
    else:
        wet0 = row[layer, first] == 1
        wet1 = row[layer, first + 1] == 1
    for c in blocks:
        c.wait()

    def ready(*names):
        for name in names:
            if name in pending:
                pending[name].wait()

    b = Buffers()
    b.xs, b.qkv, b.att = xs, qkv, att
    b.ga, b.wq, b.bias, b.wo, b.gm, b.wu, b.wd = held
    masked = None
    if layer % 2 == 1 and first == 2:
        masked = lat == bands - 1

    @pl.when(jnp.logical_and(wet0, wet1))
    def _():
        run_windows(b, [0, 1], None if masked is None else [jnp.bool_(False), masked], ready)

    @pl.when(wet0 != wet1)
    def _():
        which = jnp.where(wet1, 1, 0)
        run_windows(b, [which], None if masked is None else [jnp.logical_and(masked, wet1)], ready)

    if opening:

        @pl.when(jnp.logical_not(jnp.logical_or(wet0, wet1)))
        def _():
            ready(*NAMES)

    for low, high, half, target, to in stores:
        outs[target][to : to + high - low] = xs[low:high, half]


VM = pl.BlockSpec(memory_space=pltpu.VMEM)


def stage(layer, first, wet, held, ins, loads, aliased, outs, stores, name, opening=False):
    n_in, n_alias = len(ins), len(aliased)
    shapes = [jax.ShapeDtypeStruct(a.shape, a.dtype) for a in aliased]
    shapes += [jax.ShapeDtypeStruct(s, f32) for s in outs]
    kernel = functools.partial(stage_kernel, layer, first, loads, stores, opening, n_in, n_alias, len(shapes))
    extra = held_shapes(held) + [jax.ShapeDtypeStruct((8, LANES), jnp.int32)] if opening else []
    ahead = [HBM if opening else VM] * 8
    in_blocks = [HBM if load[4] is None else VM for load in loads[:1]] * n_in
    return pl.pallas_call(
        kernel,
        out_shape=shapes + extra,
        in_specs=ahead + in_blocks + [VM] * n_alias,
        out_specs=[VM] * len(shapes + extra),
        input_output_aliases={8 + n_in + i: i for i in range(n_alias)},
        scratch_shapes=[
            pltpu.VMEM((16, 2, 8, C), f32),
            pltpu.VMEM((2 * TOK, 3 * C), bf16),
            pltpu.VMEM((2 * TOK, C), bf16),
            pltpu.SMEM((LAYERS, 16, 32), jnp.int32),
            pltpu.SemaphoreType.DMA((7,)),
            pltpu.SemaphoreType.DMA((1 + len(loads),)),
        ],
        compiler_params=pltpu.CompilerParams(vmem_limit_bytes=24 << 20),
        cost_estimate=pl.CostEstimate(flops=4_000_000_000, bytes_accessed=6_000_000, transcendentals=800_000),
        name=name,
    )(wet, *held, *ins, *aliased)


def send(block, d_lat, d_lon):
    n_lat, n_lon = lax.axis_size("lat"), lax.axis_size("lon")
    route = [
        (a * n_lon + b, (a + d_lat) % n_lat * n_lon + (b + d_lon) % n_lon)
        for a in range(n_lat)
        for b in range(n_lon)
    ]
    return lax.ppermute(block, ("lat", "lon"), route)


def finish_kernel(lat_ref, diag_ref, low_ref, high_ref, keep_ref, out_ref, sem):
    copies = [
        pltpu.make_async_copy(keep_ref, out_ref.at[4:32, 1], sem.at[3]),
        pltpu.make_async_copy(lat_ref, out_ref.at[0:4, 1], sem.at[0]),
        pltpu.make_async_copy(diag_ref, out_ref.at[0:4, 0], sem.at[1]),
        pltpu.make_async_copy(low_ref, out_ref.at[4:20, 0], sem.at[2]),
        pltpu.make_async_copy(high_ref, out_ref.at[20:32, 0], sem.at[4]),
    ]
    for c in copies:
        c.start()
    for c in copies:
        c.wait()


SMALL = (4, 8, C)
HALF_A = (16, 8, C)
HALF_B = (12, 8, C)
STRIP = (28, 8, C)


def local(tokens, wet_flags, ln_attn, w_qkv, w_out, pos_bias, ln_mlp, w_up, w_down):
    params = [ln_attn, w_qkv, pos_bias, w_out, ln_mlp, w_up, w_down]
    wet = wet_flags.transpose(0, 2, 1)
    grid = tokens.reshape(32, 2, 8, C)
    params = [pltpu.with_memory_space_constraint(p, pltpu.HBM) for p in params]
    wet = pltpu.with_memory_space_constraint(wet, pltpu.HBM)
    grid = pltpu.with_memory_space_constraint(grid, pltpu.HBM)
    held = params
    for pair in range(LAYERS // 2):
        even, odd = 2 * pair, 2 * pair + 1
        opening = pair == 0
        if opening:
            ins_a = ins_b = [grid]
            loads_a = [(0, 16, 32, 0, None)]
            loads_b = [(0, 0, 16, 0, None)]
        else:
            held = load_params(even, params)
            ins_a = [keep, back_a, back_b]
            loads_a = [(0, 12, 28, 0, 1), (1, 12, 16, 0, 0), (2, 0, 12, 4, 0)]
            ins_b = [keep, back_a, back_lat, back_diag]
            loads_b = [(0, 0, 12, 4, 1), (1, 0, 12, 4, 0), (2, 0, 4, 0, 1), (3, 0, 4, 0, 0)]
        west_a, keep_a, *fetched = stage(
            even, 2, wet, held, ins_a, loads_a, [], [HALF_A, STRIP],
            [(0, 16, 0, 0, 0), (0, 16, 1, 1, 12)],
            f"even{pair}a", opening,
        )
        if opening:
            *held, wet = fetched
        west_a = send(west_a, 0, -1)
        keep, west_b, up_lat, up_diag = stage(
            even, 0, wet, held, ins_b, loads_b, [keep_a], [HALF_B, SMALL, SMALL],
            [(4, 16, 1, 0, 0), (4, 16, 0, 1, 0), (0, 4, 1, 2, 0), (0, 4, 0, 3, 0)],
            f"even{pair}b",
        )
        west_b = send(west_b, 0, -1)
        up_lat = send(up_lat, -1, 0)
        up_diag = send(up_diag, -1, -1)
        held = load_params(odd, params)
        back_a, keep_a = stage(
            odd, 0, wet, held, [keep, west_b, west_a],
            [(0, 0, 16, 0, 0), (1, 0, 12, 0, 1), (2, 0, 4, 12, 1)],
            [], [HALF_A, STRIP],
            [(0, 16, 1, 0, 0), (0, 16, 0, 1, 0)],
            f"odd{pair}a",
        )
        back_a = send(back_a, 0, 1)
        keep, back_b, back_lat, back_diag = stage(
            odd, 2, wet, held, [keep, west_a, up_lat, up_diag],
            [(0, 16, 28, 0, 0), (1, 4, 16, 0, 1), (2, 0, 4, 12, 0), (3, 0, 4, 12, 1)],
            [keep_a], [HALF_B, SMALL, SMALL],
            [(0, 12, 0, 0, 16), (0, 12, 1, 1, 0), (12, 16, 0, 2, 0), (12, 16, 1, 3, 0)],
            f"odd{pair}b",
        )
        back_b = send(back_b, 0, 1)
        back_lat = send(back_lat, 1, 0)
        back_diag = send(back_diag, 1, 1)
    out = pl.pallas_call(
        finish_kernel,
        out_shape=jax.ShapeDtypeStruct((32, 2, 8, C), f32),
        in_specs=[VM] * 5,
        out_specs=HBM,
        scratch_shapes=[pltpu.SemaphoreType.DMA((5,))],
        compiler_params=pltpu.CompilerParams(vmem_limit_bytes=4 << 20),
        name="finish",
    )(back_lat, back_diag, back_a, back_b, keep)
    return out.reshape(32, 16, C)


def solution(mesh):
    in_specs = (P("lat", "lon", None), P(), P(), P(), P(), P(), P(), P(), P())
    out_specs = P("lat", "lon", None)
    return jax.shard_map(local, mesh=mesh, in_specs=in_specs, out_specs=out_specs, check_vma=False)
```

```python
import functools

import jax
import jax.numpy as jnp
from jax import lax
from jax.experimental import pallas as pl
from jax.experimental.pallas import tpu as pltpu
from jax.sharding import PartitionSpec as P

C = 384
HEADS = 12
FFN = 1536
TOK = 128
LANES = 128
GROUP = 4
HEAD = 32
LAYERS = 4
CHUNK = 256
norm_eps = 1e-05
mask_fill = -1000000000.0
ERF_POLY = (
    0.7978830000512025,
    0.03633754443795962,
    -3.569087070491613e-05,
    -5.440885213149521e-05,
    3.8449560401057786e-06,
    -1.2507491956239078e-07,
    1.601666137598869e-09,
)
ERF_FLAT = 5.7 * 5.7
f32 = jnp.float32
bf16 = jnp.bfloat16
HBM = pl.BlockSpec(memory_space=pltpu.HBM)


def gelu(x):
    square = jnp.minimum(x * x, ERF_FLAT)
    poly = jnp.float32(ERF_POLY[-1])
    for factor in ERF_POLY[-2::-1]:
        poly = poly * square + factor
    half = 0.5 * x
    return half + half * jnp.tanh(x * poly)


def layer_norm(x, gain):
    center = jnp.mean(x, axis=-1, keepdims=True)
    away = x - center
    spread = jnp.mean(away * away, axis=-1, keepdims=True)
    return (away * lax.rsqrt(spread + norm_eps) * gain).astype(bf16)


def attend(q, k, v, bias_ref, group, masked):
    owner = lax.broadcasted_iota(jnp.int32, (TOK, LANES), 1) // HEAD
    zero = jnp.zeros((TOK, LANES), bf16)
    one = jnp.ones((TOK, LANES), bf16)
    keys = jnp.concatenate([jnp.where(owner == h, k, zero) for h in range(GROUP)], axis=0)
    scores = lax.dot_general(q, keys, (((1,), (1,)), ((), ())), preferred_element_type=f32)
    parts = []
    for h in range(GROUP):
        s = scores[:, h * TOK : (h + 1) * TOK] * HEAD ** (-0.5) + bias_ref[group * GROUP + h]
        if masked is not None:
            s = jnp.where(masked, mask_fill, s)
        parts.append(jnp.exp(s - jnp.max(s, axis=-1, keepdims=True)).astype(bf16))
    weights = jnp.concatenate(parts, axis=1)
    values = jnp.concatenate(
        [
            jnp.concatenate([jnp.where(owner == h, v, zero), jnp.where(owner == h, one, zero)], axis=1)
            for h in range(GROUP)
        ],
        axis=0,
    )
    both = jnp.dot(weights, values, preferred_element_type=f32)
    return (both[:, :LANES] / both[:, LANES:]).astype(bf16)


class Buffers:
    pass


def run_windows(b, ids, masked, ready):
    count = len(ids)
    rows = count * TOK
    x = jnp.concatenate([b.xs[pl.ds(i * 8, 8)].reshape(TOK, C) for i in ids], axis=0)
    ready("ga", "wq")
    b.qkv[:rows] = jnp.dot(layer_norm(x, b.ga[...]), b.wq[...], preferred_element_type=f32).astype(bf16)
    ready("bias")
    for w in range(count):
        span = slice(w * TOK, (w + 1) * TOK)
        hide = None
        if masked is not None:
            low_q = lax.broadcasted_iota(jnp.int32, (TOK, TOK), 0) >= TOK // 2
            low_k = lax.broadcasted_iota(jnp.int32, (TOK, TOK), 1) >= TOK // 2
            hide = jnp.logical_and(low_q != low_k, masked[w])
        for g in range(HEADS // GROUP):
            at = g * LANES
            b.att[span, at : at + LANES] = attend(
                b.qkv[span, at : at + LANES],
                b.qkv[span, C + at : C + at + LANES],
                b.qkv[span, 2 * C + at : 2 * C + at + LANES],
                b.bias,
                g,
                hide,
            )
    ready("wo", "gm")
    resid = x + jnp.dot(b.att[:rows], b.wo[...], preferred_element_type=f32)
    mlp_in = layer_norm(resid, b.gm[...])
    total = resid
    ready("wu", "wd")
    for f in range(0, FFN, CHUNK):
        up = jnp.dot(mlp_in, b.wu[:, f : f + CHUNK], preferred_element_type=f32)
        total = total + jnp.dot(gelu(up).astype(bf16), b.wd[f : f + CHUNK, :], preferred_element_type=f32)
    for w, i in enumerate(ids):
        b.xs[pl.ds(i * 8, 8)] = total[w * TOK : (w + 1) * TOK].reshape(8, 2, 8, C)


NAMES = ("ga", "wq", "bias", "wo", "gm", "wu", "wd")


def start_loads(params, held, layer, sem):
    copies = {}
    for n, name in enumerate(NAMES):
        source = params[n]
        part = source.at[pl.ds(layer, 1)] if len(source.shape) == 2 else source.at[layer]
        copies[name] = pltpu.make_async_copy(part, held[n], sem.at[n])
        copies[name].start()
    return copies


def held_shapes(params):
    return [jax.ShapeDtypeStruct((1, C) if p.ndim == 2 else p.shape[1:], p.dtype) for p in params]


def stage_kernel(layer, first, loads, stores, opening, brings, n_in, n_alias, n_out, *refs):
    refs = list(refs)

    def take(count):
        got, refs[:count] = refs[:count], []
        return got

    (wet,) = take(1)
    given = take(7)
    ins = take(n_in)
    take(n_alias)
    coming = take(7) if brings else []
    outs = take(n_out)
    row = wet
    held = given
    if opening:
        held = take(7)
        (row,) = take(1)
    arrived = take(7) if brings else []
    xs, qkv, att, s_wet, sem, in_sem = refs
    lat = lax.axis_index("lat")
    lon = lax.axis_index("lon")
    bands = lax.axis_size("lat")
    blocks = []
    pending = {}
    ahead = start_loads(coming, arrived, layer + 1, sem) if brings else {}
    if opening:
        flags = pltpu.make_async_copy(wet, s_wet, in_sem.at[len(loads)])
        flags.start()
    for n, (source, low, high, to, half) in enumerate(loads):
        target = xs.at[to : to + high - low] if half is None else xs.at[to : to + high - low, half]
        if half is None:
            blocks.append(pltpu.make_async_copy(ins[source].at[low:high], target, in_sem.at[n]))
            blocks[-1].start()
        else:
            target[...] = ins[source][low:high]
    if opening:
        pending = start_loads(given, held, layer, sem)
        flags.wait()
        which_layer = lax.broadcasted_iota(jnp.int32, (8, LANES), 0)
        which_window = lax.broadcasted_iota(jnp.int32, (8, LANES), 1)
        mine = jnp.zeros((8, LANES), jnp.int32)
        for n in range(LAYERS):
            for j in range(4):
                here = jnp.logical_and(which_layer == n, which_window == j)
                mine = jnp.where(here, s_wet[n, lon, lat * 4 + j], mine)
        row[...] = mine
        wet0 = s_wet[layer, lon, lat * 4 + first] == 1
        wet1 = s_wet[layer, lon, lat * 4 + first + 1] == 1
    else:
        wet0 = row[layer, first] == 1
        wet1 = row[layer, first + 1] == 1
    for c in blocks:
        c.wait()

    def ready(*names):
        for name in names:
            if name in pending:
                pending[name].wait()

    b = Buffers()
    b.xs, b.qkv, b.att = xs, qkv, att
    b.ga, b.wq, b.bias, b.wo, b.gm, b.wu, b.wd = held
    masked = None
    if layer % 2 == 1 and first == 2:
        masked = lat == bands - 1

    @pl.when(jnp.logical_and(wet0, wet1))
    def _():
        run_windows(b, [0, 1], None if masked is None else [jnp.bool_(False), masked], ready)

    @pl.when(wet0 != wet1)
    def _():
        which = jnp.where(wet1, 1, 0)
        run_windows(b, [which], None if masked is None else [jnp.logical_and(masked, wet1)], ready)

    if opening:

        @pl.when(jnp.logical_not(jnp.logical_or(wet0, wet1)))
        def _():
            ready(*NAMES)

    for low, high, half, target, to in stores:
        outs[target][to : to + high - low] = xs[low:high, half]
    for c in ahead.values():
        c.wait()


VM = pl.BlockSpec(memory_space=pltpu.VMEM)


def stage(layer, first, wet, held, ins, loads, aliased, outs, stores, name, opening=False, brings=()):
    n_in, n_alias = len(ins), len(aliased)
    shapes = [jax.ShapeDtypeStruct(a.shape, a.dtype) for a in aliased]
    shapes += [jax.ShapeDtypeStruct(s, f32) for s in outs]
    kernel = functools.partial(stage_kernel, layer, first, loads, stores, opening, bool(brings), n_in, n_alias, len(shapes))
    extra = held_shapes(held) + [jax.ShapeDtypeStruct((8, LANES), jnp.int32)] if opening else []
    extra += held_shapes(brings)
    ahead = [HBM if opening else VM] * 8
    in_blocks = [HBM if load[4] is None else VM for load in loads[:1]] * n_in
    return pl.pallas_call(
        kernel,
        out_shape=shapes + extra,
        in_specs=ahead + in_blocks + [VM] * n_alias + [HBM] * len(brings),
        out_specs=[VM] * len(shapes + extra),
        input_output_aliases={8 + n_in + i: i for i in range(n_alias)},
        scratch_shapes=[
            pltpu.VMEM((16, 2, 8, C), f32),
            pltpu.VMEM((2 * TOK, 3 * C), bf16),
            pltpu.VMEM((2 * TOK, C), bf16),
            pltpu.SMEM((LAYERS, 16, 32), jnp.int32),
            pltpu.SemaphoreType.DMA((7,)),
            pltpu.SemaphoreType.DMA((1 + len(loads),)),
        ],
        compiler_params=pltpu.CompilerParams(vmem_limit_bytes=24 << 20),
        cost_estimate=pl.CostEstimate(flops=4_000_000_000, bytes_accessed=6_000_000, transcendentals=800_000),
        name=name,
    )(wet, *held, *ins, *aliased, *brings)


def send(block, d_lat, d_lon):
    n_lat, n_lon = lax.axis_size("lat"), lax.axis_size("lon")
    route = [
        (a * n_lon + b, (a + d_lat) % n_lat * n_lon + (b + d_lon) % n_lon)
        for a in range(n_lat)
        for b in range(n_lon)
    ]
    return lax.ppermute(block, ("lat", "lon"), route)


def finish_kernel(lat_ref, diag_ref, low_ref, high_ref, keep_ref, out_ref, sem):
    copies = [
        pltpu.make_async_copy(keep_ref, out_ref.at[4:32, 1], sem.at[3]),
        pltpu.make_async_copy(lat_ref, out_ref.at[0:4, 1], sem.at[0]),
        pltpu.make_async_copy(diag_ref, out_ref.at[0:4, 0], sem.at[1]),
        pltpu.make_async_copy(low_ref, out_ref.at[4:20, 0], sem.at[2]),
        pltpu.make_async_copy(high_ref, out_ref.at[20:32, 0], sem.at[4]),
    ]
    for c in copies:
        c.start()
    for c in copies:
        c.wait()


SMALL = (4, 8, C)
HALF_A = (16, 8, C)
HALF_B = (12, 8, C)
STRIP = (28, 8, C)


def local(tokens, wet_flags, ln_attn, w_qkv, w_out, pos_bias, ln_mlp, w_up, w_down):
    params = [ln_attn, w_qkv, pos_bias, w_out, ln_mlp, w_up, w_down]
    wet = wet_flags.transpose(0, 2, 1)
    grid = tokens.reshape(32, 2, 8, C)
    params = [pltpu.with_memory_space_constraint(p, pltpu.HBM) for p in params]
    wet = pltpu.with_memory_space_constraint(wet, pltpu.HBM)
    grid = pltpu.with_memory_space_constraint(grid, pltpu.HBM)
    held = params
    for pair in range(LAYERS // 2):
        even, odd = 2 * pair, 2 * pair + 1
        opening = pair == 0
        if opening:
            ins_a = ins_b = [grid]
            loads_a = [(0, 16, 32, 0, None)]
            loads_b = [(0, 0, 16, 0, None)]
        else:
            ins_a = [keep, back_a, back_b]
            loads_a = [(0, 12, 28, 0, 1), (1, 12, 16, 0, 0), (2, 0, 12, 4, 0)]
            ins_b = [keep, back_a, back_lat, back_diag]
            loads_b = [(0, 0, 12, 4, 1), (1, 0, 12, 4, 0), (2, 0, 4, 0, 1), (3, 0, 4, 0, 0)]
        west_a, keep_a, *fetched = stage(
            even, 2, wet, held, ins_a, loads_a, [], [HALF_A, STRIP],
            [(0, 16, 0, 0, 0), (0, 16, 1, 1, 12)],
            f"even{pair}a", opening,
        )
        if opening:
            *held, wet = fetched
        west_a = send(west_a, 0, -1)
        keep, west_b, up_lat, up_diag, *coming = stage(
            even, 0, wet, held, ins_b, loads_b, [keep_a], [HALF_B, SMALL, SMALL],
            [(4, 16, 1, 0, 0), (4, 16, 0, 1, 0), (0, 4, 1, 2, 0), (0, 4, 0, 3, 0)],
            f"even{pair}b", brings=params,
        )
        west_b = send(west_b, 0, -1)
        up_lat = send(up_lat, -1, 0)
        up_diag = send(up_diag, -1, -1)
        held = coming
        back_a, keep_a = stage(
            odd, 0, wet, held, [keep, west_b, west_a],
            [(0, 0, 16, 0, 0), (1, 0, 12, 0, 1), (2, 0, 4, 12, 1)],
            [], [HALF_A, STRIP],
            [(0, 16, 1, 0, 0), (0, 16, 0, 1, 0)],
            f"odd{pair}a",
        )
        back_a = send(back_a, 0, 1)
        keep, back_b, back_lat, back_diag, *coming = stage(
            odd, 2, wet, held, [keep, west_a, up_lat, up_diag],
            [(0, 16, 28, 0, 0), (1, 4, 16, 0, 1), (2, 0, 4, 12, 0), (3, 0, 4, 12, 1)],
            [keep_a], [HALF_B, SMALL, SMALL],
            [(0, 12, 0, 0, 16), (0, 12, 1, 1, 0), (12, 16, 0, 2, 0), (12, 16, 1, 3, 0)],
            f"odd{pair}b", brings=params if odd + 1 < LAYERS else [],
        )
        back_b = send(back_b, 0, 1)
        back_lat = send(back_lat, 1, 0)
        back_diag = send(back_diag, 1, 1)
        held = coming
    out = pl.pallas_call(
        finish_kernel,
        out_shape=jax.ShapeDtypeStruct((32, 2, 8, C), f32),
        in_specs=[VM] * 5,
        out_specs=HBM,
        scratch_shapes=[pltpu.SemaphoreType.DMA((5,))],
        compiler_params=pltpu.CompilerParams(vmem_limit_bytes=4 << 20),
        name="finish",
    )(back_lat, back_diag, back_a, back_b, keep)
    return out.reshape(32, 16, C)


def solution(mesh):
    in_specs = (P("lat", "lon", None), P(), P(), P(), P(), P(), P(), P(), P())
    out_specs = P("lat", "lon", None)
    return jax.shard_map(local, mesh=mesh, in_specs=in_specs, out_specs=out_specs, check_vma=False)
```

```python
import functools

import jax
import jax.numpy as jnp
from jax import lax
from jax.experimental import pallas as pl
from jax.experimental.pallas import tpu as pltpu
from jax.sharding import PartitionSpec as P

C = 384
HEADS = 12
FFN = 1536
TOK = 128
LANES = 128
GROUP = 4
HEAD = 32
LAYERS = 4
CHUNK = 256
norm_eps = 1e-05
mask_fill = -1000000000.0
ERF_POLY = (
    0.7978830000512025,
    0.03633754443795962,
    -3.569087070491613e-05,
    -5.440885213149521e-05,
    3.8449560401057786e-06,
    -1.2507491956239078e-07,
    1.601666137598869e-09,
)
ERF_FLAT = 5.7 * 5.7
f32 = jnp.float32
bf16 = jnp.bfloat16
HBM = pl.BlockSpec(memory_space=pltpu.HBM)


def gelu(x):
    square = jnp.minimum(x * x, ERF_FLAT)
    poly = jnp.float32(ERF_POLY[-1])
    for factor in ERF_POLY[-2::-1]:
        poly = poly * square + factor
    half = 0.5 * x
    return half + half * jnp.tanh(x * poly)


def layer_norm(x, gain):
    center = jnp.mean(x, axis=-1, keepdims=True)
    away = x - center
    spread = jnp.mean(away * away, axis=-1, keepdims=True)
    return (away * lax.rsqrt(spread + norm_eps) * gain).astype(bf16)


def attend(q, k, v, bias_ref, group, masked):
    owner = lax.broadcasted_iota(jnp.int32, (TOK, LANES), 1) // HEAD
    zero = jnp.zeros((TOK, LANES), bf16)
    one = jnp.ones((TOK, LANES), bf16)
    keys = jnp.concatenate([jnp.where(owner == h, k, zero) for h in range(GROUP)], axis=0)
    scores = lax.dot_general(q, keys, (((1,), (1,)), ((), ())), preferred_element_type=f32)
    parts = []
    for h in range(GROUP):
        s = scores[:, h * TOK : (h + 1) * TOK] * HEAD ** (-0.5) + bias_ref[group * GROUP + h]
        if masked is not None:
            s = jnp.where(masked, mask_fill, s)
        parts.append(jnp.exp(s - jnp.max(s, axis=-1, keepdims=True)).astype(bf16))
    weights = jnp.concatenate(parts, axis=1)
    values = jnp.concatenate(
        [
            jnp.concatenate([jnp.where(owner == h, v, zero), jnp.where(owner == h, one, zero)], axis=1)
            for h in range(GROUP)
        ],
        axis=0,
    )
    both = jnp.dot(weights, values, preferred_element_type=f32)
    return (both[:, :LANES] / both[:, LANES:]).astype(bf16)


class Buffers:
    pass


def run_windows(b, ids, masked, ready):
    count = len(ids)
    rows = count * TOK
    x = jnp.concatenate([b.xs[pl.ds(i * 8, 8)].reshape(TOK, C) for i in ids], axis=0)
    ready("ga", "wq")
    b.qkv[:rows] = jnp.dot(layer_norm(x, b.ga[...]), b.wq[...], preferred_element_type=f32).astype(bf16)
    ready("bias")
    for w in range(count):
        span = slice(w * TOK, (w + 1) * TOK)
        hide = None
        if masked is not None:
            low_q = lax.broadcasted_iota(jnp.int32, (TOK, TOK), 0) >= TOK // 2
            low_k = lax.broadcasted_iota(jnp.int32, (TOK, TOK), 1) >= TOK // 2
            hide = jnp.logical_and(low_q != low_k, masked[w])
        for g in range(HEADS // GROUP):
            at = g * LANES
            b.att[span, at : at + LANES] = attend(
                b.qkv[span, at : at + LANES],
                b.qkv[span, C + at : C + at + LANES],
                b.qkv[span, 2 * C + at : 2 * C + at + LANES],
                b.bias,
                g,
                hide,
            )
    ready("wo", "gm")
    resid = x + jnp.dot(b.att[:rows], b.wo[...], preferred_element_type=f32)
    mlp_in = layer_norm(resid, b.gm[...])
    total = resid
    ready("wu", "wd")
    for f in range(0, FFN, CHUNK):
        up = jnp.dot(mlp_in, b.wu[:, f : f + CHUNK], preferred_element_type=f32)
        total = total + jnp.dot(gelu(up).astype(bf16), b.wd[f : f + CHUNK, :], preferred_element_type=f32)
    for w, i in enumerate(ids):
        b.xs[pl.ds(i * 8, 8)] = total[w * TOK : (w + 1) * TOK].reshape(8, 2, 8, C)


NAMES = ("ga", "wq", "bias", "wo", "gm", "wu", "wd")


def start_loads(params, held, layer, sem):
    copies = {}
    for n, name in enumerate(NAMES):
        source = params[n]
        part = source.at[pl.ds(layer, 1)] if len(source.shape) == 2 else source.at[layer]
        copies[name] = pltpu.make_async_copy(part, held[n], sem.at[n])
        copies[name].start()
    return copies


def held_shapes(params):
    return [jax.ShapeDtypeStruct((1, C) if p.ndim == 2 else p.shape[1:], p.dtype) for p in params]


def stage_kernel(layer, first, loads, stores, opening, brings, n_in, n_alias, n_out, *refs):
    refs = list(refs)

    def take(count):
        got, refs[:count] = refs[:count], []
        return got

    (wet,) = take(1)
    given = take(7)
    ins = take(n_in)
    take(n_alias)
    coming = take(7) if brings else []
    outs = take(n_out)
    row = wet
    held = given
    if opening:
        held = take(7)
        (row,) = take(1)
    arrived = take(7) if brings else []
    xs, qkv, att, s_wet, sem, in_sem = refs
    lat = lax.axis_index("lat")
    lon = lax.axis_index("lon")
    bands = lax.axis_size("lat")
    blocks = []
    pending = {}
    if opening:
        flags = pltpu.make_async_copy(wet, s_wet, in_sem.at[len(loads)])
        flags.start()
    for n, (source, low, high, to, half) in enumerate(loads):
        target = xs.at[to : to + high - low] if half is None else xs.at[to : to + high - low, half]
        if half is None:
            blocks.append(pltpu.make_async_copy(ins[source].at[low:high], target, in_sem.at[n]))
            blocks[-1].start()
        else:
            target[...] = ins[source][low:high]
    ahead = start_loads(coming, arrived, layer + 1, sem) if brings else {}
    if opening:
        pending = start_loads(given, held, layer, sem)
        flags.wait()
        which_layer = lax.broadcasted_iota(jnp.int32, (8, LANES), 0)
        which_window = lax.broadcasted_iota(jnp.int32, (8, LANES), 1)
        mine = jnp.zeros((8, LANES), jnp.int32)
        for n in range(LAYERS):
            for j in range(4):
                here = jnp.logical_and(which_layer == n, which_window == j)
                mine = jnp.where(here, s_wet[n, lon, lat * 4 + j], mine)
        row[...] = mine
        wet0 = s_wet[layer, lon, lat * 4 + first] == 1
        wet1 = s_wet[layer, lon, lat * 4 + first + 1] == 1
    else:
        wet0 = row[layer, first] == 1
        wet1 = row[layer, first + 1] == 1
    for c in blocks:
        c.wait()

    def ready(*names):
        for name in names:
            if name in pending:
                pending[name].wait()

    b = Buffers()
    b.xs, b.qkv, b.att = xs, qkv, att
    b.ga, b.wq, b.bias, b.wo, b.gm, b.wu, b.wd = held
    masked = None
    if layer % 2 == 1 and first == 2:
        masked = lat == bands - 1

    @pl.when(jnp.logical_and(wet0, wet1))
    def _():
        run_windows(b, [0, 1], None if masked is None else [jnp.bool_(False), masked], ready)

    @pl.when(wet0 != wet1)
    def _():
        which = jnp.where(wet1, 1, 0)
        run_windows(b, [which], None if masked is None else [jnp.logical_and(masked, wet1)], ready)

    if opening:

        @pl.when(jnp.logical_not(jnp.logical_or(wet0, wet1)))
        def _():
            ready(*NAMES)

    for low, high, half, target, to in stores:
        outs[target][to : to + high - low] = xs[low:high, half]
    for c in ahead.values():
        c.wait()


VM = pl.BlockSpec(memory_space=pltpu.VMEM)


def stage(layer, first, wet, held, ins, loads, aliased, outs, stores, name, opening=False, brings=()):
    n_in, n_alias = len(ins), len(aliased)
    shapes = [jax.ShapeDtypeStruct(a.shape, a.dtype) for a in aliased]
    shapes += [jax.ShapeDtypeStruct(s, f32) for s in outs]
    kernel = functools.partial(stage_kernel, layer, first, loads, stores, opening, bool(brings), n_in, n_alias, len(shapes))
    extra = held_shapes(held) + [jax.ShapeDtypeStruct((8, LANES), jnp.int32)] if opening else []
    extra += held_shapes(brings)
    ahead = [HBM if opening else VM] * 8
    in_blocks = [HBM if load[4] is None else VM for load in loads[:1]] * n_in
    return pl.pallas_call(
        kernel,
        out_shape=shapes + extra,
        in_specs=ahead + in_blocks + [VM] * n_alias + [HBM] * len(brings),
        out_specs=[VM] * len(shapes + extra),
        input_output_aliases={8 + n_in + i: i for i in range(n_alias)},
        scratch_shapes=[
            pltpu.VMEM((16, 2, 8, C), f32),
            pltpu.VMEM((2 * TOK, 3 * C), bf16),
            pltpu.VMEM((2 * TOK, C), bf16),
            pltpu.SMEM((LAYERS, 16, 32), jnp.int32),
            pltpu.SemaphoreType.DMA((7,)),
            pltpu.SemaphoreType.DMA((1 + len(loads),)),
        ],
        compiler_params=pltpu.CompilerParams(vmem_limit_bytes=24 << 20),
        cost_estimate=pl.CostEstimate(flops=4_000_000_000, bytes_accessed=6_000_000, transcendentals=800_000),
        name=name,
    )(wet, *held, *ins, *aliased, *brings)


def send(block, d_lat, d_lon):
    n_lat, n_lon = lax.axis_size("lat"), lax.axis_size("lon")
    route = [
        (a * n_lon + b, (a + d_lat) % n_lat * n_lon + (b + d_lon) % n_lon)
        for a in range(n_lat)
        for b in range(n_lon)
    ]
    return lax.ppermute(block, ("lat", "lon"), route)


def relay_kernel(*refs):
    del refs


def relay(*arrays):
    return pl.pallas_call(
        relay_kernel,
        out_shape=[jax.ShapeDtypeStruct(a.shape, a.dtype) for a in arrays],
        in_specs=[VM] * len(arrays),
        out_specs=[VM] * len(arrays),
        input_output_aliases={i: i for i in range(len(arrays))},
        compiler_params=pltpu.CompilerParams(vmem_limit_bytes=4 << 20),
        cost_estimate=pl.CostEstimate(flops=8_000_000_000, bytes_accessed=6_000_000, transcendentals=0),
        name="relay",
    )(*arrays)


def finish_kernel(lat_ref, diag_ref, high_ref, low_ref, keep_ref, out_ref, sem):
    copies = [
        pltpu.make_async_copy(keep_ref, out_ref.at[4:32, 1], sem.at[3]),
        pltpu.make_async_copy(lat_ref, out_ref.at[0:4, 1], sem.at[0]),
        pltpu.make_async_copy(diag_ref, out_ref.at[0:4, 0], sem.at[1]),
        pltpu.make_async_copy(high_ref, out_ref.at[20:32, 0], sem.at[2]),
        pltpu.make_async_copy(low_ref, out_ref.at[4:20, 0], sem.at[4]),
    ]
    for c in copies:
        c.start()
    for c in copies:
        c.wait()


SMALL = (4, 8, C)
PART_A = (12, 8, C)
PART_B = (16, 8, C)
STRIP = (28, 8, C)


def local(tokens, wet_flags, ln_attn, w_qkv, w_out, pos_bias, ln_mlp, w_up, w_down):
    params = [ln_attn, w_qkv, pos_bias, w_out, ln_mlp, w_up, w_down]
    wet = wet_flags.transpose(0, 2, 1)
    grid = tokens.reshape(32, 2, 8, C)
    params = [pltpu.with_memory_space_constraint(p, pltpu.HBM) for p in params]
    wet = pltpu.with_memory_space_constraint(wet, pltpu.HBM)
    grid = pltpu.with_memory_space_constraint(grid, pltpu.HBM)
    held = params
    for pair in range(LAYERS // 2):
        even, odd = 2 * pair, 2 * pair + 1
        opening = pair == 0
        if opening:
            ins_a = ins_b = [grid]
            loads_a = [(0, 0, 16, 0, None)]
            loads_b = [(0, 16, 32, 0, None)]
        else:
            ins_a = [keep, back_b, back_lat, back_diag]
            loads_a = [(0, 0, 12, 4, 1), (1, 0, 12, 4, 0), (2, 0, 4, 0, 1), (3, 0, 4, 0, 0)]
            ins_b = [keep, back_b, back_a]
            loads_b = [(0, 12, 28, 0, 1), (1, 12, 16, 0, 0), (2, 0, 12, 4, 0)]
        west_a, up_lat, up_diag, keep_a, *fetched = stage(
            even, 0, wet, held, ins_a, loads_a, [], [PART_A, SMALL, SMALL, STRIP],
            [(4, 16, 0, 0, 0), (0, 4, 1, 1, 0), (0, 4, 0, 2, 0), (4, 16, 1, 3, 0)],
            f"even{pair}a", opening,
        )
        if opening:
            *held, wet = fetched
        west_a = send(west_a, 0, -1)
        up_lat = send(up_lat, -1, 0)
        up_diag = send(up_diag, -1, -1)
        keep, west_b, *coming = stage(
            even, 2, wet, held, ins_b, loads_b, [keep_a], [PART_B],
            [(0, 16, 1, 0, 12), (0, 16, 0, 1, 0)],
            f"even{pair}b", brings=params,
        )
        west_b = send(west_b, 0, -1)
        held = coming
        west_a, up_lat, up_diag = relay(west_a, up_lat, up_diag)
        back_a, back_lat, back_diag, keep_a = stage(
            odd, 2, wet, held, [keep, west_b, up_lat, up_diag],
            [(0, 16, 28, 0, 0), (1, 4, 16, 0, 1), (2, 0, 4, 12, 0), (3, 0, 4, 12, 1)],
            [], [PART_A, SMALL, SMALL, STRIP],
            [(0, 12, 1, 0, 0), (12, 16, 0, 1, 0), (12, 16, 1, 2, 0), (0, 12, 0, 3, 16)],
            f"odd{pair}a",
        )
        back_a = send(back_a, 0, 1)
        back_lat = send(back_lat, 1, 0)
        back_diag = send(back_diag, 1, 1)
        keep, back_b, *coming = stage(
            odd, 0, wet, held, [keep, west_a, west_b],
            [(0, 0, 16, 0, 0), (1, 0, 12, 0, 1), (2, 0, 4, 12, 1)],
            [keep_a], [PART_B],
            [(0, 16, 0, 0, 0), (0, 16, 1, 1, 0)],
            f"odd{pair}b", brings=params if odd + 1 < LAYERS else [],
        )
        back_b = send(back_b, 0, 1)
        held = coming
        back_a, back_lat, back_diag = relay(back_a, back_lat, back_diag)
    out = pl.pallas_call(
        finish_kernel,
        out_shape=jax.ShapeDtypeStruct((32, 2, 8, C), f32),
        in_specs=[VM] * 5,
        out_specs=HBM,
        scratch_shapes=[pltpu.SemaphoreType.DMA((5,))],
        compiler_params=pltpu.CompilerParams(vmem_limit_bytes=4 << 20),
        name="finish",
    )(back_lat, back_diag, back_a, back_b, keep)
    return out.reshape(32, 16, C)


def solution(mesh):
    in_specs = (P("lat", "lon", None), P(), P(), P(), P(), P(), P(), P(), P())
    out_specs = P("lat", "lon", None)
    return jax.shard_map(local, mesh=mesh, in_specs=in_specs, out_specs=out_specs, check_vma=False)
```

```python
import functools

import jax
import jax.numpy as jnp
from jax import lax
from jax.experimental import pallas as pl
from jax.experimental.pallas import tpu as pltpu
from jax.sharding import PartitionSpec as P

C = 384
HEADS = 12
FFN = 1536
TOK = 128
LANES = 128
GROUP = 4
HEAD = 32
LAYERS = 4
CHUNK = 256
norm_eps = 1e-05
mask_fill = -1000000000.0
ERF_POLY = (
    0.7978830000512025,
    0.03633754443795962,
    -3.569087070491613e-05,
    -5.440885213149521e-05,
    3.8449560401057786e-06,
    -1.2507491956239078e-07,
    1.601666137598869e-09,
)
ERF_FLAT = 5.7 * 5.7
f32 = jnp.float32
bf16 = jnp.bfloat16
HBM = pl.BlockSpec(memory_space=pltpu.HBM)


def gelu(x):
    square = jnp.minimum(x * x, ERF_FLAT)
    poly = jnp.float32(ERF_POLY[-1])
    for factor in ERF_POLY[-2::-1]:
        poly = poly * square + factor
    half = 0.5 * x
    return half + half * jnp.tanh(x * poly)


def layer_norm(x, gain):
    center = jnp.mean(x, axis=-1, keepdims=True)
    away = x - center
    spread = jnp.mean(away * away, axis=-1, keepdims=True)
    return (away * lax.rsqrt(spread + norm_eps) * gain).astype(bf16)


def attend(q, k, v, bias_ref, group, masked):
    owner = lax.broadcasted_iota(jnp.int32, (TOK, LANES), 1) // HEAD
    zero = jnp.zeros((TOK, LANES), bf16)
    one = jnp.ones((TOK, LANES), bf16)
    keys = jnp.concatenate([jnp.where(owner == h, k, zero) for h in range(GROUP)], axis=0)
    scores = lax.dot_general(q, keys, (((1,), (1,)), ((), ())), preferred_element_type=f32)
    parts = []
    for h in range(GROUP):
        s = scores[:, h * TOK : (h + 1) * TOK] * HEAD ** (-0.5) + bias_ref[group * GROUP + h]
        if masked is not None:
            s = jnp.where(masked, mask_fill, s)
        parts.append(jnp.exp(s - jnp.max(s, axis=-1, keepdims=True)).astype(bf16))
    weights = jnp.concatenate(parts, axis=1)
    values = jnp.concatenate(
        [
            jnp.concatenate([jnp.where(owner == h, v, zero), jnp.where(owner == h, one, zero)], axis=1)
            for h in range(GROUP)
        ],
        axis=0,
    )
    both = jnp.dot(weights, values, preferred_element_type=f32)
    return (both[:, :LANES] / both[:, LANES:]).astype(bf16)


class Buffers:
    pass


def run_windows(b, ids, masked, ready):
    count = len(ids)
    rows = count * TOK
    x = jnp.concatenate([b.xs[pl.ds(i * 8, 8)].reshape(TOK, C) for i in ids], axis=0)
    ready("ga", "wq")
    b.qkv[:rows] = jnp.dot(layer_norm(x, b.ga[...]), b.wq[...], preferred_element_type=f32).astype(bf16)
    ready("bias")
    for w in range(count):
        span = slice(w * TOK, (w + 1) * TOK)
        hide = None
        if masked is not None:
            low_q = lax.broadcasted_iota(jnp.int32, (TOK, TOK), 0) >= TOK // 2
            low_k = lax.broadcasted_iota(jnp.int32, (TOK, TOK), 1) >= TOK // 2
            hide = jnp.logical_and(low_q != low_k, masked[w])
        for g in range(HEADS // GROUP):
            at = g * LANES
            b.att[span, at : at + LANES] = attend(
                b.qkv[span, at : at + LANES],
                b.qkv[span, C + at : C + at + LANES],
                b.qkv[span, 2 * C + at : 2 * C + at + LANES],
                b.bias,
                g,
                hide,
            )
    ready("wo", "gm")
    resid = x + jnp.dot(b.att[:rows], b.wo[...], preferred_element_type=f32)
    mlp_in = layer_norm(resid, b.gm[...])
    total = resid
    ready("wu", "wd")
    for f in range(0, FFN, CHUNK):
        up = jnp.dot(mlp_in, b.wu[:, f : f + CHUNK], preferred_element_type=f32)
        total = total + jnp.dot(gelu(up).astype(bf16), b.wd[f : f + CHUNK, :], preferred_element_type=f32)
    for w, i in enumerate(ids):
        b.xs[pl.ds(i * 8, 8)] = total[w * TOK : (w + 1) * TOK].reshape(8, 2, 8, C)


NAMES = ("ga", "wq", "bias", "wo", "gm", "wu", "wd")


def start_loads(params, held, layer, sem, names):
    copies = {}
    for n, name in enumerate(NAMES):
        if name not in names:
            continue
        source = params[n]
        part = source.at[pl.ds(layer, 1)] if len(source.shape) == 2 else source.at[layer]
        copies[name] = pltpu.make_async_copy(part, held[n], sem.at[n])
        copies[name].start()
    return copies


def held_shapes(params):
    return [jax.ShapeDtypeStruct((1, C) if p.ndim == 2 else p.shape[1:], p.dtype) for p in params]


VM = pl.BlockSpec(memory_space=pltpu.VMEM)


def overlaps(windows, base, segments):
    pieces = []
    for slot, window in enumerate(windows):
        top = base + 8 * window
        at = 0
        for half, low, high in segments:
            first, last = max(top, low), min(top + 8, high)
            if first < last:
                pieces.append((slot, first - top, at + first - low, last - first, half))
            at += high - low
    return pieces


def stage_kernel(layer, windows, work, sources, sinks, opening, brings, *refs):
    refs = list(refs)

    def take(count):
        got, refs[:count] = refs[:count], []
        return got

    (wet,) = take(1)
    given = take(7)
    ins = take(len(sources))
    coming = take(7) if brings else []
    outs = take(len(sinks))
    row = wet
    held = given
    if opening:
        held = take(7)
        row, rest = take(2)
    arrived = take(7) if brings else []
    xs, qkv, att, s_wet, sem, in_sem = refs
    lat = lax.axis_index("lat")
    lon = lax.axis_index("lon")
    bands = lax.axis_size("lat")
    base = 4 if layer % 2 == 1 else 0
    pending = {}
    waits = []
    if opening:
        flags = pltpu.make_async_copy(wet, s_wet, in_sem.at[0])
        block = pltpu.make_async_copy(ins[0].at[8:32], xs, in_sem.at[1])
        others = pltpu.make_async_copy(ins[0].at[0:8], rest, in_sem.at[2])
        flags.start()
        block.start()
        pending = start_loads(given, held, layer, sem, ("ga", "wq"))
        flags.wait()
        pending |= start_loads(given, held, layer, sem, ("bias", "wo", "gm", "wu", "wd"))
        others.start()
        waits.append(others)
        which_layer = lax.broadcasted_iota(jnp.int32, (8, LANES), 0)
        which_window = lax.broadcasted_iota(jnp.int32, (8, LANES), 1)
        mine = jnp.zeros((8, LANES), jnp.int32)
        for n in range(LAYERS):
            for j in range(4):
                here = jnp.logical_and(which_layer == n, which_window == j)
                mine = jnp.where(here, s_wet[n, lon, lat * 4 + j], mine)
        row[...] = mine
        is_wet = [s_wet[layer, lon, lat * 4 + windows[slot]] == 1 for slot in work]
        block.wait()
    else:
        waits = list(start_loads(coming, arrived, layer + 1, sem, NAMES).values()) if brings else []
        for source, segments in zip(ins, sources):
            for slot, to, at, count, half in overlaps(windows, base, segments):
                if half is None:
                    xs[slot * 8 + to : slot * 8 + to + count] = source[at : at + count]
                else:
                    xs[slot * 8 + to : slot * 8 + to + count, half] = source[at : at + count]
        is_wet = [row[layer, windows[slot]] == 1 for slot in work]

    def ready(*names):
        for name in names:
            if name in pending:
                pending[name].wait()

    b = Buffers()
    b.xs, b.qkv, b.att = xs, qkv, att
    b.ga, b.wq, b.bias, b.wo, b.gm, b.wu, b.wd = held
    first_slot = jnp.int32(work[-1])
    last_slot = jnp.int32(work[0])
    count = jnp.int32(0)
    for slot, flag in reversed(list(zip(work, is_wet))):
        first_slot = jnp.where(flag, slot, first_slot)
    for slot, flag in zip(work, is_wet):
        last_slot = jnp.where(flag, slot, last_slot)
        count += flag.astype(jnp.int32)
    masking = base == 4 and 3 in [windows[slot] for slot in work]

    def run(ids):
        masked = None
        if masking:
            masked = [jnp.logical_and(lat == bands - 1, i == windows.index(3)) for i in ids]
        run_windows(b, ids, masked, ready)

    if len(work) > 1:

        @pl.when(count >= 2)
        def _():
            run([first_slot, last_slot if len(work) == 2 else jnp.where(count == 3, work[1], last_slot)])
            if opening:
                pending_before = dict(pending)
                pending.clear()
                single = count == 3

                @pl.when(single)
                def _():
                    run([jnp.int32(work[2])])

                pending.update(pending_before)

    @pl.when(count == 1)
    def _():
        run([first_slot])

    if opening:

        @pl.when(count == 0)
        def _():
            ready(*NAMES)

    for target, segments in zip(outs, sinks):
        for slot, at, to, rows, half in overlaps(windows, base, segments):
            target[to : to + rows] = xs[slot * 8 + at : slot * 8 + at + rows, half]
    for c in waits:
        c.wait()


def stage(layer, windows, work, wet, held, sources, sinks, name, opening=False, brings=()):
    ins = [array for array, _ in sources]
    shapes = [jax.ShapeDtypeStruct((sum(h - l for _, l, h in segments), 8, C), f32) for segments in sinks]
    kernel = functools.partial(
        stage_kernel, layer, windows, work, [segments for _, segments in sources], sinks, opening, bool(brings)
    )
    extra = []
    if opening:
        extra = held_shapes(held)
        extra += [jax.ShapeDtypeStruct((8, LANES), jnp.int32), jax.ShapeDtypeStruct((8, 2, 8, C), f32)]
    extra += held_shapes(brings)
    place = HBM if opening else VM
    rows = min(2, len(work)) * TOK
    return pl.pallas_call(
        kernel,
        out_shape=shapes + extra,
        in_specs=[place] * (8 + len(ins)) + [HBM] * len(brings),
        out_specs=[VM] * len(shapes + extra),
        scratch_shapes=[
            pltpu.VMEM((8 * len(windows), 2, 8, C), f32),
            pltpu.VMEM((rows, 3 * C), bf16),
            pltpu.VMEM((rows, C), bf16),
            pltpu.SMEM((LAYERS, 16, 32), jnp.int32),
            pltpu.SemaphoreType.DMA((7,)),
            pltpu.SemaphoreType.DMA((3,)),
        ],
        compiler_params=pltpu.CompilerParams(vmem_limit_bytes=24 << 20),
        cost_estimate=pl.CostEstimate(flops=4_000_000_000, bytes_accessed=6_000_000, transcendentals=800_000),
        name=name,
    )(wet, *held, *ins, *brings)


def send(block, d_lat, d_lon):
    n_lat, n_lon = lax.axis_size("lat"), lax.axis_size("lon")
    route = [
        (a * n_lon + b, (a + d_lat) % n_lat * n_lon + (b + d_lon) % n_lon)
        for a in range(n_lat)
        for b in range(n_lon)
    ]
    return lax.ppermute(block, ("lat", "lon"), route)


def finish_kernel(placed, *refs):
    ins, out, sem = refs[: len(placed)], refs[len(placed)], refs[len(placed) + 1]
    copies = []
    for source, segments in zip(ins, placed):
        at = 0
        for half, low, high in segments:
            part = source.at[at : at + high - low]
            copies.append(pltpu.make_async_copy(part, out.at[low:high, half], sem.at[len(copies)]))
            copies[-1].start()
            at += high - low
    for c in copies:
        c.wait()


def local(tokens, wet_flags, ln_attn, w_qkv, w_out, pos_bias, ln_mlp, w_up, w_down):
    params = [ln_attn, w_qkv, pos_bias, w_out, ln_mlp, w_up, w_down]
    wet = wet_flags.transpose(0, 2, 1)
    grid = tokens.reshape(32, 2, 8, C)
    params = [pltpu.with_memory_space_constraint(p, pltpu.HBM) for p in params]
    wet = pltpu.with_memory_space_constraint(wet, pltpu.HBM)
    grid = pltpu.with_memory_space_constraint(grid, pltpu.HBM)
    for pair in range(LAYERS // 2):
        even, odd = 2 * pair, 2 * pair + 1
        most = [[(0, 8, 32)], [(1, 8, 32)]]
        if pair == 0:
            west_a, keep_a, *rest = stage(
                even, [1, 2, 3], [0, 1, 2], wet, params, [(grid, [])], most, "even0a", opening=True
            )
            held, wet, last = rest[:7], rest[7], [(rest[8], [(None, 0, 8)])]
        else:
            inner = stage(
                even, [2], [0], wet, held, [(back_a, [(0, 12, 28)]), (keep_e, [(1, 12, 28)])],
                [[(0, 16, 24)], [(1, 16, 24)]], f"even{pair}e",
            )
            sides = [(0, 4, 12), (0, 28, 32)]
            west_a, keep_a, *coming = stage(
                even, [1, 2, 3], [0, 2], wet, held,
                [
                    (back_b, sides),
                    (keep_l, [(1, 4, 12), (1, 28, 32)]),
                    (back_a, [(0, 12, 16), (0, 0, 8), (0, 24, 28)]),
                    (keep_e, [(1, 12, 16), (1, 0, 8), (1, 24, 28)]),
                    (inner[0], [(0, 16, 24)]),
                    (inner[1], [(1, 16, 24)]),
                ],
                most, f"even{pair}a", brings=params,
            )
            last = [(back_b, sides), (keep_l, [(1, 4, 12)]), (back_diag, [(0, 0, 4)]), (back_lat, [(1, 0, 4)])]
        west_a = send(west_a, 0, -1)
        west_b, up_lat, up_diag, keep_b, *more = stage(
            even, [0], [0], wet, held, last, [[(0, 4, 8)], [(1, 0, 4)], [(0, 0, 4)], [(1, 4, 8)]],
            f"even{pair}b", brings=params if pair == 0 else (),
        )
        west_b = send(west_b, 0, -1)
        up_lat = send(up_lat, -1, 0)
        up_diag = send(up_diag, -1, -1)
        held = more if pair == 0 else coming
        own, other = (keep_a, [(0, 8, 32)]), (west_a, [(1, 8, 32)])
        keep_e, back_a = stage(
            odd, [1, 2], [0, 1], wet, held, [own, other], [[(0, 12, 28)], [(1, 12, 28)]], f"odd{pair}a"
        )
        back_a = send(back_a, 0, 1)
        keep_l, back_b, back_lat, back_diag, *coming = stage(
            odd, [0, 3], [0, 1], wet, held,
            [own, other, (keep_b, [(0, 4, 8)]), (west_b, [(1, 4, 8)]), (up_lat, [(0, 32, 36)]), (up_diag, [(1, 32, 36)])],
            [[(0, 4, 12), (0, 28, 32)], [(1, 4, 12), (1, 28, 32)], [(0, 32, 36)], [(1, 32, 36)]],
            f"odd{pair}b", brings=params if odd + 1 < LAYERS else (),
        )
        back_b = send(back_b, 0, 1)
        back_lat = send(back_lat, 1, 0)
        back_diag = send(back_diag, 1, 1)
        held = coming
    parts = [
        (back_a, [(0, 12, 28)]),
        (back_b, [(0, 4, 12), (0, 28, 32)]),
        (back_diag, [(0, 0, 4)]),
        (back_lat, [(1, 0, 4)]),
        (keep_l, [(1, 4, 12), (1, 28, 32)]),
        (keep_e, [(1, 12, 28)]),
    ]
    out = pl.pallas_call(
        functools.partial(finish_kernel, [segments for _, segments in parts]),
        out_shape=jax.ShapeDtypeStruct((32, 2, 8, C), f32),
        in_specs=[VM] * len(parts),
        out_specs=HBM,
        scratch_shapes=[pltpu.SemaphoreType.DMA((8,))],
        compiler_params=pltpu.CompilerParams(vmem_limit_bytes=4 << 20),
        name="finish",
    )(*[array for array, _ in parts])
    return out.reshape(32, 16, C)


def solution(mesh):
    in_specs = (P("lat", "lon", None), P(), P(), P(), P(), P(), P(), P(), P())
    out_specs = P("lat", "lon", None)
    return jax.shard_map(local, mesh=mesh, in_specs=in_specs, out_specs=out_specs, check_vma=False)
```

```python
import functools

import jax
import jax.numpy as jnp
from jax import lax
from jax.experimental import pallas as pl
from jax.experimental.pallas import tpu as pltpu
from jax.sharding import PartitionSpec as P

C = 384
HEADS = 12
FFN = 1536
TOK = 128
LANES = 128
GROUP = 4
HEAD = 32
LAYERS = 4
CHUNK = 256
norm_eps = 1e-05
mask_fill = -1000000000.0
ERF_POLY = (
    0.7978830000512025,
    0.03633754443795962,
    -3.569087070491613e-05,
    -5.440885213149521e-05,
    3.8449560401057786e-06,
    -1.2507491956239078e-07,
    1.601666137598869e-09,
)
ERF_FLAT = 5.7 * 5.7
f32 = jnp.float32
bf16 = jnp.bfloat16
HBM = pl.BlockSpec(memory_space=pltpu.HBM)


def gelu(x):
    square = jnp.minimum(x * x, ERF_FLAT)
    poly = jnp.float32(ERF_POLY[-1])
    for factor in ERF_POLY[-2::-1]:
        poly = poly * square + factor
    half = 0.5 * x
    return half + half * jnp.tanh(x * poly)


def layer_norm(x, gain):
    center = jnp.mean(x, axis=-1, keepdims=True)
    away = x - center
    spread = jnp.mean(away * away, axis=-1, keepdims=True)
    return (away * lax.rsqrt(spread + norm_eps) * gain).astype(bf16)


def attend(q, k, v, bias_ref, group, masked):
    owner = lax.broadcasted_iota(jnp.int32, (TOK, LANES), 1) // HEAD
    zero = jnp.zeros((TOK, LANES), bf16)
    one = jnp.ones((TOK, LANES), bf16)
    keys = jnp.concatenate([jnp.where(owner == h, k, zero) for h in range(GROUP)], axis=0)
    scores = lax.dot_general(q, keys, (((1,), (1,)), ((), ())), preferred_element_type=f32)
    parts = []
    for h in range(GROUP):
        s = scores[:, h * TOK : (h + 1) * TOK] * HEAD ** (-0.5) + bias_ref[group * GROUP + h]
        if masked is not None:
            s = jnp.where(masked, mask_fill, s)
        parts.append(jnp.exp(s - jnp.max(s, axis=-1, keepdims=True)).astype(bf16))
    weights = jnp.concatenate(parts, axis=1)
    values = jnp.concatenate(
        [
            jnp.concatenate([jnp.where(owner == h, v, zero), jnp.where(owner == h, one, zero)], axis=1)
            for h in range(GROUP)
        ],
        axis=0,
    )
    both = jnp.dot(weights, values, preferred_element_type=f32)
    return (both[:, :LANES] / both[:, LANES:]).astype(bf16)


class Buffers:
    pass


def run_windows(b, ids, masked, ready):
    count = len(ids)
    rows = count * TOK
    x = jnp.concatenate([b.xs[pl.ds(i * 8, 8)].reshape(TOK, C) for i in ids], axis=0)
    ready("ga", "wq")
    b.qkv[:rows] = jnp.dot(layer_norm(x, b.ga[...]), b.wq[...], preferred_element_type=f32).astype(bf16)
    ready("bias")
    for w in range(count):
        span = slice(w * TOK, (w + 1) * TOK)
        hide = None
        if masked is not None:
            low_q = lax.broadcasted_iota(jnp.int32, (TOK, TOK), 0) >= TOK // 2
            low_k = lax.broadcasted_iota(jnp.int32, (TOK, TOK), 1) >= TOK // 2
            hide = jnp.logical_and(low_q != low_k, masked[w])
        for g in range(HEADS // GROUP):
            at = g * LANES
            b.att[span, at : at + LANES] = attend(
                b.qkv[span, at : at + LANES],
                b.qkv[span, C + at : C + at + LANES],
                b.qkv[span, 2 * C + at : 2 * C + at + LANES],
                b.bias,
                g,
                hide,
            )
    ready("wo", "gm")
    resid = x + jnp.dot(b.att[:rows], b.wo[...], preferred_element_type=f32)
    mlp_in = layer_norm(resid, b.gm[...])
    total = resid
    ready("wu", "wd")
    for f in range(0, FFN, CHUNK):
        up = jnp.dot(mlp_in, b.wu[:, f : f + CHUNK], preferred_element_type=f32)
        total = total + jnp.dot(gelu(up).astype(bf16), b.wd[f : f + CHUNK, :], preferred_element_type=f32)
    for w, i in enumerate(ids):
        b.xs[pl.ds(i * 8, 8)] = total[w * TOK : (w + 1) * TOK].reshape(8, 2, 8, C)


NAMES = ("ga", "wq", "bias", "wo", "gm", "wu", "wd")


def start_loads(params, held, layer, sem, names):
    copies = {}
    for n, name in enumerate(NAMES):
        if name not in names:
            continue
        source = params[n]
        part = source.at[pl.ds(layer, 1)] if len(source.shape) == 2 else source.at[layer]
        copies[name] = pltpu.make_async_copy(part, held[n], sem.at[n])
        copies[name].start()
    return copies


def held_shapes(params):
    return [jax.ShapeDtypeStruct((1, C) if p.ndim == 2 else p.shape[1:], p.dtype) for p in params]


VM = pl.BlockSpec(memory_space=pltpu.VMEM)


def overlaps(windows, base, segments):
    pieces = []
    for slot, window in enumerate(windows):
        top = base + 8 * window
        at = 0
        for half, low, high in segments:
            first, last = max(top, low), min(top + 8, high)
            if first < last:
                pieces.append((slot, first - top, at + first - low, last - first, half))
            at += high - low
    return pieces


def stage_kernel(layer, windows, work, sources, sinks, opening, brings, *refs):
    refs = list(refs)

    def take(count):
        got, refs[:count] = refs[:count], []
        return got

    (wet,) = take(1)
    given = take(7)
    ins = take(len(sources))
    coming = take(7) if brings else []
    outs = take(len(sinks))
    row = wet
    held = given
    if opening:
        held = take(7)
        row, rest = take(2)
    arrived = take(7) if brings else []
    xs, qkv, att, s_wet, sem, in_sem = refs
    lat = lax.axis_index("lat")
    lon = lax.axis_index("lon")
    bands = lax.axis_size("lat")
    base = 4 if layer % 2 == 1 else 0
    pending = {}
    waits = []
    if opening:
        flags = pltpu.make_async_copy(wet, s_wet, in_sem.at[0])
        block = pltpu.make_async_copy(ins[0].at[8:32], xs, in_sem.at[1])
        others = pltpu.make_async_copy(ins[0].at[0:8], rest, in_sem.at[2])
        flags.start()
        block.start()
        pending = start_loads(given, held, layer, sem, ("ga", "wq"))
        flags.wait()
        pending |= start_loads(given, held, layer, sem, ("bias", "wo", "gm", "wu", "wd"))
        others.start()
        waits.append(others)
        which_layer = lax.broadcasted_iota(jnp.int32, (8, LANES), 0)
        which_window = lax.broadcasted_iota(jnp.int32, (8, LANES), 1)
        mine = jnp.zeros((8, LANES), jnp.int32)
        for n in range(LAYERS):
            for j in range(4):
                here = jnp.logical_and(which_layer == n, which_window == j)
                mine = jnp.where(here, s_wet[n, lon, lat * 4 + j], mine)
        row[...] = mine
        is_wet = [s_wet[layer, lon, lat * 4 + windows[slot]] == 1 for slot in work]
        block.wait()
    else:
        waits = list(start_loads(coming, arrived, layer + 1, sem, NAMES).values()) if brings else []
        for source, segments in zip(ins, sources):
            for slot, to, at, count, half in overlaps(windows, base, segments):
                if half is None:
                    xs[slot * 8 + to : slot * 8 + to + count] = source[at : at + count]
                else:
                    xs[slot * 8 + to : slot * 8 + to + count, half] = source[at : at + count]
        is_wet = [row[layer, windows[slot]] == 1 for slot in work]

    def ready(*names):
        for name in names:
            if name in pending:
                pending[name].wait()

    b = Buffers()
    b.xs, b.qkv, b.att = xs, qkv, att
    b.ga, b.wq, b.bias, b.wo, b.gm, b.wu, b.wd = held
    first_slot = jnp.int32(work[-1])
    last_slot = jnp.int32(work[0])
    count = jnp.int32(0)
    for slot, flag in reversed(list(zip(work, is_wet))):
        first_slot = jnp.where(flag, slot, first_slot)
    for slot, flag in zip(work, is_wet):
        last_slot = jnp.where(flag, slot, last_slot)
        count += flag.astype(jnp.int32)
    masking = base == 4 and 3 in [windows[slot] for slot in work]

    def run(ids):
        masked = None
        if masking:
            masked = [jnp.logical_and(lat == bands - 1, i == windows.index(3)) for i in ids]
        run_windows(b, ids, masked, ready)

    if len(work) > 1:

        @pl.when(count >= 2)
        def _():
            run([first_slot, last_slot if len(work) == 2 else jnp.where(count == 3, work[1], last_slot)])
            if opening:
                pending_before = dict(pending)
                pending.clear()
                single = count == 3

                @pl.when(single)
                def _():
                    run([jnp.int32(work[2])])

                pending.update(pending_before)

    @pl.when(count == 1)
    def _():
        run([first_slot])

    if opening:

        @pl.when(count == 0)
        def _():
            ready(*NAMES)

    for target, segments in zip(outs, sinks):
        for slot, at, to, rows, half in overlaps(windows, base, segments):
            target[to : to + rows] = xs[slot * 8 + at : slot * 8 + at + rows, half]
    for c in waits:
        c.wait()


def stage(layer, windows, work, wet, held, sources, sinks, name, opening=False, brings=()):
    ins = [array for array, _ in sources]
    shapes = [jax.ShapeDtypeStruct((sum(h - l for _, l, h in segments), 8, C), f32) for segments in sinks]
    kernel = functools.partial(
        stage_kernel, layer, windows, work, [segments for _, segments in sources], sinks, opening, bool(brings)
    )
    extra = []
    if opening:
        extra = held_shapes(held)
        extra += [jax.ShapeDtypeStruct((8, LANES), jnp.int32), jax.ShapeDtypeStruct((8, 2, 8, C), f32)]
    extra += held_shapes(brings)
    place = HBM if opening else VM
    rows = min(2, len(work)) * TOK
    return pl.pallas_call(
        kernel,
        out_shape=shapes + extra,
        in_specs=[place] * (8 + len(ins)) + [HBM] * len(brings),
        out_specs=[VM] * len(shapes + extra),
        scratch_shapes=[
            pltpu.VMEM((8 * len(windows), 2, 8, C), f32),
            pltpu.VMEM((rows, 3 * C), bf16),
            pltpu.VMEM((rows, C), bf16),
            pltpu.SMEM((LAYERS, 16, 32), jnp.int32),
            pltpu.SemaphoreType.DMA((7,)),
            pltpu.SemaphoreType.DMA((3,)),
        ],
        compiler_params=pltpu.CompilerParams(vmem_limit_bytes=24 << 20),
        cost_estimate=pl.CostEstimate(flops=4_000_000_000, bytes_accessed=6_000_000, transcendentals=800_000),
        name=name,
    )(wet, *held, *ins, *brings)


def send(block, d_lat, d_lon):
    n_lat, n_lon = lax.axis_size("lat"), lax.axis_size("lon")
    route = [
        (a * n_lon + b, (a + d_lat) % n_lat * n_lon + (b + d_lon) % n_lon)
        for a in range(n_lat)
        for b in range(n_lon)
    ]
    return lax.ppermute(block, ("lat", "lon"), route)


def relay_kernel(*refs):
    del refs


def relay(*arrays):
    return pl.pallas_call(
        relay_kernel,
        out_shape=[jax.ShapeDtypeStruct(a.shape, a.dtype) for a in arrays],
        in_specs=[VM] * len(arrays),
        out_specs=[VM] * len(arrays),
        input_output_aliases={i: i for i in range(len(arrays))},
        compiler_params=pltpu.CompilerParams(vmem_limit_bytes=4 << 20),
        cost_estimate=pl.CostEstimate(flops=8_000_000_000, bytes_accessed=6_000_000, transcendentals=0),
        name="relay",
    )(*arrays)


def finish_kernel(placed, *refs):
    ins, out, sem = refs[: len(placed)], refs[len(placed)], refs[len(placed) + 1]
    copies = []
    for source, segments in zip(ins, placed):
        at = 0
        for half, low, high in segments:
            part = source.at[at : at + high - low]
            copies.append(pltpu.make_async_copy(part, out.at[low:high, half], sem.at[len(copies)]))
            copies[-1].start()
            at += high - low
    for c in copies:
        c.wait()


def local(tokens, wet_flags, ln_attn, w_qkv, w_out, pos_bias, ln_mlp, w_up, w_down):
    params = [ln_attn, w_qkv, pos_bias, w_out, ln_mlp, w_up, w_down]
    wet = wet_flags.transpose(0, 2, 1)
    grid = tokens.reshape(32, 2, 8, C)
    params = [pltpu.with_memory_space_constraint(p, pltpu.HBM) for p in params]
    wet = pltpu.with_memory_space_constraint(wet, pltpu.HBM)
    grid = pltpu.with_memory_space_constraint(grid, pltpu.HBM)
    for pair in range(LAYERS // 2):
        even, odd = 2 * pair, 2 * pair + 1
        most = [[(0, 8, 32)], [(1, 8, 32)]]
        if pair == 0:
            west_a, keep_a, *rest = stage(
                even, [1, 2, 3], [0, 1, 2], wet, params, [(grid, [])], most, "even0a", opening=True
            )
            held, wet, last = rest[:7], rest[7], [(rest[8], [(None, 0, 8)])]
        else:
            inner = stage(
                even, [2], [0], wet, held, [(back_a, [(0, 12, 28)]), (keep_e, [(1, 12, 28)])],
                [[(0, 16, 24)], [(1, 16, 24)]], f"even{pair}e",
            )
            sides = [(0, 4, 12), (0, 28, 32)]
            west_a, keep_a, *coming = stage(
                even, [1, 2, 3], [0, 2], wet, held,
                [
                    (back_b, sides),
                    (keep_l, [(1, 4, 12), (1, 28, 32)]),
                    (back_a, [(0, 12, 16), (0, 0, 8), (0, 24, 28)]),
                    (keep_e, [(1, 12, 16), (1, 0, 8), (1, 24, 28)]),
                    (inner[0], [(0, 16, 24)]),
                    (inner[1], [(1, 16, 24)]),
                ],
                most, f"even{pair}a", brings=params,
            )
            last = [(back_b, sides), (keep_l, [(1, 4, 12)]), (back_diag, [(0, 0, 4)]), (back_lat, [(1, 0, 4)])]
        west_a = send(west_a, 0, -1)
        west_b, up_lat, up_diag, keep_b, *more = stage(
            even, [0], [0], wet, held, last, [[(0, 4, 8)], [(1, 0, 4)], [(0, 0, 4)], [(1, 4, 8)]],
            f"even{pair}b", brings=params if pair == 0 else (),
        )
        west_b = send(west_b, 0, -1)
        up_lat = send(up_lat, -1, 0)
        up_diag = send(up_diag, -1, -1)
        held = more if pair == 0 else coming
        own, other = (keep_a, [(0, 8, 32)]), (west_a, [(1, 8, 32)])
        keep_e, back_a = stage(
            odd, [1, 2], [0, 1], wet, held, [own, other], [[(0, 12, 28)], [(1, 12, 28)]], f"odd{pair}a"
        )
        back_a = send(back_a, 0, 1)
        sources = [
            own, other, (keep_b, [(0, 4, 8)]), (west_b, [(1, 4, 8)]), (up_lat, [(0, 32, 36)]), (up_diag, [(1, 32, 36)])
        ]
        outer = [[(0, 4, 12), (0, 28, 32)], [(1, 4, 12), (1, 28, 32)]]
        around = [[(0, 32, 36)], [(1, 32, 36)]]
        if odd + 1 < LAYERS:
            keep_l, back_b, back_lat, back_diag, *held = stage(
                odd, [0, 3], [0, 1], wet, held, sources, outer + around, f"odd{pair}b", brings=params
            )
        else:
            back_lat, back_diag, *edge = stage(
                odd, [3], [0], wet, held, [own, other, *sources[4:]],
                [*around, [(0, 28, 32)], [(1, 28, 32)]], f"odd{pair}b",
            )
            keep_l, back_b = stage(
                odd, [0, 3], [0], wet, held,
                [(keep_a, [(0, 8, 28)]), (west_a, [(1, 8, 28)]), *sources[2:4], (edge[0], [(0, 28, 32)]), (edge[1], [(1, 28, 32)])], outer, f"odd{pair}c",
            )
        back_b = send(back_b, 0, 1)
        back_lat = send(back_lat, 1, 0)
        back_diag = send(back_diag, 1, 1)
    back_lat, back_diag = relay(back_lat, back_diag)
    parts = [
        (back_a, [(0, 12, 28)]),
        (back_b, [(0, 4, 12), (0, 28, 32)]),
        (back_diag, [(0, 0, 4)]),
        (back_lat, [(1, 0, 4)]),
        (keep_l, [(1, 4, 12), (1, 28, 32)]),
        (keep_e, [(1, 12, 28)]),
    ]
    out = pl.pallas_call(
        functools.partial(finish_kernel, [segments for _, segments in parts]),
        out_shape=jax.ShapeDtypeStruct((32, 2, 8, C), f32),
        in_specs=[VM] * len(parts),
        out_specs=HBM,
        scratch_shapes=[pltpu.SemaphoreType.DMA((8,))],
        compiler_params=pltpu.CompilerParams(vmem_limit_bytes=4 << 20),
        name="finish",
    )(*[array for array, _ in parts])
    return out.reshape(32, 16, C)


def solution(mesh):
    in_specs = (P("lat", "lon", None), P(), P(), P(), P(), P(), P(), P(), P())
    out_specs = P("lat", "lon", None)
    return jax.shard_map(local, mesh=mesh, in_specs=in_specs, out_specs=out_specs, check_vma=False)
```

```python
import functools

import jax
import jax.numpy as jnp
from jax import lax
from jax.experimental import pallas as pl
from jax.experimental.pallas import tpu as pltpu
from jax.sharding import PartitionSpec as P

C = 384
HEADS = 12
FFN = 1536
TOK = 128
LANES = 128
GROUP = 4
HEAD = 32
LAYERS = 4
CHUNK = 256
norm_eps = 1e-05
mask_fill = -1000000000.0
ERF_POLY = (
    0.7978275160691982,
    0.03647005390043865,
    -0.00012554234498973965,
    -3.0455015643046705e-05,
    1.1119467340375738e-06,
)
f32 = jnp.float32
bf16 = jnp.bfloat16
HBM = pl.BlockSpec(memory_space=pltpu.HBM)


def gelu(x):
    rounded = x.astype(bf16)
    square = rounded * rounded
    poly = bf16(ERF_POLY[-1])
    for factor in ERF_POLY[-2::-1]:
        poly = poly * square + bf16(factor)
    half = 0.5 * x
    return half + half * jnp.tanh((rounded * poly).astype(f32))


def layer_norm(x, gain):
    center = jnp.mean(x, axis=-1, keepdims=True)
    away = x - center
    spread = jnp.mean(away * away, axis=-1, keepdims=True)
    return (away * lax.rsqrt(spread + norm_eps) * gain).astype(bf16)


def attend(q, k, v, bias_ref, group, masked):
    owner = lax.broadcasted_iota(jnp.int32, (TOK, LANES), 1) // HEAD
    zero = jnp.zeros((TOK, LANES), bf16)
    one = jnp.ones((TOK, LANES), bf16)
    keys = jnp.concatenate([jnp.where(owner == h, k, zero) for h in range(GROUP)], axis=0)
    scores = lax.dot_general(q, keys, (((1,), (1,)), ((), ())), preferred_element_type=f32)
    parts = []
    for h in range(GROUP):
        s = scores[:, h * TOK : (h + 1) * TOK] * HEAD ** (-0.5) + bias_ref[group * GROUP + h]
        if masked is not None:
            s = jnp.where(masked, mask_fill, s)
        parts.append(jnp.exp(s - jnp.max(s, axis=-1, keepdims=True)).astype(bf16))
    weights = jnp.concatenate(parts, axis=1)
    values = jnp.concatenate(
        [
            jnp.concatenate([jnp.where(owner == h, v, zero), jnp.where(owner == h, one, zero)], axis=1)
            for h in range(GROUP)
        ],
        axis=0,
    )
    both = jnp.dot(weights, values, preferred_element_type=f32)
    return (both[:, :LANES] / both[:, LANES:]).astype(bf16)


class Buffers:
    pass


def run_windows(b, ids, masked, ready):
    count = len(ids)
    rows = count * TOK
    x = jnp.concatenate([b.xs[pl.ds(i * 8, 8)].reshape(TOK, C) for i in ids], axis=0)
    ready("ga", "wq")
    b.qkv[:rows] = jnp.dot(layer_norm(x, b.ga[...]), b.wq[...], preferred_element_type=f32).astype(bf16)
    ready("bias")
    for w in range(count):
        span = slice(w * TOK, (w + 1) * TOK)
        hide = None
        if masked is not None:
            low_q = lax.broadcasted_iota(jnp.int32, (TOK, TOK), 0) >= TOK // 2
            low_k = lax.broadcasted_iota(jnp.int32, (TOK, TOK), 1) >= TOK // 2
            hide = jnp.logical_and(low_q != low_k, masked[w])
        for g in range(HEADS // GROUP):
            at = g * LANES
            b.att[span, at : at + LANES] = attend(
                b.qkv[span, at : at + LANES],
                b.qkv[span, C + at : C + at + LANES],
                b.qkv[span, 2 * C + at : 2 * C + at + LANES],
                b.bias,
                g,
                hide,
            )
    ready("wo", "gm")
    resid = x + jnp.dot(b.att[:rows], b.wo[...], preferred_element_type=f32)
    mlp_in = layer_norm(resid, b.gm[...])
    total = resid
    ready("wu", "wd")
    for f in range(0, FFN, CHUNK):
        up = jnp.dot(mlp_in, b.wu[:, f : f + CHUNK], preferred_element_type=f32)
        total = total + jnp.dot(gelu(up).astype(bf16), b.wd[f : f + CHUNK, :], preferred_element_type=f32)
    for w, i in enumerate(ids):
        b.xs[pl.ds(i * 8, 8)] = total[w * TOK : (w + 1) * TOK].reshape(8, 2, 8, C)


NAMES = ("ga", "wq", "bias", "wo", "gm", "wu", "wd")


def start_loads(params, held, layer, sem, names):
    copies = {}
    for n, name in enumerate(NAMES):
        if name not in names:
            continue
        source = params[n]
        part = source.at[pl.ds(layer, 1)] if len(source.shape) == 2 else source.at[layer]
        copies[name] = pltpu.make_async_copy(part, held[n], sem.at[n])
        copies[name].start()
    return copies


def held_shapes(params):
    return [jax.ShapeDtypeStruct((1, C) if p.ndim == 2 else p.shape[1:], p.dtype) for p in params]


VM = pl.BlockSpec(memory_space=pltpu.VMEM)


def overlaps(windows, base, segments):
    pieces = []
    for slot, window in enumerate(windows):
        top = base + 8 * window
        at = 0
        for half, low, high in segments:
            first, last = max(top, low), min(top + 8, high)
            if first < last:
                pieces.append((slot, first - top, at + first - low, last - first, half))
            at += high - low
    return pieces


def stage_kernel(layer, windows, work, sources, sinks, opening, brings, *refs):
    refs = list(refs)

    def take(count):
        got, refs[:count] = refs[:count], []
        return got

    (wet,) = take(1)
    given = take(7)
    ins = take(len(sources))
    coming = take(7) if brings else []
    outs = take(len(sinks))
    row = wet
    held = given
    if opening:
        held = take(7)
        row, rest = take(2)
    arrived = take(7) if brings else []
    xs, qkv, att, s_wet, sem, in_sem = refs
    lat = lax.axis_index("lat")
    lon = lax.axis_index("lon")
    bands = lax.axis_size("lat")
    base = 4 if layer % 2 == 1 else 0
    pending = {}
    waits = []
    if opening:
        flags = pltpu.make_async_copy(wet, s_wet, in_sem.at[0])
        block = pltpu.make_async_copy(ins[0].at[8:32], xs, in_sem.at[1])
        others = pltpu.make_async_copy(ins[0].at[0:8], rest, in_sem.at[2])
        flags.start()
        block.start()
        pending = start_loads(given, held, layer, sem, ("ga", "wq"))
        flags.wait()
        pending |= start_loads(given, held, layer, sem, ("bias", "wo", "gm", "wu", "wd"))
        others.start()
        waits.append(others)
        which_layer = lax.broadcasted_iota(jnp.int32, (8, LANES), 0)
        which_window = lax.broadcasted_iota(jnp.int32, (8, LANES), 1)
        mine = jnp.zeros((8, LANES), jnp.int32)
        for n in range(LAYERS):
            for j in range(4):
                here = jnp.logical_and(which_layer == n, which_window == j)
                mine = jnp.where(here, s_wet[n, lon, lat * 4 + j], mine)
        row[...] = mine
        is_wet = [s_wet[layer, lon, lat * 4 + windows[slot]] == 1 for slot in work]
        block.wait()
    else:
        waits = list(start_loads(coming, arrived, layer + 1, sem, NAMES).values()) if brings else []
        for source, segments in zip(ins, sources):
            for slot, to, at, count, half in overlaps(windows, base, segments):
                if half is None:
                    xs[slot * 8 + to : slot * 8 + to + count] = source[at : at + count]
                else:
                    xs[slot * 8 + to : slot * 8 + to + count, half] = source[at : at + count]
        is_wet = [row[layer, windows[slot]] == 1 for slot in work]

    def ready(*names):
        for name in names:
            if name in pending:
                pending[name].wait()

    b = Buffers()
    b.xs, b.qkv, b.att = xs, qkv, att
    b.ga, b.wq, b.bias, b.wo, b.gm, b.wu, b.wd = held
    first_slot = jnp.int32(work[-1])
    last_slot = jnp.int32(work[0])
    count = jnp.int32(0)
    for slot, flag in reversed(list(zip(work, is_wet))):
        first_slot = jnp.where(flag, slot, first_slot)
    for slot, flag in zip(work, is_wet):
        last_slot = jnp.where(flag, slot, last_slot)
        count += flag.astype(jnp.int32)
    masking = base == 4 and 3 in [windows[slot] for slot in work]

    def run(ids):
        masked = None
        if masking:
            masked = [jnp.logical_and(lat == bands - 1, i == windows.index(3)) for i in ids]
        run_windows(b, ids, masked, ready)

    if len(work) > 1:

        @pl.when(count >= 2)
        def _():
            run([first_slot, last_slot if len(work) == 2 else jnp.where(count == 3, work[1], last_slot)])
            if opening:
                pending_before = dict(pending)
                pending.clear()
                single = count == 3

                @pl.when(single)
                def _():
                    run([jnp.int32(work[2])])

                pending.update(pending_before)

    @pl.when(count == 1)
    def _():
        run([first_slot])

    if opening:

        @pl.when(count == 0)
        def _():
            ready(*NAMES)

    for target, segments in zip(outs, sinks):
        for slot, at, to, rows, half in overlaps(windows, base, segments):
            target[to : to + rows] = xs[slot * 8 + at : slot * 8 + at + rows, half]
    for c in waits:
        c.wait()


def stage(layer, windows, work, wet, held, sources, sinks, name, opening=False, brings=()):
    ins = [array for array, _ in sources]
    shapes = [jax.ShapeDtypeStruct((sum(h - l for _, l, h in segments), 8, C), f32) for segments in sinks]
    kernel = functools.partial(
        stage_kernel, layer, windows, work, [segments for _, segments in sources], sinks, opening, bool(brings)
    )
    extra = []
    if opening:
        extra = held_shapes(held)
        extra += [jax.ShapeDtypeStruct((8, LANES), jnp.int32), jax.ShapeDtypeStruct((8, 2, 8, C), f32)]
    extra += held_shapes(brings)
    place = HBM if opening else VM
    rows = min(2, len(work)) * TOK
    return pl.pallas_call(
        kernel,
        out_shape=shapes + extra,
        in_specs=[place] * (8 + len(ins)) + [HBM] * len(brings),
        out_specs=[VM] * len(shapes + extra),
        scratch_shapes=[
            pltpu.VMEM((8 * len(windows), 2, 8, C), f32),
            pltpu.VMEM((rows, 3 * C), bf16),
            pltpu.VMEM((rows, C), bf16),
            pltpu.SMEM((LAYERS, 16, 32), jnp.int32),
            pltpu.SemaphoreType.DMA((7,)),
            pltpu.SemaphoreType.DMA((3,)),
        ],
        compiler_params=pltpu.CompilerParams(vmem_limit_bytes=24 << 20),
        cost_estimate=pl.CostEstimate(flops=4_000_000_000, bytes_accessed=6_000_000, transcendentals=800_000),
        name=name,
    )(wet, *held, *ins, *brings)


def send(block, d_lat, d_lon):
    n_lat, n_lon = lax.axis_size("lat"), lax.axis_size("lon")
    route = [
        (a * n_lon + b, (a + d_lat) % n_lat * n_lon + (b + d_lon) % n_lon)
        for a in range(n_lat)
        for b in range(n_lon)
    ]
    return lax.ppermute(block, ("lat", "lon"), route)


def finish_kernel(placed, *refs):
    ins, out, sem = refs[: len(placed)], refs[len(placed)], refs[len(placed) + 1]
    copies = []
    for source, segments in zip(ins, placed):
        at = 0
        for half, low, high in segments:
            part = source.at[at : at + high - low]
            copies.append(pltpu.make_async_copy(part, out.at[low:high, half], sem.at[len(copies)]))
            copies[-1].start()
            at += high - low
    for c in copies:
        c.wait()


def local(tokens, wet_flags, ln_attn, w_qkv, w_out, pos_bias, ln_mlp, w_up, w_down):
    params = [ln_attn, w_qkv, pos_bias, w_out, ln_mlp, w_up, w_down]
    wet = wet_flags.transpose(0, 2, 1)
    grid = tokens.reshape(32, 2, 8, C)
    params = [pltpu.with_memory_space_constraint(p, pltpu.HBM) for p in params]
    wet = pltpu.with_memory_space_constraint(wet, pltpu.HBM)
    grid = pltpu.with_memory_space_constraint(grid, pltpu.HBM)
    for pair in range(LAYERS // 2):
        even, odd = 2 * pair, 2 * pair + 1
        most = [[(0, 8, 32)], [(1, 8, 32)]]
        if pair == 0:
            west_a, keep_a, *rest = stage(
                even, [1, 2, 3], [0, 1, 2], wet, params, [(grid, [])], most, "even0a", opening=True
            )
            held, wet, last = rest[:7], rest[7], [(rest[8], [(None, 0, 8)])]
        else:
            inner = stage(
                even, [2], [0], wet, held, [(back_a, [(0, 12, 28)]), (keep_e, [(1, 12, 28)])],
                [[(0, 16, 24)], [(1, 16, 24)]], f"even{pair}e",
            )
            sides = [(0, 4, 12), (0, 28, 32)]
            west_a, keep_a, *coming = stage(
                even, [1, 2, 3], [0, 2], wet, held,
                [
                    (back_b, sides),
                    (keep_l, [(1, 4, 12), (1, 28, 32)]),
                    (back_a, [(0, 12, 16), (0, 0, 8), (0, 24, 28)]),
                    (keep_e, [(1, 12, 16), (1, 0, 8), (1, 24, 28)]),
                    (inner[0], [(0, 16, 24)]),
                    (inner[1], [(1, 16, 24)]),
                ],
                most, f"even{pair}a", brings=params,
            )
            last = [(back_b, sides), (keep_l, [(1, 4, 12)]), (back_diag, [(0, 0, 4)]), (back_lat, [(1, 0, 4)])]
        west_a = send(west_a, 0, -1)
        west_b, up_lat, up_diag, keep_b, *more = stage(
            even, [0], [0], wet, held, last, [[(0, 4, 8)], [(1, 0, 4)], [(0, 0, 4)], [(1, 4, 8)]],
            f"even{pair}b", brings=params if pair == 0 else (),
        )
        west_b = send(west_b, 0, -1)
        up_lat = send(up_lat, -1, 0)
        up_diag = send(up_diag, -1, -1)
        held = more if pair == 0 else coming
        own, other = (keep_a, [(0, 8, 32)]), (west_a, [(1, 8, 32)])
        keep_e, back_a = stage(
            odd, [1, 2], [0, 1], wet, held, [own, other], [[(0, 12, 28)], [(1, 12, 28)]], f"odd{pair}a"
        )
        back_a = send(back_a, 0, 1)
        keep_l, back_b, back_lat, back_diag, *coming = stage(
            odd, [0, 3], [0, 1], wet, held,
            [own, other, (keep_b, [(0, 4, 8)]), (west_b, [(1, 4, 8)]), (up_lat, [(0, 32, 36)]), (up_diag, [(1, 32, 36)])],
            [[(0, 4, 12), (0, 28, 32)], [(1, 4, 12), (1, 28, 32)], [(0, 32, 36)], [(1, 32, 36)]],
            f"odd{pair}b", brings=params if odd + 1 < LAYERS else (),
        )
        back_b = send(back_b, 0, 1)
        back_lat = send(back_lat, 1, 0)
        back_diag = send(back_diag, 1, 1)
        held = coming
    parts = [
        (back_a, [(0, 12, 28)]),
        (back_b, [(0, 4, 12), (0, 28, 32)]),
        (back_diag, [(0, 0, 4)]),
        (back_lat, [(1, 0, 4)]),
        (keep_l, [(1, 4, 12), (1, 28, 32)]),
        (keep_e, [(1, 12, 28)]),
    ]
    out = pl.pallas_call(
        functools.partial(finish_kernel, [segments for _, segments in parts]),
        out_shape=jax.ShapeDtypeStruct((32, 2, 8, C), f32),
        in_specs=[VM] * len(parts),
        out_specs=HBM,
        scratch_shapes=[pltpu.SemaphoreType.DMA((8,))],
        compiler_params=pltpu.CompilerParams(vmem_limit_bytes=4 << 20),
        name="finish",
    )(*[array for array, _ in parts])
    return out.reshape(32, 16, C)


def solution(mesh):
    in_specs = (P("lat", "lon", None), P(), P(), P(), P(), P(), P(), P(), P())
    out_specs = P("lat", "lon", None)
    return jax.shard_map(local, mesh=mesh, in_specs=in_specs, out_specs=out_specs, check_vma=False)
```

```python
import functools

import jax
import jax.numpy as jnp
from jax import lax
from jax.experimental import pallas as pl
from jax.experimental.pallas import tpu as pltpu
from jax.sharding import PartitionSpec as P

C = 384
HEADS = 12
FFN = 1536
TOK = 128
LANES = 128
GROUP = 4
HEAD = 32
LAYERS = 4
CHUNK = 256
norm_eps = 1e-05
mask_fill = -1000000000.0
ERF_POLY = (
    0.7978275160691982,
    0.03647005390043865,
    -0.00012554234498973965,
    -3.0455015643046705e-05,
    1.1119467340375738e-06,
)
f32 = jnp.float32
bf16 = jnp.bfloat16
HBM = pl.BlockSpec(memory_space=pltpu.HBM)


def gelu(x):
    rounded = x.astype(bf16)
    square = rounded * rounded
    poly = bf16(ERF_POLY[-1])
    for factor in ERF_POLY[-2::-1]:
        poly = poly * square + bf16(factor)
    half = 0.5 * x
    return half + half * jnp.tanh((rounded * poly).astype(f32))


def layer_norm(x, gain):
    center = jnp.mean(x, axis=-1, keepdims=True)
    away = x - center
    spread = jnp.mean(away * away, axis=-1, keepdims=True)
    return (away * lax.rsqrt(spread + norm_eps) * gain).astype(bf16)


def attend(q, k, v, bias_ref, group, masked):
    owner = lax.broadcasted_iota(jnp.int32, (TOK, LANES), 1) // HEAD
    zero = jnp.zeros((TOK, LANES), bf16)
    one = jnp.ones((TOK, LANES), bf16)
    keys = jnp.concatenate([jnp.where(owner == h, k, zero) for h in range(GROUP)], axis=0)
    scores = lax.dot_general(q, keys, (((1,), (1,)), ((), ())), preferred_element_type=f32)
    parts = []
    for h in range(GROUP):
        s = scores[:, h * TOK : (h + 1) * TOK] * HEAD ** (-0.5) + bias_ref[group * GROUP + h]
        if masked is not None:
            s = jnp.where(masked, mask_fill, s)
        parts.append(jnp.exp(s - jnp.max(s, axis=-1, keepdims=True)).astype(bf16))
    weights = jnp.concatenate(parts, axis=1)
    values = jnp.concatenate(
        [
            jnp.concatenate([jnp.where(owner == h, v, zero), jnp.where(owner == h, one, zero)], axis=1)
            for h in range(GROUP)
        ],
        axis=0,
    )
    both = jnp.dot(weights, values, preferred_element_type=f32)
    return (both[:, :LANES] / both[:, LANES:]).astype(bf16)


class Buffers:
    pass


def run_windows(b, ids, masked, ready):
    count = len(ids)
    rows = count * TOK
    x = jnp.concatenate([b.xs[pl.ds(i * 8, 8)].reshape(TOK, C) for i in ids], axis=0)
    ready("ga", "wq")
    b.qkv[:rows] = jnp.dot(layer_norm(x, b.ga[...]), b.wq[...], preferred_element_type=f32).astype(bf16)
    ready("bias")
    for w in range(count):
        span = slice(w * TOK, (w + 1) * TOK)
        hide = None
        if masked is not None:
            low_q = lax.broadcasted_iota(jnp.int32, (TOK, TOK), 0) >= TOK // 2
            low_k = lax.broadcasted_iota(jnp.int32, (TOK, TOK), 1) >= TOK // 2
            hide = jnp.logical_and(low_q != low_k, masked[w])
        for g in range(HEADS // GROUP):
            at = g * LANES
            b.att[span, at : at + LANES] = attend(
                b.qkv[span, at : at + LANES],
                b.qkv[span, C + at : C + at + LANES],
                b.qkv[span, 2 * C + at : 2 * C + at + LANES],
                b.bias,
                g,
                hide,
            )
    ready("wo", "gm")
    resid = x + jnp.dot(b.att[:rows], b.wo[...], preferred_element_type=f32)
    mlp_in = layer_norm(resid, b.gm[...])
    total = resid
    ready("wu", "wd")
    for f in range(0, FFN, CHUNK):
        up = jnp.dot(mlp_in, b.wu[:, f : f + CHUNK], preferred_element_type=f32)
        total = total + jnp.dot(gelu(up).astype(bf16), b.wd[f : f + CHUNK, :], preferred_element_type=f32)
    for w, i in enumerate(ids):
        b.xs[pl.ds(i * 8, 8)] = total[w * TOK : (w + 1) * TOK].reshape(8, 2, 8, C)


NAMES = ("ga", "wq", "bias", "wo", "gm", "wu", "wd")


def start_loads(params, held, layer, sem, names, wanted):
    copies = {}
    for n, name in enumerate(names):
        if name not in wanted:
            continue
        source = params[n]
        part = source.at[pl.ds(layer, 1)] if len(source.shape) == 2 else source.at[layer]
        copies[name] = pltpu.make_async_copy(part, held[n], sem.at[n])
        copies[name].start()
    return copies


def held_shapes(params):
    return [jax.ShapeDtypeStruct((1, C) if p.ndim == 2 else p.shape[1:], p.dtype) for p in params]


VM = pl.BlockSpec(memory_space=pltpu.VMEM)


def overlaps(windows, base, segments):
    pieces = []
    for slot, window in enumerate(windows):
        top = base + 8 * window
        at = 0
        for half, low, high in segments:
            first, last = max(top, low), min(top + 8, high)
            if first < last:
                pieces.append((slot, first - top, at + first - low, last - first, half))
            at += high - low
    return pieces


def stage_kernel(layer, windows, work, sources, sinks, opening, names, *refs):
    refs = list(refs)

    def take(count):
        got, refs[:count] = refs[:count], []
        return got

    (wet,) = take(1)
    given = take(7)
    ins = take(len(sources))
    coming = take(len(names))
    outs = take(len(sinks))
    row = wet
    held = given
    if opening:
        held = take(7)
        row, rest = take(2)
    arrived = take(len(names))
    xs, qkv, att, s_wet, sem, in_sem = refs
    lat = lax.axis_index("lat")
    lon = lax.axis_index("lon")
    bands = lax.axis_size("lat")
    base = 4 if layer % 2 == 1 else 0
    pending = {}
    waits = []
    if opening:
        flags = pltpu.make_async_copy(wet, s_wet, in_sem.at[0])
        block = pltpu.make_async_copy(ins[0].at[8:32], xs, in_sem.at[1])
        others = pltpu.make_async_copy(ins[0].at[0:8], rest, in_sem.at[2])
        flags.start()
        block.start()
        pending = start_loads(given, held, layer, sem, NAMES, ("ga", "wq"))
        flags.wait()
        pending |= start_loads(given, held, layer, sem, NAMES, ("bias", "wo", "gm", "wu", "wd"))
        others.start()
        waits.append(others)
        which_layer = lax.broadcasted_iota(jnp.int32, (8, LANES), 0)
        which_window = lax.broadcasted_iota(jnp.int32, (8, LANES), 1)
        mine = jnp.zeros((8, LANES), jnp.int32)
        for n in range(LAYERS):
            for j in range(4):
                here = jnp.logical_and(which_layer == n, which_window == j)
                mine = jnp.where(here, s_wet[n, lon, lat * 4 + j], mine)
        row[...] = mine
        is_wet = [s_wet[layer, lon, lat * 4 + windows[slot]] == 1 for slot in work]
        block.wait()
    else:
        waits = list(start_loads(coming, arrived, layer + 1, sem, names, names).values())
        for source, segments in zip(ins, sources):
            for slot, to, at, count, half in overlaps(windows, base, segments):
                if half is None:
                    xs[slot * 8 + to : slot * 8 + to + count] = source[at : at + count]
                else:
                    xs[slot * 8 + to : slot * 8 + to + count, half] = source[at : at + count]
        is_wet = [row[layer, windows[slot]] == 1 for slot in work]

    def ready(*names):
        for name in names:
            if name in pending:
                pending[name].wait()

    b = Buffers()
    b.xs, b.qkv, b.att = xs, qkv, att
    b.ga, b.wq, b.bias, b.wo, b.gm, b.wu, b.wd = held
    first_slot = jnp.int32(work[-1])
    last_slot = jnp.int32(work[0])
    count = jnp.int32(0)
    for slot, flag in reversed(list(zip(work, is_wet))):
        first_slot = jnp.where(flag, slot, first_slot)
    for slot, flag in zip(work, is_wet):
        last_slot = jnp.where(flag, slot, last_slot)
        count += flag.astype(jnp.int32)
    masking = base == 4 and 3 in [windows[slot] for slot in work]

    def run(ids):
        masked = None
        if masking:
            masked = [jnp.logical_and(lat == bands - 1, i == windows.index(3)) for i in ids]
        run_windows(b, ids, masked, ready)

    if len(work) > 1:

        @pl.when(count >= 2)
        def _():
            run([first_slot, last_slot if len(work) == 2 else jnp.where(count == 3, work[1], last_slot)])
            if opening:
                pending_before = dict(pending)
                pending.clear()
                single = count == 3

                @pl.when(single)
                def _():
                    run([jnp.int32(work[2])])

                pending.update(pending_before)

    @pl.when(count == 1)
    def _():
        run([first_slot])

    if opening:

        @pl.when(count == 0)
        def _():
            ready(*NAMES)

    for target, segments in zip(outs, sinks):
        for slot, at, to, rows, half in overlaps(windows, base, segments):
            target[to : to + rows] = xs[slot * 8 + at : slot * 8 + at + rows, half]
    for c in waits:
        c.wait()


def stage(layer, windows, work, wet, held, sources, sinks, name, opening=False, brings=None):
    brings = brings or {}
    ins = [array for array, _ in sources]
    shapes = [jax.ShapeDtypeStruct((sum(h - l for _, l, h in segments), 8, C), f32) for segments in sinks]
    kernel = functools.partial(
        stage_kernel, layer, windows, work, [segments for _, segments in sources], sinks, opening, tuple(brings)
    )
    extra = []
    if opening:
        extra = held_shapes(held)
        extra += [jax.ShapeDtypeStruct((8, LANES), jnp.int32), jax.ShapeDtypeStruct((8, 2, 8, C), f32)]
    extra += held_shapes(list(brings.values()))
    place = HBM if opening else VM
    rows = min(2, len(work)) * TOK
    return pl.pallas_call(
        kernel,
        out_shape=shapes + extra,
        in_specs=[place] * (8 + len(ins)) + [HBM] * len(brings),
        out_specs=[VM] * len(shapes + extra),
        scratch_shapes=[
            pltpu.VMEM((8 * len(windows), 2, 8, C), f32),
            pltpu.VMEM((rows, 3 * C), bf16),
            pltpu.VMEM((rows, C), bf16),
            pltpu.SMEM((LAYERS, 16, 32), jnp.int32),
            pltpu.SemaphoreType.DMA((7,)),
            pltpu.SemaphoreType.DMA((3,)),
        ],
        compiler_params=pltpu.CompilerParams(vmem_limit_bytes=24 << 20),
        cost_estimate=pl.CostEstimate(flops=4_000_000_000, bytes_accessed=6_000_000, transcendentals=800_000),
        name=name,
    )(wet, *held, *ins, *brings.values())


def send(block, d_lat, d_lon):
    n_lat, n_lon = lax.axis_size("lat"), lax.axis_size("lon")
    route = [
        (a * n_lon + b, (a + d_lat) % n_lat * n_lon + (b + d_lon) % n_lon)
        for a in range(n_lat)
        for b in range(n_lon)
    ]
    return lax.ppermute(block, ("lat", "lon"), route)


def finish_kernel(placed, *refs):
    ins, out, sem = refs[: len(placed)], refs[len(placed)], refs[len(placed) + 1]
    copies = []
    for source, segments in zip(ins, placed):
        at = 0
        for half, low, high in segments:
            part = source.at[at : at + high - low]
            copies.append(pltpu.make_async_copy(part, out.at[low:high, half], sem.at[len(copies)]))
            copies[-1].start()
            at += high - low
    for c in copies:
        c.wait()


def local(tokens, wet_flags, ln_attn, w_qkv, w_out, pos_bias, ln_mlp, w_up, w_down):
    params = [ln_attn, w_qkv, pos_bias, w_out, ln_mlp, w_up, w_down]
    wet = wet_flags.transpose(0, 2, 1)
    grid = tokens.reshape(32, 2, 8, C)
    params = [pltpu.with_memory_space_constraint(p, pltpu.HBM) for p in params]
    wet = pltpu.with_memory_space_constraint(wet, pltpu.HBM)
    grid = pltpu.with_memory_space_constraint(grid, pltpu.HBM)
    first = {name: p for name, p in zip(NAMES, params) if name in ("wu", "wd")}
    second = {name: p for name, p in zip(NAMES, params) if name not in first}
    for pair in range(LAYERS // 2):
        even, odd = 2 * pair, 2 * pair + 1
        most = [[(0, 8, 32)], [(1, 8, 32)]]
        if pair == 0:
            west_a, keep_a, *rest = stage(
                even, [1, 2, 3], [0, 1, 2], wet, params, [(grid, [])], most, "even0a", opening=True
            )
            held, wet, last = rest[:7], rest[7], [(rest[8], [(None, 0, 8)])]
        else:
            *inner, wu, wd = stage(
                even, [2], [0], wet, held, [(back_a, [(0, 12, 28)]), (keep_e, [(1, 12, 28)])],
                [[(0, 16, 24)], [(1, 16, 24)]], f"even{pair}e", brings=first,
            )
            sides = [(0, 4, 12), (0, 28, 32)]
            west_a, keep_a, *coming = stage(
                even, [1, 2, 3], [0, 2], wet, held,
                [
                    (back_b, sides),
                    (keep_l, [(1, 4, 12), (1, 28, 32)]),
                    (back_a, [(0, 12, 16), (0, 0, 8), (0, 24, 28)]),
                    (keep_e, [(1, 12, 16), (1, 0, 8), (1, 24, 28)]),
                    (inner[0], [(0, 16, 24)]),
                    (inner[1], [(1, 16, 24)]),
                ],
                most, f"even{pair}a", brings=second,
            )
            last = [(back_b, sides), (keep_l, [(1, 4, 12)]), (back_diag, [(0, 0, 4)]), (back_lat, [(1, 0, 4)])]
        west_a = send(west_a, 0, -1)
        west_b, up_lat, up_diag, keep_b, *more = stage(
            even, [0], [0], wet, held, last, [[(0, 4, 8)], [(1, 0, 4)], [(0, 0, 4)], [(1, 4, 8)]],
            f"even{pair}b", brings=dict(zip(NAMES, params)) if pair == 0 else None,
        )
        west_b = send(west_b, 0, -1)
        up_lat = send(up_lat, -1, 0)
        up_diag = send(up_diag, -1, -1)
        held = more if pair == 0 else [*coming, wu, wd]
        own, other = (keep_a, [(0, 8, 32)]), (west_a, [(1, 8, 32)])
        more = odd + 1 < LAYERS
        keep_e, back_a, *wide = stage(
            odd, [1, 2], [0, 1], wet, held, [own, other], [[(0, 12, 28)], [(1, 12, 28)]], f"odd{pair}a",
            brings=first if more else None,
        )
        back_a = send(back_a, 0, 1)
        keep_l, back_b, back_lat, back_diag, *coming = stage(
            odd, [0, 3], [0, 1], wet, held,
            [own, other, (keep_b, [(0, 4, 8)]), (west_b, [(1, 4, 8)]), (up_lat, [(0, 32, 36)]), (up_diag, [(1, 32, 36)])],
            [[(0, 4, 12), (0, 28, 32)], [(1, 4, 12), (1, 28, 32)], [(0, 32, 36)], [(1, 32, 36)]],
            f"odd{pair}b", brings=second if more else None,
        )
        back_b = send(back_b, 0, 1)
        back_lat = send(back_lat, 1, 0)
        back_diag = send(back_diag, 1, 1)
        held = [*coming, *wide]
    parts = [
        (back_a, [(0, 12, 28)]),
        (back_b, [(0, 4, 12), (0, 28, 32)]),
        (back_diag, [(0, 0, 4)]),
        (back_lat, [(1, 0, 4)]),
        (keep_l, [(1, 4, 12), (1, 28, 32)]),
        (keep_e, [(1, 12, 28)]),
    ]
    out = pl.pallas_call(
        functools.partial(finish_kernel, [segments for _, segments in parts]),
        out_shape=jax.ShapeDtypeStruct((32, 2, 8, C), f32),
        in_specs=[VM] * len(parts),
        out_specs=HBM,
        scratch_shapes=[pltpu.SemaphoreType.DMA((8,))],
        compiler_params=pltpu.CompilerParams(vmem_limit_bytes=4 << 20),
        name="finish",
    )(*[array for array, _ in parts])
    return out.reshape(32, 16, C)


def solution(mesh):
    in_specs = (P("lat", "lon", None), P(), P(), P(), P(), P(), P(), P(), P())
    out_specs = P("lat", "lon", None)
    return jax.shard_map(local, mesh=mesh, in_specs=in_specs, out_specs=out_specs, check_vma=False)
```

```python
import functools

import jax
import jax.numpy as jnp
from jax import lax
from jax.experimental import pallas as pl
from jax.experimental.pallas import tpu as pltpu
from jax.sharding import PartitionSpec as P

C = 384
HEADS = 12
FFN = 1536
TOK = 128
LANES = 128
GROUP = 4
HEAD = 32
LAYERS = 4
CHUNK = 256
norm_eps = 1e-05
mask_fill = -1000000000.0
ERF_POLY = (
    0.7978275160691982,
    0.03647005390043865,
    -0.00012554234498973965,
    -3.0455015643046705e-05,
    1.1119467340375738e-06,
)
f32 = jnp.float32
bf16 = jnp.bfloat16
HBM = pl.BlockSpec(memory_space=pltpu.HBM)


def gelu(x):
    rounded = x.astype(bf16)
    square = rounded * rounded
    poly = bf16(ERF_POLY[-1])
    for factor in ERF_POLY[-2::-1]:
        poly = poly * square + bf16(factor)
    half = 0.5 * x
    return half + half * jnp.tanh((rounded * poly).astype(f32))


def layer_norm(x, gain):
    center = jnp.mean(x, axis=-1, keepdims=True)
    away = x - center
    spread = jnp.mean(away * away, axis=-1, keepdims=True)
    return (away * lax.rsqrt(spread + norm_eps) * gain).astype(bf16)


def attend(q, k, v, bias_ref, group, masked):
    owner = lax.broadcasted_iota(jnp.int32, (TOK, LANES), 1) // HEAD
    zero = jnp.zeros((TOK, LANES), bf16)
    one = jnp.ones((TOK, LANES), bf16)
    keys = jnp.concatenate([jnp.where(owner == h, k, zero) for h in range(GROUP)], axis=0)
    scores = lax.dot_general(q, keys, (((1,), (1,)), ((), ())), preferred_element_type=f32)
    parts = []
    for h in range(GROUP):
        s = scores[:, h * TOK : (h + 1) * TOK] * HEAD ** (-0.5) + bias_ref[group * GROUP + h]
        if masked is not None:
            s = jnp.where(masked, mask_fill, s)
        parts.append(jnp.exp(s - jnp.max(s, axis=-1, keepdims=True)).astype(bf16))
    weights = jnp.concatenate(parts, axis=1)
    values = jnp.concatenate(
        [
            jnp.concatenate([jnp.where(owner == h, v, zero), jnp.where(owner == h, one, zero)], axis=1)
            for h in range(GROUP)
        ],
        axis=0,
    )
    both = jnp.dot(weights, values, preferred_element_type=f32)
    return (both[:, :LANES] / both[:, LANES:]).astype(bf16)


class Buffers:
    pass


def run_windows(b, ids, masked, ready):
    count = len(ids)
    rows = count * TOK
    x = jnp.concatenate([b.xs[pl.ds(i * 8, 8)].reshape(TOK, C) for i in ids], axis=0)
    ready("ga", "wq")
    b.qkv[:rows] = jnp.dot(layer_norm(x, b.ga[...]), b.wq[...], preferred_element_type=f32).astype(bf16)
    ready("bias")
    for w in range(count):
        span = slice(w * TOK, (w + 1) * TOK)
        hide = None
        if masked is not None:
            low_q = lax.broadcasted_iota(jnp.int32, (TOK, TOK), 0) >= TOK // 2
            low_k = lax.broadcasted_iota(jnp.int32, (TOK, TOK), 1) >= TOK // 2
            hide = jnp.logical_and(low_q != low_k, masked[w])
        for g in range(HEADS // GROUP):
            at = g * LANES
            b.att[span, at : at + LANES] = attend(
                b.qkv[span, at : at + LANES],
                b.qkv[span, C + at : C + at + LANES],
                b.qkv[span, 2 * C + at : 2 * C + at + LANES],
                b.bias,
                g,
                hide,
            )
    ready("wo", "gm")
    resid = x + jnp.dot(b.att[:rows], b.wo[...], preferred_element_type=f32)
    mlp_in = layer_norm(resid, b.gm[...])
    total = resid
    ready("wu", "wd")
    for f in range(0, FFN, CHUNK):
        up = jnp.dot(mlp_in, b.wu[:, f : f + CHUNK], preferred_element_type=f32)
        total = total + jnp.dot(gelu(up).astype(bf16), b.wd[f : f + CHUNK, :], preferred_element_type=f32)
    for w, i in enumerate(ids):
        b.xs[pl.ds(i * 8, 8)] = total[w * TOK : (w + 1) * TOK].reshape(8, 2, 8, C)


NAMES = ("ga", "wq", "bias", "wo", "gm", "wu", "wd")


def start_loads(params, held, layer, sem, names):
    copies = {}
    for n, name in enumerate(NAMES):
        if name not in names:
            continue
        source = params[n]
        part = source.at[pl.ds(layer, 1)] if len(source.shape) == 2 else source.at[layer]
        copies[name] = pltpu.make_async_copy(part, held[n], sem.at[n])
        copies[name].start()
    return copies


def held_shapes(params):
    return [jax.ShapeDtypeStruct((1, C) if p.ndim == 2 else p.shape[1:], p.dtype) for p in params]


VM = pl.BlockSpec(memory_space=pltpu.VMEM)


def overlaps(windows, base, segments):
    pieces = []
    for slot, window in enumerate(windows):
        top = base + 8 * window
        at = 0
        for half, low, high in segments:
            first, last = max(top, low), min(top + 8, high)
            if first < last:
                pieces.append((slot, first - top, at + first - low, last - first, half))
            at += high - low
    return pieces


def stage_kernel(layer, windows, work, sources, sinks, opening, brings, *refs):
    refs = list(refs)

    def take(count):
        got, refs[:count] = refs[:count], []
        return got

    (wet,) = take(1)
    given = take(7)
    ins = take(len(sources))
    coming = take(7) if brings else []
    outs = take(len(sinks))
    row = wet
    held = given
    if opening:
        held = take(7)
        row, rest = take(2)
    arrived = take(7) if brings else []
    xs, qkv, att, s_wet, sem, in_sem = refs
    lat = lax.axis_index("lat")
    lon = lax.axis_index("lon")
    bands = lax.axis_size("lat")
    base = 4 if layer % 2 == 1 else 0
    pending = {}
    waits = []
    if opening:
        flags = pltpu.make_async_copy(wet, s_wet, in_sem.at[0])
        block = pltpu.make_async_copy(ins[0].at[8:32], xs, in_sem.at[1])
        others = pltpu.make_async_copy(ins[0].at[0:8], rest, in_sem.at[2])
        flags.start()
        block.start()
        pending = start_loads(given, held, layer, sem, ("ga", "wq"))
        flags.wait()
        pending |= start_loads(given, held, layer, sem, ("bias", "wo", "gm", "wu", "wd"))
        others.start()
        waits.append(others)
        which_layer = lax.broadcasted_iota(jnp.int32, (8, LANES), 0)
        which_window = lax.broadcasted_iota(jnp.int32, (8, LANES), 1)
        mine = jnp.zeros((8, LANES), jnp.int32)
        for n in range(LAYERS):
            for j in range(4):
                here = jnp.logical_and(which_layer == n, which_window == j)
                mine = jnp.where(here, s_wet[n, lon, lat * 4 + j], mine)
        row[...] = mine
        is_wet = [s_wet[layer, lon, lat * 4 + windows[slot]] == 1 for slot in work]
        block.wait()
    else:
        waits = list(start_loads(coming, arrived, layer + 1, sem, NAMES).values()) if brings else []
        for source, segments in zip(ins, sources):
            for slot, to, at, count, half in overlaps(windows, base, segments):
                if half is None:
                    xs[slot * 8 + to : slot * 8 + to + count] = source[at : at + count]
                else:
                    xs[slot * 8 + to : slot * 8 + to + count, half] = source[at : at + count]
        is_wet = [row[layer, windows[slot]] == 1 for slot in work]

    def ready(*names):
        for name in names:
            if name in pending:
                pending[name].wait()

    b = Buffers()
    b.xs, b.qkv, b.att = xs, qkv, att
    b.ga, b.wq, b.bias, b.wo, b.gm, b.wu, b.wd = held
    first_slot = jnp.int32(work[-1])
    last_slot = jnp.int32(work[0])
    count = jnp.int32(0)
    for slot, flag in reversed(list(zip(work, is_wet))):
        first_slot = jnp.where(flag, slot, first_slot)
    for slot, flag in zip(work, is_wet):
        last_slot = jnp.where(flag, slot, last_slot)
        count += flag.astype(jnp.int32)
    masking = base == 4 and 3 in [windows[slot] for slot in work]

    def run(ids):
        masked = None
        if masking:
            masked = [jnp.logical_and(lat == bands - 1, i == windows.index(3)) for i in ids]
        run_windows(b, ids, masked, ready)

    if len(work) > 1:

        @pl.when(count >= 2)
        def _():
            run([first_slot, last_slot if len(work) == 2 else jnp.where(count == 3, work[1], last_slot)])
            if opening:
                pending_before = dict(pending)
                pending.clear()
                single = count == 3

                @pl.when(single)
                def _():
                    run([jnp.int32(work[2])])

                pending.update(pending_before)

    @pl.when(count == 1)
    def _():
        run([first_slot])

    if opening:

        @pl.when(count == 0)
        def _():
            ready(*NAMES)

    for target, segments in zip(outs, sinks):
        for slot, at, to, rows, half in overlaps(windows, base, segments):
            target[to : to + rows] = xs[slot * 8 + at : slot * 8 + at + rows, half]
    for c in waits:
        c.wait()


def stage(layer, windows, work, wet, held, sources, sinks, name, opening=False, brings=()):
    ins = [array for array, _ in sources]
    shapes = [jax.ShapeDtypeStruct((sum(h - l for _, l, h in segments), 8, C), f32) for segments in sinks]
    kernel = functools.partial(
        stage_kernel, layer, windows, work, [segments for _, segments in sources], sinks, opening, bool(brings)
    )
    extra = []
    if opening:
        extra = held_shapes(held)
        extra += [jax.ShapeDtypeStruct((8, LANES), jnp.int32), jax.ShapeDtypeStruct((8, 2, 8, C), f32)]
    extra += held_shapes(brings)
    place = HBM if opening else VM
    rows = min(2, len(work)) * TOK
    return pl.pallas_call(
        kernel,
        out_shape=shapes + extra,
        in_specs=[place] * (8 + len(ins)) + [HBM] * len(brings),
        out_specs=[VM] * len(shapes + extra),
        scratch_shapes=[
            pltpu.VMEM((8 * len(windows), 2, 8, C), f32),
            pltpu.VMEM((rows, 3 * C), bf16),
            pltpu.VMEM((rows, C), bf16),
            pltpu.SMEM((LAYERS, 16, 32), jnp.int32),
            pltpu.SemaphoreType.DMA((7,)),
            pltpu.SemaphoreType.DMA((3,)),
        ],
        compiler_params=pltpu.CompilerParams(vmem_limit_bytes=24 << 20),
        cost_estimate=pl.CostEstimate(flops=4_000_000_000, bytes_accessed=6_000_000, transcendentals=800_000),
        name=name,
    )(wet, *held, *ins, *brings)


def send(block, d_lat, d_lon):
    n_lat, n_lon = lax.axis_size("lat"), lax.axis_size("lon")
    route = [
        (a * n_lon + b, (a + d_lat) % n_lat * n_lon + (b + d_lon) % n_lon)
        for a in range(n_lat)
        for b in range(n_lon)
    ]
    return lax.ppermute(block, ("lat", "lon"), route)


def finish_kernel(placed, *refs):
    ins, out, sem = refs[: len(placed)], refs[len(placed)], refs[len(placed) + 1]
    copies = []
    for source, segments in zip(ins, placed):
        at = 0
        for half, low, high in segments:
            part = source.at[at : at + high - low]
            copies.append(pltpu.make_async_copy(part, out.at[low:high, half], sem.at[len(copies)]))
            copies[-1].start()
            at += high - low
    for c in copies:
        c.wait()


def local(tokens, wet_flags, ln_attn, w_qkv, w_out, pos_bias, ln_mlp, w_up, w_down):
    params = [ln_attn, w_qkv, pos_bias, w_out, ln_mlp, w_up, w_down]
    wet = wet_flags.transpose(0, 2, 1)
    grid = tokens.reshape(32, 2, 8, C)
    params = [pltpu.with_memory_space_constraint(p, pltpu.HBM) for p in params]
    wet = pltpu.with_memory_space_constraint(wet, pltpu.HBM)
    grid = pltpu.with_memory_space_constraint(grid, pltpu.HBM)
    for pair in range(LAYERS // 2):
        even, odd = 2 * pair, 2 * pair + 1
        rim = [(0, 8, 12), (0, 28, 32)]
        most = [[(0, 12, 28)], [(1, 8, 32)], rim]
        if pair == 0:
            west_a, keep_a, edge, *rest = stage(
                even, [1, 2, 3], [0, 1, 2], wet, params, [(grid, [])], most, "even0a", opening=True
            )
            held, wet, last = rest[:7], rest[7], [(rest[8], [(None, 0, 8)])]
        else:
            inner = stage(
                even, [2], [0], wet, held, [(back_a, [(0, 12, 28)]), (keep_e, [(1, 12, 28)])],
                [[(0, 16, 24)], [(1, 16, 24)]], f"even{pair}e",
            )
            sides = [(0, 4, 12), (0, 28, 32)]
            west_a, keep_a, edge, *coming = stage(
                even, [1, 2, 3], [0, 2], wet, held,
                [
                    (back_b, sides),
                    (keep_l, [(1, 4, 12), (1, 28, 32)]),
                    (back_a, [(0, 12, 16), (0, 0, 8), (0, 24, 28)]),
                    (keep_e, [(1, 12, 16), (1, 0, 8), (1, 24, 28)]),
                    (inner[0], [(0, 16, 24)]),
                    (inner[1], [(1, 16, 24)]),
                ],
                most, f"even{pair}a", brings=params,
            )
            last = [(back_b, sides), (keep_l, [(1, 4, 12)]), (back_diag, [(0, 0, 4)]), (back_lat, [(1, 0, 4)])]
        west_a = send(west_a, 0, -1)
        west_b, up_lat, up_diag, keep_b, *more = stage(
            even, [0, 1, 3], [0], wet, held, [*last, (edge, rim)],
            [[(0, 4, 12), (0, 28, 32)], [(1, 0, 4)], [(0, 0, 4)], [(1, 4, 8)]],
            f"even{pair}b", brings=params if pair == 0 else (),
        )
        west_b = send(west_b, 0, -1)
        up_lat = send(up_lat, -1, 0)
        up_diag = send(up_diag, -1, -1)
        held = more if pair == 0 else coming
        own, other = (keep_a, [(0, 8, 32)]), (west_a, [(1, 12, 28)])
        keep_e, back_a = stage(
            odd, [1, 2], [0, 1], wet, held, [own, other], [[(0, 12, 28)], [(1, 12, 28)]], f"odd{pair}a"
        )
        back_a = send(back_a, 0, 1)
        keep_l, back_b, back_lat, back_diag, *coming = stage(
            odd, [0, 3], [0, 1], wet, held,
            [own, other, (keep_b, [(0, 4, 8)]), (west_b, [(1, 4, 12), (1, 28, 32)]), (up_lat, [(0, 32, 36)]), (up_diag, [(1, 32, 36)])],
            [[(0, 4, 12), (0, 28, 32)], [(1, 4, 12), (1, 28, 32)], [(0, 32, 36)], [(1, 32, 36)]],
            f"odd{pair}b", brings=params if odd + 1 < LAYERS else (),
        )
        back_b = send(back_b, 0, 1)
        back_lat = send(back_lat, 1, 0)
        back_diag = send(back_diag, 1, 1)
        held = coming
    parts = [
        (back_a, [(0, 12, 28)]),
        (back_b, [(0, 4, 12), (0, 28, 32)]),
        (back_diag, [(0, 0, 4)]),
        (back_lat, [(1, 0, 4)]),
        (keep_l, [(1, 4, 12), (1, 28, 32)]),
        (keep_e, [(1, 12, 28)]),
    ]
    out = pl.pallas_call(
        functools.partial(finish_kernel, [segments for _, segments in parts]),
        out_shape=jax.ShapeDtypeStruct((32, 2, 8, C), f32),
        in_specs=[VM] * len(parts),
        out_specs=HBM,
        scratch_shapes=[pltpu.SemaphoreType.DMA((8,))],
        compiler_params=pltpu.CompilerParams(vmem_limit_bytes=4 << 20),
        name="finish",
    )(*[array for array, _ in parts])
    return out.reshape(32, 16, C)


def solution(mesh):
    in_specs = (P("lat", "lon", None), P(), P(), P(), P(), P(), P(), P(), P())
    out_specs = P("lat", "lon", None)
    return jax.shard_map(local, mesh=mesh, in_specs=in_specs, out_specs=out_specs, check_vma=False)
```

```python
import functools

import jax
import jax.numpy as jnp
from jax import lax
from jax.experimental import pallas as pl
from jax.experimental.pallas import tpu as pltpu
from jax.sharding import PartitionSpec as P

C = 384
HEADS = 12
FFN = 1536
TOK = 128
LANES = 128
GROUP = 4
HEAD = 32
LAYERS = 4
CHUNK = 256
norm_eps = 1e-05
mask_fill = -1000000000.0
ERF_POLY = (
    0.7978275160691982,
    0.03647005390043865,
    -0.00012554234498973965,
    -3.0455015643046705e-05,
    1.1119467340375738e-06,
)
f32 = jnp.float32
bf16 = jnp.bfloat16
HBM = pl.BlockSpec(memory_space=pltpu.HBM)


def gelu(x):
    rounded = x.astype(bf16)
    square = rounded * rounded
    poly = bf16(ERF_POLY[-1])
    for factor in ERF_POLY[-2::-1]:
        poly = poly * square + bf16(factor)
    half = 0.5 * x
    return half + half * jnp.tanh((rounded * poly).astype(f32))


def layer_norm(x, gain):
    center = jnp.mean(x, axis=-1, keepdims=True)
    away = x - center
    spread = jnp.mean(away * away, axis=-1, keepdims=True)
    return (away * lax.rsqrt(spread + norm_eps) * gain).astype(bf16)


def attend(q, k, v, bias_ref, group, masked):
    owner = lax.broadcasted_iota(jnp.int32, (TOK, LANES), 1) // HEAD
    zero = jnp.zeros((TOK, LANES), bf16)
    one = jnp.ones((TOK, LANES), bf16)
    keys = jnp.concatenate([jnp.where(owner == h, k, zero) for h in range(GROUP)], axis=0)
    scores = lax.dot_general(q, keys, (((1,), (1,)), ((), ())), preferred_element_type=f32)
    parts = []
    for h in range(GROUP):
        s = scores[:, h * TOK : (h + 1) * TOK] * HEAD ** (-0.5) + bias_ref[group * GROUP + h]
        if masked is not None:
            s = jnp.where(masked, mask_fill, s)
        parts.append(jnp.exp(s - jnp.max(s, axis=-1, keepdims=True)).astype(bf16))
    weights = jnp.concatenate(parts, axis=1)
    values = jnp.concatenate(
        [
            jnp.concatenate([jnp.where(owner == h, v, zero), jnp.where(owner == h, one, zero)], axis=1)
            for h in range(GROUP)
        ],
        axis=0,
    )
    both = jnp.dot(weights, values, preferred_element_type=f32)
    return (both[:, :LANES] / both[:, LANES:]).astype(bf16)


class Buffers:
    pass


def run_windows(b, ids, masked, ready):
    count = len(ids)
    rows = count * TOK
    x = jnp.concatenate([b.xs[pl.ds(i * 8, 8)].reshape(TOK, C) for i in ids], axis=0)
    ready("ga", "wq")
    b.qkv[:rows] = jnp.dot(layer_norm(x, b.ga[...]), b.wq[...], preferred_element_type=f32).astype(bf16)
    ready("bias")
    for w in range(count):
        span = slice(w * TOK, (w + 1) * TOK)
        hide = None
        if masked is not None:
            low_q = lax.broadcasted_iota(jnp.int32, (TOK, TOK), 0) >= TOK // 2
            low_k = lax.broadcasted_iota(jnp.int32, (TOK, TOK), 1) >= TOK // 2
            hide = jnp.logical_and(low_q != low_k, masked[w])
        for g in range(HEADS // GROUP):
            at = g * LANES
            b.att[span, at : at + LANES] = attend(
                b.qkv[span, at : at + LANES],
                b.qkv[span, C + at : C + at + LANES],
                b.qkv[span, 2 * C + at : 2 * C + at + LANES],
                b.bias,
                g,
                hide,
            )
    ready("wo", "gm")
    resid = x + jnp.dot(b.att[:rows], b.wo[...], preferred_element_type=f32)
    mlp_in = layer_norm(resid, b.gm[...])
    total = resid
    ready("wu", "wd")
    for f in range(0, FFN, CHUNK):
        up = jnp.dot(mlp_in, b.wu[:, f : f + CHUNK], preferred_element_type=f32)
        total = total + jnp.dot(gelu(up).astype(bf16), b.wd[f : f + CHUNK, :], preferred_element_type=f32)
    for w, i in enumerate(ids):
        b.xs[pl.ds(i * 8, 8)] = total[w * TOK : (w + 1) * TOK].reshape(8, 2, 8, C)


NAMES = ("ga", "wq", "bias", "wo", "gm", "wu", "wd")


def start_loads(params, held, layer, sem, names):
    copies = {}
    for n, name in enumerate(NAMES):
        if name not in names:
            continue
        source = params[n]
        part = source.at[pl.ds(layer, 1)] if len(source.shape) == 2 else source.at[layer]
        copies[name] = pltpu.make_async_copy(part, held[n], sem.at[n])
        copies[name].start()
    return copies


def held_shapes(params):
    return [jax.ShapeDtypeStruct((1, C) if p.ndim == 2 else p.shape[1:], p.dtype) for p in params]


VM = pl.BlockSpec(memory_space=pltpu.VMEM)


def overlaps(windows, base, segments):
    pieces = []
    for slot, window in enumerate(windows):
        top = base + 8 * window
        at = 0
        for half, low, high in segments:
            first, last = max(top, low), min(top + 8, high)
            if first < last:
                pieces.append((slot, first - top, at + first - low, last - first, half))
            at += high - low
    return pieces


def stage_kernel(layer, windows, work, sources, sinks, opening, brings, *refs):
    refs = list(refs)

    def take(count):
        got, refs[:count] = refs[:count], []
        return got

    (wet,) = take(1)
    given = take(7)
    ins = take(len(sources))
    coming = take(7) if brings else []
    outs = take(len(sinks))
    row = wet
    held = given
    if opening:
        held = take(7)
        row, rest = take(2)
    arrived = take(7) if brings else []
    xs, qkv, att, s_wet, sem, in_sem = refs
    lat = lax.axis_index("lat")
    lon = lax.axis_index("lon")
    bands = lax.axis_size("lat")
    base = 4 if layer % 2 == 1 else 0
    pending = {}
    waits = []
    if opening:
        flags = pltpu.make_async_copy(wet, s_wet, in_sem.at[0])
        block = pltpu.make_async_copy(ins[0].at[8:32], xs, in_sem.at[1])
        others = pltpu.make_async_copy(ins[0].at[0:8], rest, in_sem.at[2])
        flags.start()
        block.start()
        pending = start_loads(given, held, layer, sem, ("ga", "wq"))
        flags.wait()
        pending |= start_loads(given, held, layer, sem, ("bias", "wo", "gm", "wu", "wd"))
        others.start()
        waits.append(others)
        which_layer = lax.broadcasted_iota(jnp.int32, (8, LANES), 0)
        which_window = lax.broadcasted_iota(jnp.int32, (8, LANES), 1)
        mine = jnp.zeros((8, LANES), jnp.int32)
        for n in range(LAYERS):
            for j in range(4):
                here = jnp.logical_and(which_layer == n, which_window == j)
                mine = jnp.where(here, s_wet[n, lon, lat * 4 + j], mine)
        row[...] = mine
        is_wet = [s_wet[layer, lon, lat * 4 + windows[slot]] == 1 for slot in work]
        block.wait()
    else:
        waits = list(start_loads(coming, arrived, layer + 1, sem, NAMES).values()) if brings else []
        for source, segments in zip(ins, sources):
            for slot, to, at, count, half in overlaps(windows, base, segments):
                if half is None:
                    xs[slot * 8 + to : slot * 8 + to + count] = source[at : at + count]
                else:
                    xs[slot * 8 + to : slot * 8 + to + count, half] = source[at : at + count]
        is_wet = [row[layer, windows[slot]] == 1 for slot in work]

    def ready(*names):
        for name in names:
            if name in pending:
                pending[name].wait()

    b = Buffers()
    b.xs, b.qkv, b.att = xs, qkv, att
    b.ga, b.wq, b.bias, b.wo, b.gm, b.wu, b.wd = held
    first_slot = jnp.int32(work[-1])
    last_slot = jnp.int32(work[0])
    count = jnp.int32(0)
    for slot, flag in reversed(list(zip(work, is_wet))):
        first_slot = jnp.where(flag, slot, first_slot)
    for slot, flag in zip(work, is_wet):
        last_slot = jnp.where(flag, slot, last_slot)
        count += flag.astype(jnp.int32)
    masking = base == 4 and 3 in [windows[slot] for slot in work]

    def run(ids):
        masked = None
        if masking:
            masked = [jnp.logical_and(lat == bands - 1, i == windows.index(3)) for i in ids]
        run_windows(b, ids, masked, ready)

    if len(work) > 1:

        @pl.when(count >= 2)
        def _():
            run([first_slot, last_slot if len(work) == 2 else jnp.where(count == 3, work[1], last_slot)])
            if opening:
                pending_before = dict(pending)
                pending.clear()
                single = count == 3

                @pl.when(single)
                def _():
                    run([jnp.int32(work[2])])

                pending.update(pending_before)

    @pl.when(count == 1)
    def _():
        run([first_slot])

    if opening:

        @pl.when(count == 0)
        def _():
            ready(*NAMES)

    for target, segments in zip(outs, sinks):
        for slot, at, to, rows, half in overlaps(windows, base, segments):
            target[to : to + rows] = xs[slot * 8 + at : slot * 8 + at + rows, half]
    for c in waits:
        c.wait()


def stage(layer, windows, work, wet, held, sources, sinks, name, opening=False, brings=()):
    ins = [array for array, _ in sources]
    shapes = [jax.ShapeDtypeStruct((sum(h - l for _, l, h in segments), 8, C), f32) for segments in sinks]
    kernel = functools.partial(
        stage_kernel, layer, windows, work, [segments for _, segments in sources], sinks, opening, bool(brings)
    )
    extra = []
    if opening:
        extra = held_shapes(held)
        extra += [jax.ShapeDtypeStruct((8, LANES), jnp.int32), jax.ShapeDtypeStruct((8, 2, 8, C), f32)]
    extra += held_shapes(brings)
    place = HBM if opening else VM
    cost = 200_000_000 if name[-1] == "e" or layer % 2 == 1 and 1 in windows else 4_000_000_000
    rows = min(2, len(work)) * TOK
    return pl.pallas_call(
        kernel,
        out_shape=shapes + extra,
        in_specs=[place] * (8 + len(ins)) + [HBM] * len(brings),
        out_specs=[VM] * len(shapes + extra),
        scratch_shapes=[
            pltpu.VMEM((8 * len(windows), 2, 8, C), f32),
            pltpu.VMEM((rows, 3 * C), bf16),
            pltpu.VMEM((rows, C), bf16),
            pltpu.SMEM((LAYERS, 16, 32), jnp.int32),
            pltpu.SemaphoreType.DMA((7,)),
            pltpu.SemaphoreType.DMA((3,)),
        ],
        compiler_params=pltpu.CompilerParams(vmem_limit_bytes=24 << 20),
        cost_estimate=pl.CostEstimate(flops=cost, bytes_accessed=100_000, transcendentals=0),
        name=name,
    )(wet, *held, *ins, *brings)


def send(block, d_lat, d_lon):
    n_lat, n_lon = lax.axis_size("lat"), lax.axis_size("lon")
    route = [
        (a * n_lon + b, (a + d_lat) % n_lat * n_lon + (b + d_lon) % n_lon)
        for a in range(n_lat)
        for b in range(n_lon)
    ]
    return lax.ppermute(block, ("lat", "lon"), route)


def finish_kernel(placed, *refs):
    ins, out, sem = refs[: len(placed)], refs[len(placed)], refs[len(placed) + 1]
    copies = []
    for source, segments in zip(ins, placed):
        at = 0
        for half, low, high in segments:
            part = source.at[at : at + high - low]
            copies.append(pltpu.make_async_copy(part, out.at[low:high, half], sem.at[len(copies)]))
            copies[-1].start()
            at += high - low
    for c in copies:
        c.wait()


def local(tokens, wet_flags, ln_attn, w_qkv, w_out, pos_bias, ln_mlp, w_up, w_down):
    params = [ln_attn, w_qkv, pos_bias, w_out, ln_mlp, w_up, w_down]
    wet = wet_flags.transpose(0, 2, 1)
    grid = tokens.reshape(32, 2, 8, C)
    params = [pltpu.with_memory_space_constraint(p, pltpu.HBM) for p in params]
    wet = pltpu.with_memory_space_constraint(wet, pltpu.HBM)
    grid = pltpu.with_memory_space_constraint(grid, pltpu.HBM)
    for pair in range(LAYERS // 2):
        even, odd = 2 * pair, 2 * pair + 1
        rim = [(0, 8, 12), (0, 28, 32)]
        most = [[(0, 12, 28)], [(1, 8, 32)], rim]
        if pair == 0:
            west_a, keep_a, edge, *rest = stage(
                even, [1, 2, 3], [0, 1, 2], wet, params, [(grid, [])], most, "even0a", opening=True
            )
            held, wet, last = rest[:7], rest[7], [(rest[8], [(None, 0, 8)])]
        else:
            inner = stage(
                even, [2], [0], wet, held, [(back_a, [(0, 12, 28)]), (keep_e, [(1, 12, 28)])],
                [[(0, 16, 24)], [(1, 16, 24)]], f"even{pair}e",
            )
            sides = [(0, 4, 12), (0, 28, 32)]
            west_a, keep_a, edge, *coming = stage(
                even, [1, 2, 3], [0, 2], wet, held,
                [
                    (back_b, sides),
                    (keep_l, [(1, 4, 12), (1, 28, 32)]),
                    (back_a, [(0, 12, 16), (0, 0, 8), (0, 24, 28)]),
                    (keep_e, [(1, 12, 16), (1, 0, 8), (1, 24, 28)]),
                    (inner[0], [(0, 16, 24)]),
                    (inner[1], [(1, 16, 24)]),
                ],
                most, f"even{pair}a", brings=params,
            )
            last = [(back_b, sides), (keep_l, [(1, 4, 12)]), (back_diag, [(0, 0, 4)]), (back_lat, [(1, 0, 4)])]
        west_a = send(west_a, 0, -1)
        west_b, up_lat, up_diag, keep_b, *more = stage(
            even, [0, 1, 3], [0], wet, held, [*last, (edge, rim)],
            [[(0, 4, 12), (0, 28, 32)], [(1, 0, 4)], [(0, 0, 4)], [(1, 4, 8)]],
            f"even{pair}b", brings=params if pair == 0 else (),
        )
        west_b = send(west_b, 0, -1)
        up_lat = send(up_lat, -1, 0)
        up_diag = send(up_diag, -1, -1)
        held = more if pair == 0 else coming
        own, other = (keep_a, [(0, 8, 32)]), (west_a, [(1, 12, 28)])
        keep_e, back_a = stage(
            odd, [1, 2], [0, 1], wet, held, [own, other], [[(0, 12, 28)], [(1, 12, 28)]], f"odd{pair}a"
        )
        back_a = send(back_a, 0, 1)
        keep_l, back_b, back_lat, back_diag, *coming = stage(
            odd, [0, 3], [0, 1], wet, held,
            [own, other, (keep_b, [(0, 4, 8)]), (west_b, [(1, 4, 12), (1, 28, 32)]), (up_lat, [(0, 32, 36)]), (up_diag, [(1, 32, 36)])],
            [[(0, 4, 12), (0, 28, 32)], [(1, 4, 12), (1, 28, 32)], [(0, 32, 36)], [(1, 32, 36)]],
            f"odd{pair}b", brings=params if odd + 1 < LAYERS else (),
        )
        back_b = send(back_b, 0, 1)
        back_lat = send(back_lat, 1, 0)
        back_diag = send(back_diag, 1, 1)
        held = coming
    parts = [
        (back_a, [(0, 12, 28)]),
        (back_b, [(0, 4, 12), (0, 28, 32)]),
        (back_diag, [(0, 0, 4)]),
        (back_lat, [(1, 0, 4)]),
        (keep_l, [(1, 4, 12), (1, 28, 32)]),
        (keep_e, [(1, 12, 28)]),
    ]
    out = pl.pallas_call(
        functools.partial(finish_kernel, [segments for _, segments in parts]),
        out_shape=jax.ShapeDtypeStruct((32, 2, 8, C), f32),
        in_specs=[VM] * len(parts),
        out_specs=HBM,
        scratch_shapes=[pltpu.SemaphoreType.DMA((8,))],
        compiler_params=pltpu.CompilerParams(vmem_limit_bytes=4 << 20),
        name="finish",
    )(*[array for array, _ in parts])
    return out.reshape(32, 16, C)


def solution(mesh):
    in_specs = (P("lat", "lon", None), P(), P(), P(), P(), P(), P(), P(), P())
    out_specs = P("lat", "lon", None)
    return jax.shard_map(local, mesh=mesh, in_specs=in_specs, out_specs=out_specs, check_vma=False)
```

```python
import functools

import jax
import jax.numpy as jnp
from jax import lax
from jax.experimental import pallas as pl
from jax.experimental.pallas import tpu as pltpu
from jax.sharding import PartitionSpec as P

C = 384
HEADS = 12
FFN = 1536
TOK = 128
LANES = 128
GROUP = 4
HEAD = 32
LAYERS = 4
CHUNK = 256
norm_eps = 1e-05
mask_fill = -1000000000.0
ERF_POLY = (
    0.7978275160691982,
    0.03647005390043865,
    -0.00012554234498973965,
    -3.0455015643046705e-05,
    1.1119467340375738e-06,
)
f32 = jnp.float32
bf16 = jnp.bfloat16
HBM = pl.BlockSpec(memory_space=pltpu.HBM)


def gelu(x):
    rounded = x.astype(bf16)
    square = rounded * rounded
    poly = bf16(ERF_POLY[-1])
    for factor in ERF_POLY[-2::-1]:
        poly = poly * square + bf16(factor)
    half = 0.5 * x
    return half + half * jnp.tanh((rounded * poly).astype(f32))


def layer_norm(x, gain):
    center = jnp.mean(x, axis=-1, keepdims=True)
    away = x - center
    spread = jnp.mean(away * away, axis=-1, keepdims=True)
    return (away * lax.rsqrt(spread + norm_eps) * gain).astype(bf16)


def attend(q, k, v, bias_ref, group, masked):
    owner = lax.broadcasted_iota(jnp.int32, (TOK, LANES), 1) // HEAD
    zero = jnp.zeros((TOK, LANES), bf16)
    one = jnp.ones((TOK, LANES), bf16)
    keys = jnp.concatenate([jnp.where(owner == h, k, zero) for h in range(GROUP)], axis=0)
    scores = lax.dot_general(q, keys, (((1,), (1,)), ((), ())), preferred_element_type=f32)
    parts = []
    for h in range(GROUP):
        s = scores[:, h * TOK : (h + 1) * TOK] * HEAD ** (-0.5) + bias_ref[group * GROUP + h]
        if masked is not None:
            s = jnp.where(masked, mask_fill, s)
        parts.append(jnp.exp(s - jnp.max(s, axis=-1, keepdims=True)).astype(bf16))
    weights = jnp.concatenate(parts, axis=1)
    values = jnp.concatenate(
        [
            jnp.concatenate([jnp.where(owner == h, v, zero), jnp.where(owner == h, one, zero)], axis=1)
            for h in range(GROUP)
        ],
        axis=0,
    )
    both = jnp.dot(weights, values, preferred_element_type=f32)
    return (both[:, :LANES] / both[:, LANES:]).astype(bf16)


class Buffers:
    pass


def run_windows(b, ids, masked, ready):
    count = len(ids)
    rows = count * TOK
    x = jnp.concatenate([b.xs[pl.ds(i * 8, 8)].reshape(TOK, C) for i in ids], axis=0)
    ready("ga", "wq")
    b.qkv[:rows] = jnp.dot(layer_norm(x, b.ga[...]), b.wq[...], preferred_element_type=f32).astype(bf16)
    ready("bias")
    for w in range(count):
        span = slice(w * TOK, (w + 1) * TOK)
        hide = None
        if masked is not None:
            low_q = lax.broadcasted_iota(jnp.int32, (TOK, TOK), 0) >= TOK // 2
            low_k = lax.broadcasted_iota(jnp.int32, (TOK, TOK), 1) >= TOK // 2
            hide = jnp.logical_and(low_q != low_k, masked[w])
        for g in range(HEADS // GROUP):
            at = g * LANES
            b.att[span, at : at + LANES] = attend(
                b.qkv[span, at : at + LANES],
                b.qkv[span, C + at : C + at + LANES],
                b.qkv[span, 2 * C + at : 2 * C + at + LANES],
                b.bias,
                g,
                hide,
            )
    ready("wo", "gm")
    resid = x + jnp.dot(b.att[:rows], b.wo[...], preferred_element_type=f32)
    mlp_in = layer_norm(resid, b.gm[...])
    total = resid
    ready("wu", "wd")
    for f in range(0, FFN, CHUNK):
        up = jnp.dot(mlp_in, b.wu[:, f : f + CHUNK], preferred_element_type=f32)
        total = total + jnp.dot(gelu(up).astype(bf16), b.wd[f : f + CHUNK, :], preferred_element_type=f32)
    for w, i in enumerate(ids):
        b.xs[pl.ds(i * 8, 8)] = total[w * TOK : (w + 1) * TOK].reshape(8, 2, 8, C)


NAMES = ("ga", "wq", "bias", "wo", "gm", "wu", "wd")


def start_loads(params, held, layer, sem, names):
    copies = {}
    for n, name in enumerate(NAMES):
        if name not in names:
            continue
        source = params[n]
        part = source.at[pl.ds(layer, 1)] if len(source.shape) == 2 else source.at[layer]
        copies[name] = pltpu.make_async_copy(part, held[n], sem.at[n])
        copies[name].start()
    return copies


def held_shapes(params):
    return [jax.ShapeDtypeStruct((1, C) if p.ndim == 2 else p.shape[1:], p.dtype) for p in params]


VM = pl.BlockSpec(memory_space=pltpu.VMEM)


def overlaps(windows, base, segments):
    pieces = []
    for slot, window in enumerate(windows):
        top = base + 8 * window
        at = 0
        for half, low, high in segments:
            first, last = max(top, low), min(top + 8, high)
            if first < last:
                pieces.append((slot, first - top, at + first - low, last - first, half))
            at += high - low
    return pieces


def stage_kernel(layer, windows, work, sources, sinks, opening, brings, *refs):
    refs = list(refs)

    def take(count):
        got, refs[:count] = refs[:count], []
        return got

    (wet,) = take(1)
    given = take(7)
    ins = take(len(sources))
    coming = take(7) if brings else []
    outs = take(len(sinks))
    row = wet
    held = given
    if opening:
        held = take(7)
        row, rest = take(2)
    arrived = take(7) if brings else []
    xs, qkv, att, s_wet, sem, in_sem = refs
    lat = lax.axis_index("lat")
    lon = lax.axis_index("lon")
    bands = lax.axis_size("lat")
    base = 4 if layer % 2 == 1 else 0
    pending = {}
    waits = []
    if opening:
        flags = pltpu.make_async_copy(wet, s_wet, in_sem.at[0])
        block = pltpu.make_async_copy(ins[0].at[8:32], xs, in_sem.at[1])
        others = pltpu.make_async_copy(ins[0].at[0:8], rest, in_sem.at[2])
        flags.start()
        block.start()
        pending = start_loads(given, held, layer, sem, ("ga", "wq"))
        flags.wait()
        pending |= start_loads(given, held, layer, sem, ("bias", "wo", "gm", "wu", "wd"))
        others.start()
        waits.append(others)
        which_layer = lax.broadcasted_iota(jnp.int32, (8, LANES), 0)
        which_window = lax.broadcasted_iota(jnp.int32, (8, LANES), 1)
        mine = jnp.zeros((8, LANES), jnp.int32)
        for n in range(LAYERS):
            for j in range(4):
                here = jnp.logical_and(which_layer == n, which_window == j)
                mine = jnp.where(here, s_wet[n, lon, lat * 4 + j], mine)
        row[...] = mine
        is_wet = [s_wet[layer, lon, lat * 4 + windows[slot]] == 1 for slot in work]
        block.wait()
    else:
        waits = list(start_loads(coming, arrived, layer + 1, sem, NAMES).values()) if brings else []
        for source, segments in zip(ins, sources):
            for slot, to, at, count, half in overlaps(windows, base, segments):
                if half is None:
                    xs[slot * 8 + to : slot * 8 + to + count] = source[at : at + count]
                else:
                    xs[slot * 8 + to : slot * 8 + to + count, half] = source[at : at + count]
        is_wet = [row[layer, windows[slot]] == 1 for slot in work]

    def ready(*names):
        for name in names:
            if name in pending:
                pending[name].wait()

    b = Buffers()
    b.xs, b.qkv, b.att = xs, qkv, att
    b.ga, b.wq, b.bias, b.wo, b.gm, b.wu, b.wd = held
    first_slot = jnp.int32(work[-1])
    last_slot = jnp.int32(work[0])
    count = jnp.int32(0)
    for slot, flag in reversed(list(zip(work, is_wet))):
        first_slot = jnp.where(flag, slot, first_slot)
    for slot, flag in zip(work, is_wet):
        last_slot = jnp.where(flag, slot, last_slot)
        count += flag.astype(jnp.int32)
    masking = base == 4 and 3 in [windows[slot] for slot in work]

    def run(ids):
        masked = None
        if masking:
            masked = [jnp.logical_and(lat == bands - 1, i == windows.index(3)) for i in ids]
        run_windows(b, ids, masked, ready)

    if len(work) > 1:

        @pl.when(count >= 2)
        def _():
            run([first_slot, last_slot if len(work) == 2 else jnp.where(count == 3, work[1], last_slot)])
            if opening:
                pending_before = dict(pending)
                pending.clear()
                single = count == 3

                @pl.when(single)
                def _():
                    run([jnp.int32(work[2])])

                pending.update(pending_before)

    @pl.when(count == 1)
    def _():
        run([first_slot])

    if opening:

        @pl.when(count == 0)
        def _():
            ready(*NAMES)

    for target, segments in zip(outs, sinks):
        for slot, at, to, rows, half in overlaps(windows, base, segments):
            target[to : to + rows] = xs[slot * 8 + at : slot * 8 + at + rows, half]
    for c in waits:
        c.wait()


def stage(layer, windows, work, wet, held, sources, sinks, name, opening=False, brings=()):
    ins = [array for array, _ in sources]
    shapes = [jax.ShapeDtypeStruct((sum(h - l for _, l, h in segments), 8, C), f32) for segments in sinks]
    kernel = functools.partial(
        stage_kernel, layer, windows, work, [segments for _, segments in sources], sinks, opening, bool(brings)
    )
    extra = []
    if opening:
        extra = held_shapes(held)
        extra += [jax.ShapeDtypeStruct((8, LANES), jnp.int32), jax.ShapeDtypeStruct((8, 2, 8, C), f32)]
    extra += held_shapes(brings)
    place = HBM if opening else VM
    cost = 200_000_000 if name[-1] == "e" or layer % 2 == 1 and 1 in windows else 4_000_000_000
    rows = min(2, len(work)) * TOK
    return pl.pallas_call(
        kernel,
        out_shape=shapes + extra,
        in_specs=[place] * (8 + len(ins)) + [HBM] * len(brings),
        out_specs=[VM] * len(shapes + extra),
        scratch_shapes=[
            pltpu.VMEM((8 * len(windows), 2, 8, C), f32),
            pltpu.VMEM((rows, 3 * C), bf16),
            pltpu.VMEM((rows, C), bf16),
            pltpu.SMEM((LAYERS, 16, 32), jnp.int32),
            pltpu.SemaphoreType.DMA((7,)),
            pltpu.SemaphoreType.DMA((3,)),
        ],
        compiler_params=pltpu.CompilerParams(vmem_limit_bytes=24 << 20),
        cost_estimate=pl.CostEstimate(flops=cost, bytes_accessed=100_000, transcendentals=0),
        name=name,
    )(wet, *held, *ins, *brings)


def send(block, d_lat, d_lon):
    n_lat, n_lon = lax.axis_size("lat"), lax.axis_size("lon")
    route = [
        (a * n_lon + b, (a + d_lat) % n_lat * n_lon + (b + d_lon) % n_lon)
        for a in range(n_lat)
        for b in range(n_lon)
    ]
    return lax.ppermute(block, ("lat", "lon"), route)


def relay_kernel(*refs):
    del refs


def relay(*arrays):
    return pl.pallas_call(
        relay_kernel,
        out_shape=[jax.ShapeDtypeStruct(a.shape, a.dtype) for a in arrays],
        in_specs=[VM] * len(arrays),
        out_specs=[VM] * len(arrays),
        input_output_aliases={i: i for i in range(len(arrays))},
        compiler_params=pltpu.CompilerParams(vmem_limit_bytes=4 << 20),
        cost_estimate=pl.CostEstimate(flops=8_000_000_000, bytes_accessed=6_000_000, transcendentals=0),
        name="relay",
    )(*arrays)


def finish_kernel(placed, *refs):
    ins, out, sem = refs[: len(placed)], refs[len(placed)], refs[len(placed) + 1]
    copies = []
    for source, segments in zip(ins, placed):
        at = 0
        for half, low, high in segments:
            part = source.at[at : at + high - low]
            copies.append(pltpu.make_async_copy(part, out.at[low:high, half], sem.at[len(copies)]))
            copies[-1].start()
            at += high - low
    for c in copies:
        c.wait()


def local(tokens, wet_flags, ln_attn, w_qkv, w_out, pos_bias, ln_mlp, w_up, w_down):
    params = [ln_attn, w_qkv, pos_bias, w_out, ln_mlp, w_up, w_down]
    wet = wet_flags.transpose(0, 2, 1)
    grid = tokens.reshape(32, 2, 8, C)
    params = [pltpu.with_memory_space_constraint(p, pltpu.HBM) for p in params]
    wet = pltpu.with_memory_space_constraint(wet, pltpu.HBM)
    grid = pltpu.with_memory_space_constraint(grid, pltpu.HBM)
    for pair in range(LAYERS // 2):
        even, odd = 2 * pair, 2 * pair + 1
        rim = [(0, 8, 12), (0, 28, 32)]
        most = [[(0, 12, 28)], [(1, 8, 32)], rim]
        if pair == 0:
            west_a, keep_a, edge, *rest = stage(
                even, [1, 2, 3], [0, 1, 2], wet, params, [(grid, [])], most, "even0a", opening=True
            )
            held, wet, last = rest[:7], rest[7], [(rest[8], [(None, 0, 8)])]
        else:
            inner = stage(
                even, [2], [0], wet, held, [(back_a, [(0, 12, 28)]), (keep_e, [(1, 12, 28)])],
                [[(0, 16, 24)], [(1, 16, 24)]], f"even{pair}e",
            )
            sides = [(0, 4, 12), (0, 28, 32)]
            west_a, keep_a, edge, *coming = stage(
                even, [1, 2, 3], [0, 2], wet, held,
                [
                    (back_b, sides),
                    (keep_l, [(1, 4, 12), (1, 28, 32)]),
                    (back_a, [(0, 12, 16), (0, 0, 8), (0, 24, 28)]),
                    (keep_e, [(1, 12, 16), (1, 0, 8), (1, 24, 28)]),
                    (inner[0], [(0, 16, 24)]),
                    (inner[1], [(1, 16, 24)]),
                ],
                most, f"even{pair}a", brings=params,
            )
            last = [(back_b, sides), (keep_l, [(1, 4, 12)]), (back_diag, [(0, 0, 4)]), (back_lat, [(1, 0, 4)])]
        west_a = send(west_a, 0, -1)
        west_b, up_lat, up_diag, keep_b, *more = stage(
            even, [0, 1, 3], [0], wet, held, [*last, (edge, rim)],
            [[(0, 4, 12), (0, 28, 32)], [(1, 0, 4)], [(0, 0, 4)], [(1, 4, 8)]],
            f"even{pair}b", brings=params if pair == 0 else (),
        )
        west_b = send(west_b, 0, -1)
        up_lat = send(up_lat, -1, 0)
        up_diag = send(up_diag, -1, -1)
        held = more if pair == 0 else coming
        own, other = (keep_a, [(0, 8, 32)]), (west_a, [(1, 12, 28)])
        keep_e, back_a = stage(
            odd, [1, 2], [0, 1], wet, held, [own, other], [[(0, 12, 28)], [(1, 12, 28)]], f"odd{pair}a"
        )
        back_a = send(back_a, 0, 1)
        keep_l, back_b, back_lat, back_diag, *coming = stage(
            odd, [0, 3], [0, 1], wet, held,
            [own, other, (keep_b, [(0, 4, 8)]), (west_b, [(1, 4, 12), (1, 28, 32)]), (up_lat, [(0, 32, 36)]), (up_diag, [(1, 32, 36)])],
            [[(0, 4, 12), (0, 28, 32)], [(1, 4, 12), (1, 28, 32)], [(0, 32, 36)], [(1, 32, 36)]],
            f"odd{pair}b", brings=params if odd + 1 < LAYERS else (),
        )
        back_b = send(back_b, 0, 1)
        back_lat = send(back_lat, 1, 0)
        back_diag = send(back_diag, 1, 1)
        held = coming
    back_lat, back_diag = relay(back_lat, back_diag)
    parts = [
        (back_a, [(0, 12, 28)]),
        (back_b, [(0, 4, 12), (0, 28, 32)]),
        (back_diag, [(0, 0, 4)]),
        (back_lat, [(1, 0, 4)]),
        (keep_l, [(1, 4, 12), (1, 28, 32)]),
        (keep_e, [(1, 12, 28)]),
    ]
    out = pl.pallas_call(
        functools.partial(finish_kernel, [segments for _, segments in parts]),
        out_shape=jax.ShapeDtypeStruct((32, 2, 8, C), f32),
        in_specs=[VM] * len(parts),
        out_specs=HBM,
        scratch_shapes=[pltpu.SemaphoreType.DMA((8,))],
        compiler_params=pltpu.CompilerParams(vmem_limit_bytes=4 << 20),
        name="finish",
    )(*[array for array, _ in parts])
    return out.reshape(32, 16, C)


def solution(mesh):
    in_specs = (P("lat", "lon", None), P(), P(), P(), P(), P(), P(), P(), P())
    out_specs = P("lat", "lon", None)
    return jax.shard_map(local, mesh=mesh, in_specs=in_specs, out_specs=out_specs, check_vma=False)
```

```python
import functools

import jax
import jax.numpy as jnp
from jax import lax
from jax.experimental import pallas as pl
from jax.experimental.pallas import tpu as pltpu
from jax.sharding import PartitionSpec as P

C = 384
HEADS = 12
FFN = 1536
TOK = 128
LANES = 128
GROUP = 4
HEAD = 32
LAYERS = 4
CHUNK = 256
norm_eps = 1e-05
mask_fill = -1000000000.0
ERF_POLY = (
    0.7978275160691982,
    0.03647005390043865,
    -0.00012554234498973965,
    -3.0455015643046705e-05,
    1.1119467340375738e-06,
)
f32 = jnp.float32
bf16 = jnp.bfloat16
HBM = pl.BlockSpec(memory_space=pltpu.HBM)


def gelu(x):
    rounded = x.astype(bf16)
    square = rounded * rounded
    poly = bf16(ERF_POLY[-1])
    for factor in ERF_POLY[-2::-1]:
        poly = poly * square + bf16(factor)
    half = 0.5 * x
    return half + half * jnp.tanh((rounded * poly).astype(f32))


def layer_norm(x, gain):
    center = jnp.mean(x, axis=-1, keepdims=True)
    away = x - center
    spread = jnp.mean(away * away, axis=-1, keepdims=True)
    return (away * lax.rsqrt(spread + norm_eps) * gain).astype(bf16)


def attend(q, k, v, bias_ref, group, masked):
    owner = lax.broadcasted_iota(jnp.int32, (TOK, LANES), 1) // HEAD
    zero = jnp.zeros((TOK, LANES), bf16)
    one = jnp.ones((TOK, LANES), bf16)
    keys = jnp.concatenate([jnp.where(owner == h, k, zero) for h in range(GROUP)], axis=0)
    scores = lax.dot_general(q, keys, (((1,), (1,)), ((), ())), preferred_element_type=f32)
    parts = []
    for h in range(GROUP):
        s = scores[:, h * TOK : (h + 1) * TOK] * HEAD ** (-0.5) + bias_ref[group * GROUP + h]
        if masked is not None:
            s = jnp.where(masked, mask_fill, s)
        parts.append(jnp.exp(s - jnp.max(s, axis=-1, keepdims=True)).astype(bf16))
    weights = jnp.concatenate(parts, axis=1)
    values = jnp.concatenate(
        [
            jnp.concatenate([jnp.where(owner == h, v, zero), jnp.where(owner == h, one, zero)], axis=1)
            for h in range(GROUP)
        ],
        axis=0,
    )
    both = jnp.dot(weights, values, preferred_element_type=f32)
    return (both[:, :LANES] / both[:, LANES:]).astype(bf16)


class Buffers:
    pass


def run_windows(b, ids, masked, ready):
    count = len(ids)
    rows = count * TOK
    x = jnp.concatenate([b.xs[pl.ds(i * 8, 8)].reshape(TOK, C) for i in ids], axis=0)
    ready("ga", "wq")
    b.qkv[:rows] = jnp.dot(layer_norm(x, b.ga[...]), b.wq[...], preferred_element_type=f32).astype(bf16)
    ready("bias")
    for w in range(count):
        span = slice(w * TOK, (w + 1) * TOK)
        hide = None
        if masked is not None:
            low_q = lax.broadcasted_iota(jnp.int32, (TOK, TOK), 0) >= TOK // 2
            low_k = lax.broadcasted_iota(jnp.int32, (TOK, TOK), 1) >= TOK // 2
            hide = jnp.logical_and(low_q != low_k, masked[w])
        for g in range(HEADS // GROUP):
            at = g * LANES
            b.att[span, at : at + LANES] = attend(
                b.qkv[span, at : at + LANES],
                b.qkv[span, C + at : C + at + LANES],
                b.qkv[span, 2 * C + at : 2 * C + at + LANES],
                b.bias,
                g,
                hide,
            )
    ready("wo", "gm")
    resid = x + jnp.dot(b.att[:rows], b.wo[...], preferred_element_type=f32)
    mlp_in = layer_norm(resid, b.gm[...])
    total = resid
    ready("wu", "wd")
    for f in range(0, FFN, CHUNK):
        up = jnp.dot(mlp_in, b.wu[:, f : f + CHUNK], preferred_element_type=f32)
        total = total + jnp.dot(gelu(up).astype(bf16), b.wd[f : f + CHUNK, :], preferred_element_type=f32)
    for w, i in enumerate(ids):
        b.xs[pl.ds(i * 8, 8)] = total[w * TOK : (w + 1) * TOK].reshape(8, 2, 8, C)


NAMES = ("ga", "wq", "bias", "wo", "gm", "wu", "wd")


def start_loads(params, held, layer, sem, names):
    copies = {}
    for n, name in enumerate(NAMES):
        if name not in names:
            continue
        source = params[n]
        part = source.at[pl.ds(layer, 1)] if len(source.shape) == 2 else source.at[layer]
        copies[name] = pltpu.make_async_copy(part, held[n], sem.at[n])
        copies[name].start()
    return copies


def held_shapes(params):
    return [jax.ShapeDtypeStruct((1, C) if p.ndim == 2 else p.shape[1:], p.dtype) for p in params]


VM = pl.BlockSpec(memory_space=pltpu.VMEM)


def overlaps(windows, base, segments):
    pieces = []
    for slot, window in enumerate(windows):
        top = base + 8 * window
        at = 0
        for half, low, high in segments:
            first, last = max(top, low), min(top + 8, high)
            if first < last:
                pieces.append((slot, first - top, at + first - low, last - first, half))
            at += high - low
    return pieces


def stage_kernel(layer, windows, work, sources, sinks, opening, brings, *refs):
    refs = list(refs)

    def take(count):
        got, refs[:count] = refs[:count], []
        return got

    (wet,) = take(1)
    given = take(7)
    ins = take(len(sources))
    coming = take(7) if brings else []
    outs = take(len(sinks))
    row = wet
    held = given
    if opening:
        held = take(7)
        row, rest = take(2)
    arrived = take(7) if brings else []
    xs, qkv, att, s_wet, sem, in_sem = refs
    lat = lax.axis_index("lat")
    lon = lax.axis_index("lon")
    bands = lax.axis_size("lat")
    base = 4 if layer % 2 == 1 else 0
    pending = {}
    waits = []
    if opening:
        flags = pltpu.make_async_copy(wet, s_wet, in_sem.at[0])
        block = pltpu.make_async_copy(ins[0].at[8:32], xs, in_sem.at[1])
        others = pltpu.make_async_copy(ins[0].at[0:8], rest, in_sem.at[2])
        flags.start()
        block.start()
        pending = start_loads(given, held, layer, sem, ("ga", "wq"))
        flags.wait()
        pending |= start_loads(given, held, layer, sem, ("bias", "wo", "gm", "wu", "wd"))
        others.start()
        waits.append(others)
        which_layer = lax.broadcasted_iota(jnp.int32, (8, LANES), 0)
        which_window = lax.broadcasted_iota(jnp.int32, (8, LANES), 1)
        mine = jnp.zeros((8, LANES), jnp.int32)
        for n in range(LAYERS):
            for j in range(4):
                here = jnp.logical_and(which_layer == n, which_window == j)
                mine = jnp.where(here, s_wet[n, lon, lat * 4 + j], mine)
        row[...] = mine
        is_wet = [s_wet[layer, lon, lat * 4 + windows[slot]] == 1 for slot in work]
        block.wait()
    else:
        waits = list(start_loads(coming, arrived, layer + 1, sem, NAMES).values()) if brings else []
        for source, segments in zip(ins, sources):
            for slot, to, at, count, half in overlaps(windows, base, segments):
                if half is None:
                    xs[slot * 8 + to : slot * 8 + to + count] = source[at : at + count]
                else:
                    xs[slot * 8 + to : slot * 8 + to + count, half] = source[at : at + count]
        is_wet = [row[layer, windows[slot]] == 1 for slot in work]

    def ready(*names):
        for name in names:
            if name in pending:
                pending[name].wait()

    b = Buffers()
    b.xs, b.qkv, b.att = xs, qkv, att
    b.ga, b.wq, b.bias, b.wo, b.gm, b.wu, b.wd = held
    first_slot = jnp.int32(work[-1])
    last_slot = jnp.int32(work[0])
    count = jnp.int32(0)
    for slot, flag in reversed(list(zip(work, is_wet))):
        first_slot = jnp.where(flag, slot, first_slot)
    for slot, flag in zip(work, is_wet):
        last_slot = jnp.where(flag, slot, last_slot)
        count += flag.astype(jnp.int32)
    masking = base == 4 and 3 in [windows[slot] for slot in work]

    def run(ids):
        masked = None
        if masking:
            masked = [jnp.logical_and(lat == bands - 1, i == windows.index(3)) for i in ids]
        run_windows(b, ids, masked, ready)

    if len(work) > 1:

        @pl.when(count >= 2)
        def _():
            run([first_slot, last_slot if len(work) == 2 else jnp.where(count == 3, work[1], last_slot)])
            if opening:
                pending_before = dict(pending)
                pending.clear()
                single = count == 3

                @pl.when(single)
                def _():
                    run([jnp.int32(work[2])])

                pending.update(pending_before)

    @pl.when(count == 1)
    def _():
        run([first_slot])

    if opening:

        @pl.when(count == 0)
        def _():
            ready(*NAMES)

    for target, segments in zip(outs, sinks):
        for slot, at, to, rows, half in overlaps(windows, base, segments):
            target[to : to + rows] = xs[slot * 8 + at : slot * 8 + at + rows, half]
    for c in waits:
        c.wait()


def stage(layer, windows, work, wet, held, sources, sinks, name, opening=False, brings=()):
    ins = [array for array, _ in sources]
    shapes = [jax.ShapeDtypeStruct((sum(h - l for _, l, h in segments), 8, C), f32) for segments in sinks]
    kernel = functools.partial(
        stage_kernel, layer, windows, work, [segments for _, segments in sources], sinks, opening, bool(brings)
    )
    extra = []
    if opening:
        extra = held_shapes(held)
        extra += [jax.ShapeDtypeStruct((8, LANES), jnp.int32), jax.ShapeDtypeStruct((8, 2, 8, C), f32)]
    extra += held_shapes(brings)
    place = HBM if opening else VM
    cost = 200_000_000 if name[-1] == "e" or layer % 2 == 1 and 1 in windows else 4_000_000_000
    rows = min(2, len(work)) * TOK
    return pl.pallas_call(
        kernel,
        out_shape=shapes + extra,
        in_specs=[place] * (8 + len(ins)) + [HBM] * len(brings),
        out_specs=[VM] * len(shapes + extra),
        scratch_shapes=[
            pltpu.VMEM((8 * len(windows), 2, 8, C), f32),
            pltpu.VMEM((rows, 3 * C), bf16),
            pltpu.VMEM((rows, C), bf16),
            pltpu.SMEM((LAYERS, 16, 32), jnp.int32),
            pltpu.SemaphoreType.DMA((7,)),
            pltpu.SemaphoreType.DMA((3,)),
        ],
        compiler_params=pltpu.CompilerParams(vmem_limit_bytes=24 << 20),
        cost_estimate=pl.CostEstimate(flops=cost, bytes_accessed=100_000, transcendentals=0),
        name=name,
    )(wet, *held, *ins, *brings)


def send(block, d_lat, d_lon):
    n_lat, n_lon = lax.axis_size("lat"), lax.axis_size("lon")
    route = [
        (a * n_lon + b, (a + d_lat) % n_lat * n_lon + (b + d_lon) % n_lon)
        for a in range(n_lat)
        for b in range(n_lon)
    ]
    return lax.ppermute(block, ("lat", "lon"), route)


def relay_kernel(*refs):
    del refs


def relay(*arrays):
    return pl.pallas_call(
        relay_kernel,
        out_shape=[jax.ShapeDtypeStruct(a.shape, a.dtype) for a in arrays],
        in_specs=[VM] * len(arrays),
        out_specs=[VM] * len(arrays),
        input_output_aliases={i: i for i in range(len(arrays))},
        compiler_params=pltpu.CompilerParams(vmem_limit_bytes=4 << 20),
        cost_estimate=pl.CostEstimate(flops=8_000_000_000, bytes_accessed=6_000_000, transcendentals=0),
        name="relay",
    )(*arrays)


def finish_kernel(placed, *refs):
    ins, out, sem = refs[: len(placed)], refs[len(placed)], refs[len(placed) + 1]
    copies = []
    for source, segments in zip(ins, placed):
        at = 0
        for half, low, high in segments:
            part = source.at[at : at + high - low]
            copies.append(pltpu.make_async_copy(part, out.at[low:high, half], sem.at[len(copies)]))
            copies[-1].start()
            at += high - low
    for c in copies:
        c.wait()


def local(tokens, wet_flags, ln_attn, w_qkv, w_out, pos_bias, ln_mlp, w_up, w_down):
    params = [ln_attn, w_qkv, pos_bias, w_out, ln_mlp, w_up, w_down]
    wet = wet_flags.transpose(0, 2, 1)
    grid = tokens.reshape(32, 2, 8, C)
    params = [pltpu.with_memory_space_constraint(p, pltpu.HBM) for p in params]
    wet = pltpu.with_memory_space_constraint(wet, pltpu.HBM)
    grid = pltpu.with_memory_space_constraint(grid, pltpu.HBM)
    for pair in range(LAYERS // 2):
        even, odd = 2 * pair, 2 * pair + 1
        rim = [(0, 8, 12), (0, 28, 32)]
        most = [[(0, 12, 28)], [(1, 8, 32)], rim]
        if pair == 0:
            west_a, keep_a, edge, *rest = stage(
                even, [1, 2, 3], [0, 1, 2], wet, params, [(grid, [])], most, "even0a", opening=True
            )
            held, wet, last = rest[:7], rest[7], [(rest[8], [(None, 0, 8)])]
        else:
            inner = stage(
                even, [2], [0], wet, held, [(back_a, [(0, 12, 28)]), (keep_e, [(1, 12, 28)])],
                [[(0, 16, 24)], [(1, 16, 24)]], f"even{pair}e",
            )
            sides = [(0, 4, 12), (0, 28, 32)]
            west_a, keep_a, edge, *coming = stage(
                even, [1, 2, 3], [0, 2], wet, held,
                [
                    (back_b, sides),
                    (keep_l, [(1, 4, 12), (1, 28, 32)]),
                    (back_a, [(0, 12, 16), (0, 0, 8), (0, 24, 28)]),
                    (keep_e, [(1, 12, 16), (1, 0, 8), (1, 24, 28)]),
                    (inner[0], [(0, 16, 24)]),
                    (inner[1], [(1, 16, 24)]),
                ],
                most, f"even{pair}a", brings=params,
            )
            last = [(back_b, sides), (keep_l, [(1, 4, 12)]), (back_diag, [(0, 0, 4)]), (back_lat, [(1, 0, 4)])]
        west_a = send(west_a, 0, -1)
        west_b, up_lat, up_diag, keep_b, *more = stage(
            even, [0, 1, 3], [0], wet, held, [*last, (edge, rim)],
            [[(0, 4, 12), (0, 28, 32)], [(1, 0, 4)], [(0, 0, 4)], [(1, 4, 8)]],
            f"even{pair}b", brings=params if pair == 0 else (),
        )
        west_b = send(west_b, 0, -1)
        up_lat = send(up_lat, -1, 0)
        up_diag = send(up_diag, -1, -1)
        held = more if pair == 0 else coming
        own, other = (keep_a, [(0, 8, 32)]), (west_a, [(1, 12, 28)])
        keep_e, back_a = stage(
            odd, [1, 2], [0, 1], wet, held, [own, other], [[(0, 12, 28)], [(1, 12, 28)]], f"odd{pair}a"
        )
        back_a = send(back_a, 0, 1)
        keep_l, back_b, back_lat, back_diag, *coming = stage(
            odd, [0, 3], [0, 1], wet, held,
            [own, other, (keep_b, [(0, 4, 8)]), (west_b, [(1, 4, 12), (1, 28, 32)]), (up_lat, [(0, 32, 36)]), (up_diag, [(1, 32, 36)]), (keep_e, [])],
            [[(0, 4, 12), (0, 28, 32)], [(1, 4, 12), (1, 28, 32)], [(0, 32, 36)], [(1, 32, 36)]],
            f"odd{pair}b", brings=params if odd + 1 < LAYERS else (),
        )
        back_b = send(back_b, 0, 1)
        back_lat = send(back_lat, 1, 0)
        back_diag = send(back_diag, 1, 1)
        held = coming
    back_a, back_lat, back_diag = relay(back_a, back_lat, back_diag)
    parts = [
        (back_a, [(0, 12, 28)]),
        (back_b, [(0, 4, 12), (0, 28, 32)]),
        (back_diag, [(0, 0, 4)]),
        (back_lat, [(1, 0, 4)]),
        (keep_l, [(1, 4, 12), (1, 28, 32)]),
        (keep_e, [(1, 12, 28)]),
    ]
    out = pl.pallas_call(
        functools.partial(finish_kernel, [segments for _, segments in parts]),
        out_shape=jax.ShapeDtypeStruct((32, 2, 8, C), f32),
        in_specs=[VM] * len(parts),
        out_specs=HBM,
        scratch_shapes=[pltpu.SemaphoreType.DMA((8,))],
        compiler_params=pltpu.CompilerParams(vmem_limit_bytes=4 << 20),
        name="finish",
    )(*[array for array, _ in parts])
    return out.reshape(32, 16, C)


def solution(mesh):
    in_specs = (P("lat", "lon", None), P(), P(), P(), P(), P(), P(), P(), P())
    out_specs = P("lat", "lon", None)
    return jax.shard_map(local, mesh=mesh, in_specs=in_specs, out_specs=out_specs, check_vma=False)
```

```python
import functools

import jax
import jax.numpy as jnp
from jax import lax
from jax.experimental import pallas as pl
from jax.experimental.pallas import tpu as pltpu
from jax.sharding import PartitionSpec as P

C = 384
HEADS = 12
FFN = 1536
TOK = 128
LANES = 128
GROUP = 4
HEAD = 32
LAYERS = 4
CHUNK = 256
norm_eps = 1e-05
mask_fill = -1000000000.0
ERF_POLY = (
    0.7978275160691982,
    0.03647005390043865,
    -0.00012554234498973965,
    -3.0455015643046705e-05,
    1.1119467340375738e-06,
)
f32 = jnp.float32
bf16 = jnp.bfloat16
HBM = pl.BlockSpec(memory_space=pltpu.HBM)


def gelu(x):
    rounded = x.astype(bf16)
    square = rounded * rounded
    poly = bf16(ERF_POLY[-1])
    for factor in ERF_POLY[-2::-1]:
        poly = poly * square + bf16(factor)
    half = 0.5 * x
    return half + half * jnp.tanh((rounded * poly).astype(f32))


def layer_norm(x, gain):
    center = jnp.mean(x, axis=-1, keepdims=True)
    away = x - center
    spread = jnp.mean(away * away, axis=-1, keepdims=True)
    return (away * lax.rsqrt(spread + norm_eps) * gain).astype(bf16)


def attend(q, k, v, bias_ref, group, masked):
    owner = lax.broadcasted_iota(jnp.int32, (TOK, LANES), 1) // HEAD
    zero = jnp.zeros((TOK, LANES), bf16)
    one = jnp.ones((TOK, LANES), bf16)
    keys = jnp.concatenate([jnp.where(owner == h, k, zero) for h in range(GROUP)], axis=0)
    scores = lax.dot_general(q, keys, (((1,), (1,)), ((), ())), preferred_element_type=f32)
    parts = []
    for h in range(GROUP):
        s = scores[:, h * TOK : (h + 1) * TOK] * HEAD ** (-0.5) + bias_ref[group * GROUP + h]
        if masked is not None:
            s = jnp.where(masked, mask_fill, s)
        parts.append(jnp.exp(s - jnp.max(s, axis=-1, keepdims=True)).astype(bf16))
    weights = jnp.concatenate(parts, axis=1)
    values = jnp.concatenate(
        [
            jnp.concatenate([jnp.where(owner == h, v, zero), jnp.where(owner == h, one, zero)], axis=1)
            for h in range(GROUP)
        ],
        axis=0,
    )
    both = jnp.dot(weights, values, preferred_element_type=f32)
    return (both[:, :LANES] / both[:, LANES:]).astype(bf16)


class Buffers:
    pass


def run_windows(b, ids, masked, ready):
    count = len(ids)
    rows = count * TOK
    x = jnp.concatenate([b.xs[pl.ds(i * 8, 8)].reshape(TOK, C) for i in ids], axis=0)
    ready("ga", "wq")
    b.qkv[:rows] = jnp.dot(layer_norm(x, b.ga[...]), b.wq[...], preferred_element_type=f32).astype(bf16)
    ready("bias")
    for w in range(count):
        span = slice(w * TOK, (w + 1) * TOK)
        hide = None
        if masked is not None:
            low_q = lax.broadcasted_iota(jnp.int32, (TOK, TOK), 0) >= TOK // 2
            low_k = lax.broadcasted_iota(jnp.int32, (TOK, TOK), 1) >= TOK // 2
            hide = jnp.logical_and(low_q != low_k, masked[w])
        for g in range(HEADS // GROUP):
            at = g * LANES
            b.att[span, at : at + LANES] = attend(
                b.qkv[span, at : at + LANES],
                b.qkv[span, C + at : C + at + LANES],
                b.qkv[span, 2 * C + at : 2 * C + at + LANES],
                b.bias,
                g,
                hide,
            )
    ready("wo", "gm")
    resid = x + jnp.dot(b.att[:rows], b.wo[...], preferred_element_type=f32)
    mlp_in = layer_norm(resid, b.gm[...])
    total = resid
    ready("wu", "wd")
    for f in range(0, FFN, CHUNK):
        up = jnp.dot(mlp_in, b.wu[:, f : f + CHUNK], preferred_element_type=f32)
        total = total + jnp.dot(gelu(up).astype(bf16), b.wd[f : f + CHUNK, :], preferred_element_type=f32)
    for w, i in enumerate(ids):
        b.xs[pl.ds(i * 8, 8)] = total[w * TOK : (w + 1) * TOK].reshape(8, 2, 8, C)


NAMES = ("ga", "wq", "bias", "wo", "gm", "wu", "wd")


def start_loads(params, held, layer, sem, names):
    copies = {}
    for n, name in enumerate(NAMES):
        if name not in names:
            continue
        source = params[n]
        part = source.at[pl.ds(layer, 1)] if len(source.shape) == 2 else source.at[layer]
        copies[name] = pltpu.make_async_copy(part, held[n], sem.at[n])
        copies[name].start()
    return copies


def held_shapes(params):
    return [jax.ShapeDtypeStruct((1, C) if p.ndim == 2 else p.shape[1:], p.dtype) for p in params]


VM = pl.BlockSpec(memory_space=pltpu.VMEM)


def overlaps(windows, base, segments):
    pieces = []
    for slot, window in enumerate(windows):
        top = base + 8 * window
        at = 0
        for half, low, high in segments:
            first, last = max(top, low), min(top + 8, high)
            if first < last:
                pieces.append((slot, first - top, at + first - low, last - first, half))
            at += high - low
    return pieces


def stage_kernel(layer, windows, work, sources, sinks, opening, brings, *refs):
    refs = list(refs)

    def take(count):
        got, refs[:count] = refs[:count], []
        return got

    (wet,) = take(1)
    given = take(7)
    ins = take(len(sources))
    coming = take(7) if brings else []
    outs = take(len(sinks))
    row = wet
    held = given
    if opening:
        held = take(7)
        row, rest = take(2)
    arrived = take(7) if brings else []
    xs, qkv, att, s_wet, sem, in_sem = refs
    lat = lax.axis_index("lat")
    lon = lax.axis_index("lon")
    bands = lax.axis_size("lat")
    base = 4 if layer % 2 == 1 else 0
    pending = {}
    waits = []
    if opening:
        flags = pltpu.make_async_copy(wet, s_wet, in_sem.at[0])
        block = pltpu.make_async_copy(ins[0].at[8:32], xs, in_sem.at[1])
        others = pltpu.make_async_copy(ins[0].at[0:8], rest, in_sem.at[2])
        flags.start()
        block.start()
        pending = start_loads(given, held, layer, sem, ("ga", "wq"))
        pending |= start_loads(given, held, layer, sem, ("bias", "wo", "gm", "wu", "wd"))
        others.start()
        waits.append(others)
        flags.wait()
        which_layer = lax.broadcasted_iota(jnp.int32, (8, LANES), 0)
        which_window = lax.broadcasted_iota(jnp.int32, (8, LANES), 1)
        mine = jnp.zeros((8, LANES), jnp.int32)
        for n in range(LAYERS):
            for j in range(4):
                here = jnp.logical_and(which_layer == n, which_window == j)
                mine = jnp.where(here, s_wet[n, lon, lat * 4 + j], mine)
        row[...] = mine
        is_wet = [s_wet[layer, lon, lat * 4 + windows[slot]] == 1 for slot in work]
        block.wait()
    else:
        waits = list(start_loads(coming, arrived, layer + 1, sem, NAMES).values()) if brings else []
        for source, segments in zip(ins, sources):
            for slot, to, at, count, half in overlaps(windows, base, segments):
                if half is None:
                    xs[slot * 8 + to : slot * 8 + to + count] = source[at : at + count]
                else:
                    xs[slot * 8 + to : slot * 8 + to + count, half] = source[at : at + count]
        is_wet = [row[layer, windows[slot]] == 1 for slot in work]

    def ready(*names):
        for name in names:
            if name in pending:
                pending[name].wait()

    b = Buffers()
    b.xs, b.qkv, b.att = xs, qkv, att
    b.ga, b.wq, b.bias, b.wo, b.gm, b.wu, b.wd = held
    first_slot = jnp.int32(work[-1])
    last_slot = jnp.int32(work[0])
    count = jnp.int32(0)
    for slot, flag in reversed(list(zip(work, is_wet))):
        first_slot = jnp.where(flag, slot, first_slot)
    for slot, flag in zip(work, is_wet):
        last_slot = jnp.where(flag, slot, last_slot)
        count += flag.astype(jnp.int32)
    masking = base == 4 and 3 in [windows[slot] for slot in work]

    def run(ids):
        masked = None
        if masking:
            masked = [jnp.logical_and(lat == bands - 1, i == windows.index(3)) for i in ids]
        run_windows(b, ids, masked, ready)

    if len(work) > 1:

        @pl.when(count >= 2)
        def _():
            run([first_slot, last_slot if len(work) == 2 else jnp.where(count == 3, work[1], last_slot)])
            if opening:
                pending_before = dict(pending)
                pending.clear()
                single = count == 3

                @pl.when(single)
                def _():
                    run([jnp.int32(work[2])])

                pending.update(pending_before)

    @pl.when(count == 1)
    def _():
        run([first_slot])

    if opening:

        @pl.when(count == 0)
        def _():
            ready(*NAMES)

    for target, segments in zip(outs, sinks):
        for slot, at, to, rows, half in overlaps(windows, base, segments):
            target[to : to + rows] = xs[slot * 8 + at : slot * 8 + at + rows, half]
    for c in waits:
        c.wait()


def stage(layer, windows, work, wet, held, sources, sinks, name, opening=False, brings=()):
    ins = [array for array, _ in sources]
    shapes = [jax.ShapeDtypeStruct((sum(h - l for _, l, h in segments), 8, C), f32) for segments in sinks]
    kernel = functools.partial(
        stage_kernel, layer, windows, work, [segments for _, segments in sources], sinks, opening, bool(brings)
    )
    extra = []
    if opening:
        extra = held_shapes(held)
        extra += [jax.ShapeDtypeStruct((8, LANES), jnp.int32), jax.ShapeDtypeStruct((8, 2, 8, C), f32)]
    extra += held_shapes(brings)
    place = HBM if opening else VM
    rows = min(2, len(work)) * TOK
    return pl.pallas_call(
        kernel,
        out_shape=shapes + extra,
        in_specs=[place] * (8 + len(ins)) + [HBM] * len(brings),
        out_specs=[VM] * len(shapes + extra),
        scratch_shapes=[
            pltpu.VMEM((8 * len(windows), 2, 8, C), f32),
            pltpu.VMEM((rows, 3 * C), bf16),
            pltpu.VMEM((rows, C), bf16),
            pltpu.SMEM((LAYERS, 16, 32), jnp.int32),
            pltpu.SemaphoreType.DMA((7,)),
            pltpu.SemaphoreType.DMA((3,)),
        ],
        compiler_params=pltpu.CompilerParams(vmem_limit_bytes=24 << 20),
        cost_estimate=pl.CostEstimate(flops=4_000_000_000, bytes_accessed=6_000_000, transcendentals=800_000),
        name=name,
    )(wet, *held, *ins, *brings)


def send(block, d_lat, d_lon):
    n_lat, n_lon = lax.axis_size("lat"), lax.axis_size("lon")
    route = [
        (a * n_lon + b, (a + d_lat) % n_lat * n_lon + (b + d_lon) % n_lon)
        for a in range(n_lat)
        for b in range(n_lon)
    ]
    return lax.ppermute(block, ("lat", "lon"), route)


def finish_kernel(placed, *refs):
    ins, out, sem = refs[: len(placed)], refs[len(placed)], refs[len(placed) + 1]
    copies = []
    for source, segments in zip(ins, placed):
        at = 0
        for half, low, high in segments:
            part = source.at[at : at + high - low]
            copies.append(pltpu.make_async_copy(part, out.at[low:high, half], sem.at[len(copies)]))
            copies[-1].start()
            at += high - low
    for c in copies:
        c.wait()


def local(tokens, wet_flags, ln_attn, w_qkv, w_out, pos_bias, ln_mlp, w_up, w_down):
    params = [ln_attn, w_qkv, pos_bias, w_out, ln_mlp, w_up, w_down]
    wet = wet_flags.transpose(0, 2, 1)
    grid = tokens.reshape(32, 2, 8, C)
    params = [pltpu.with_memory_space_constraint(p, pltpu.HBM) for p in params]
    wet = pltpu.with_memory_space_constraint(wet, pltpu.HBM)
    grid = pltpu.with_memory_space_constraint(grid, pltpu.HBM)
    for pair in range(LAYERS // 2):
        even, odd = 2 * pair, 2 * pair + 1
        most = [[(0, 8, 32)], [(1, 8, 32)]]
        if pair == 0:
            west_a, keep_a, *rest = stage(
                even, [1, 2, 3], [0, 1, 2], wet, params, [(grid, [])], most, "even0a", opening=True
            )
            held, wet, last = rest[:7], rest[7], [(rest[8], [(None, 0, 8)])]
        else:
            inner = stage(
                even, [2], [0], wet, held, [(back_a, [(0, 12, 28)]), (keep_e, [(1, 12, 28)])],
                [[(0, 16, 24)], [(1, 16, 24)]], f"even{pair}e",
            )
            sides = [(0, 4, 12), (0, 28, 32)]
            west_a, keep_a, *coming = stage(
                even, [1, 2, 3], [0, 2], wet, held,
                [
                    (back_b, sides),
                    (keep_l, [(1, 4, 12), (1, 28, 32)]),
                    (back_a, [(0, 12, 16), (0, 0, 8), (0, 24, 28)]),
                    (keep_e, [(1, 12, 16), (1, 0, 8), (1, 24, 28)]),
                    (inner[0], [(0, 16, 24)]),
                    (inner[1], [(1, 16, 24)]),
                ],
                most, f"even{pair}a", brings=params,
            )
            last = [(back_b, sides), (keep_l, [(1, 4, 12)]), (back_diag, [(0, 0, 4)]), (back_lat, [(1, 0, 4)])]
        west_a = send(west_a, 0, -1)
        west_b, up_lat, up_diag, keep_b, *more = stage(
            even, [0], [0], wet, held, last, [[(0, 4, 8)], [(1, 0, 4)], [(0, 0, 4)], [(1, 4, 8)]],
            f"even{pair}b", brings=params if pair == 0 else (),
        )
        west_b = send(west_b, 0, -1)
        up_lat = send(up_lat, -1, 0)
        up_diag = send(up_diag, -1, -1)
        held = more if pair == 0 else coming
        own, other = (keep_a, [(0, 8, 32)]), (west_a, [(1, 8, 32)])
        keep_e, back_a = stage(
            odd, [1, 2], [0, 1], wet, held, [own, other], [[(0, 12, 28)], [(1, 12, 28)]], f"odd{pair}a"
        )
        back_a = send(back_a, 0, 1)
        keep_l, back_b, back_lat, back_diag, *coming = stage(
            odd, [0, 3], [0, 1], wet, held,
            [own, other, (keep_b, [(0, 4, 8)]), (west_b, [(1, 4, 8)]), (up_lat, [(0, 32, 36)]), (up_diag, [(1, 32, 36)])],
            [[(0, 4, 12), (0, 28, 32)], [(1, 4, 12), (1, 28, 32)], [(0, 32, 36)], [(1, 32, 36)]],
            f"odd{pair}b", brings=params if odd + 1 < LAYERS else (),
        )
        back_b = send(back_b, 0, 1)
        back_lat = send(back_lat, 1, 0)
        back_diag = send(back_diag, 1, 1)
        held = coming
    parts = [
        (back_a, [(0, 12, 28)]),
        (back_b, [(0, 4, 12), (0, 28, 32)]),
        (back_diag, [(0, 0, 4)]),
        (back_lat, [(1, 0, 4)]),
        (keep_l, [(1, 4, 12), (1, 28, 32)]),
        (keep_e, [(1, 12, 28)]),
    ]
    out = pl.pallas_call(
        functools.partial(finish_kernel, [segments for _, segments in parts]),
        out_shape=jax.ShapeDtypeStruct((32, 2, 8, C), f32),
        in_specs=[VM] * len(parts),
        out_specs=HBM,
        scratch_shapes=[pltpu.SemaphoreType.DMA((8,))],
        compiler_params=pltpu.CompilerParams(vmem_limit_bytes=4 << 20),
        name="finish",
    )(*[array for array, _ in parts])
    return out.reshape(32, 16, C)


def solution(mesh):
    in_specs = (P("lat", "lon", None), P(), P(), P(), P(), P(), P(), P(), P())
    out_specs = P("lat", "lon", None)
    return jax.shard_map(local, mesh=mesh, in_specs=in_specs, out_specs=out_specs, check_vma=False)
```
